512 devices in a mesh: space: 128 (over z, y, core), mem: 4 (over x).
Axes of the slice: x: 4, y: 4, z: 16, core: 2. Of those that a mesh axis runs over, the one named last changes fastest.
Arguments:
- prior_ensemble: float32 [512, 512, 128], P('mem', 'space'), may hold values from -70 to 70
- stencil_factors: float32 [4, 512, 128], P(None, 'space'), may hold values from 0.02 to 0.22
- sea_mask: int32 [512, 128], P('space'), may hold values 0 or 1
- measured_site_positions: int32 [128, 128], P('space'), may hold values from 0 to 511
- measured_data: float32 [16384], P('space'), may hold values from -16 to 16
- measurement_precision: float32 [16384], P('space'), may hold values from 0.5 to 2
- cotangent: float32 [512, 512, 128], P('mem', 'space'), may hold values from -6 to 6
Outputs:
- grad_prior: float32 [512, 512, 128], P('mem', 'space')
- grad_coef: float32 [4, 512, 128], P(None, 'space')
The draws below stay inside these ranges and needn't reach their ends.
Inputs may be any that keep to these rules, and one draw needn't show every extreme that they name: `measured_site_positions`: the flat position row * 128 + column, within its strip of 4 rows, of each observed cell; strip s holds rows s * 4 to (s + 1) * 4 - 1. `sea_mask`: 1 marks a sea cell, 0 a land cell.
All inputs are finite; a program needn't handle non-finite values. No bound on the sum of `sea_mask` on one device may be relied on, other than what follows from the above.
Results may differ from the reference program's by a relative error of at most 0.0003.
Values sent between devices are 32-bit elements; how exact they have to be, the bound alone decides.
No kernel may reach another device: no remote copies, remote signals or barrier semaphores. Data moves between devices by JAX's collectives and lax.ppermute only.
A program may use at most 64 MiB of HBM per device.

```python
import math
import jax
import jax.numpy as jnp
from jax import lax

SAMPLE_TOTAL = 512
MESH_LONGITUDES = 128
BAND_LATITUDES = 4
K = 128
ITERS = 2
TILES = 128
MESH_LATITUDES = 512
NOBS = 16384


def draw_prior_ensemble(key, part):
    key_scale, key_noise = jax.random.split(key, 2)
    member_pos = (jnp.arange(SAMPLE_TOTAL, dtype=jnp.float32) + jax.random.uniform(key_scale, (SAMPLE_TOTAL,))) / SAMPLE_TOTAL
    row_pos = jnp.arange(MESH_LATITUDES, dtype=jnp.float32) / MESH_LATITUDES
    scales = 0.3 * 10.0 ** member_pos
    strip_ramp = 3.0 ** row_pos
    noise_field = jax.random.truncated_normal(key_noise, -4.0, 4.0, (SAMPLE_TOTAL, MESH_LATITUDES, MESH_LONGITUDES))
    return (scales[:, None, None] * strip_ramp[None, :, None] * noise_field).astype(jnp.float32)


def with_ends(result, stream_key, least, largest):
    longest = result.shape.index(max(result.shape))
    spots = []
    for shift in (0, 1):
        where = [jax.random.randint(jax.random.fold_in(stream_key, axis), (), 0, length) for axis, length in enumerate(result.shape)]
        where[longest] = (where[longest] + shift) % result.shape[longest]
        spots.append(tuple(where))
    return result.at[spots[0]].set(least).at[spots[1]].set(largest)


def block_levels(own_key, dims, cuts, low, high):
    def one(dim, blocks):
        draws = jax.random.uniform(jax.random.fold_in(jax.random.fold_in(own_key, 6), dim), (blocks,), jnp.float32, low / len(cuts), high / len(cuts))
        return jnp.repeat(jnp.exp(draws), dims[dim] // blocks).reshape((-1,) + (1,) * (len(dims) - dim - 1))

    loudness = one(*cuts[0])
    for cut in cuts[1:]:
        loudness = loudness * one(*cut)
    return loudness


def normal_values(own_key, shape, width, most, pieces=(), kind=jnp.bfloat16):
    gain = block_levels(own_key, shape, pieces, -0.22, 0.18) if pieces else 1.0
    drawn = jax.random.normal(own_key, shape, jnp.float32) * width * gain
    return jnp.minimum(jnp.maximum(drawn, -most), most).astype(kind)


def setup_inputs(seed: int = 0) -> dict:
    splits = jax.random.split(jax.random.key(seed), 8)
    return {
        "prior_ensemble": draw_prior_ensemble(jax.random.fold_in(splits[7], 71), 0),
        "stencil_factors": jnp.clip(0.02 + 0.2 * jax.random.uniform(splits[1], (4, MESH_LATITUDES, MESH_LONGITUDES), jnp.float32) ** block_levels(splits[1], (4, MESH_LATITUDES, MESH_LONGITUDES), ((1, 128),), -0.2, 0.2), 0.02, 0.22),
        "sea_mask": with_ends((jax.random.randint(splits[2], (MESH_LATITUDES, MESH_LONGITUDES), 0, 5) < 4).astype(jnp.int32), jax.random.fold_in(splits[2], 1), 0, 1),
        "measured_site_positions": with_ends(jax.random.randint(splits[3], (TILES, K), 0, BAND_LATITUDES * MESH_LONGITUDES), jax.random.fold_in(splits[3], 1), 0, (BAND_LATITUDES * MESH_LONGITUDES) - 1).astype(jnp.int32),
        "measured_data": normal_values(splits[4], (NOBS,), 4.0, 16.0, ((0, 128),), jnp.float32),
        "measurement_precision": jnp.clip(jnp.exp(math.log(2.0) - 1.3862944 * jax.random.uniform(splits[5], (NOBS,), jnp.float32) ** block_levels(splits[5], (NOBS,), ((0, 128),), -0.2, 0.2)), 0.5, 2.0),
        "cotangent": normal_values(splits[6], (SAMPLE_TOTAL, MESH_LATITUDES, MESH_LONGITUDES), 1.0, 6.0, ((0, 4), (1, 128)), jnp.float32),
    }


highest = lax.Precision.HIGHEST

def product(left_side, right_side):
    return jnp.dot(left_side, right_side, precision=highest, preferred_element_type=jnp.float32)

def substep(state_band_piece, stencil_factors, ocean_share):
    padded = jnp.pad(state_band_piece, ((0, 0), (1, 1), (1, 1)))
    northern = padded[:, :-2, 1:-1]
    southern = padded[:, 2:, 1:-1]
    western = padded[:, 1:-1, :-2]
    eastern = padded[:, 1:-1, 2:]
    advanced = state_band_piece + stencil_factors[0] * (northern - state_band_piece) + stencil_factors[1] * (southern - state_band_piece) + stencil_factors[2] * (western - state_band_piece) + stencil_factors[3] * (eastern - state_band_piece)
    return ocean_share * advanced

def predicted_samples(state_band_piece, stencil_factors, ocean_share):
    return substep(substep(state_band_piece, stencil_factors, ocean_share), stencil_factors, ocean_share)

def corrected_state(predict_advance, measured_site_positions, measured_data, measurement_precision):
    covariance_factor_matrix = jnp.sqrt(jnp.float32(SAMPLE_TOTAL - 1))
    sample_average = lax.optimization_barrier(jnp.mean(predict_advance, axis=0))
    sample_deviations = (predict_advance - sample_average) / covariance_factor_matrix
    mesh_bands = predict_advance.reshape(SAMPLE_TOTAL, MESH_LATITUDES // BAND_LATITUDES, BAND_LATITUDES * MESH_LONGITUDES)
    where_seen = jnp.broadcast_to(measured_site_positions[None, :, :], (SAMPLE_TOTAL, MESH_LATITUDES // BAND_LATITUDES, K))
    picked = jnp.take_along_axis(mesh_bands, where_seen, axis=2).reshape(SAMPLE_TOTAL, NOBS)
    observed = picked + 0.5 * jnp.tanh(picked)
    observed_mean = lax.optimization_barrier(jnp.mean(observed, axis=0))
    obs_anom = (observed - observed_mean) * measurement_precision / covariance_factor_matrix
    innovation = measurement_precision * (measured_data - observed_mean)
    identity = jnp.eye(SAMPLE_TOTAL, dtype=jnp.float32)
    system = identity + product(obs_anom, obs_anom.T)
    norm_scale = jnp.sqrt(jnp.sum(system * system))
    obs_pull = product(obs_anom, innovation)
    approach = system / norm_scale
    polar = identity
    for iteration in range(ITERS):
        factor = 1.5 * identity - 0.5 * product(polar, approach)
        approach = product(approach, factor)
        polar = product(factor, polar)
    transform = polar / jnp.sqrt(norm_scale)
    mean_weights = product(transform, product(transform, obs_pull))
    mixing = covariance_factor_matrix * transform + mean_weights[None, :]
    flattened = sample_deviations.reshape(SAMPLE_TOTAL, MESH_LATITUDES * MESH_LONGITUDES)
    return sample_average + product(mixing, flattened).reshape(SAMPLE_TOTAL, MESH_LATITUDES, MESH_LONGITUDES)

def reference(prior_ensemble, stencil_factors, sea_mask, measured_site_positions, measured_data, measurement_precision, cotangent):
    ocean_share = sea_mask.astype(jnp.float32)
    gathered_samples = prior_ensemble.reshape(SAMPLE_TOTAL // 64, 64, MESH_LATITUDES, MESH_LONGITUDES)
    predict_advance = lax.map(lambda sample_band_piece: predicted_samples(sample_band_piece, stencil_factors, ocean_share), gathered_samples).reshape(SAMPLE_TOTAL, MESH_LATITUDES, MESH_LONGITUDES)
    advance_product, cotangent_mapping = jax.vjp(lambda state_argument: corrected_state(state_argument, measured_site_positions, measured_data, measurement_precision), predict_advance)
    field_bar, = cotangent_mapping(cotangent)

    def block_grad(block_pair):
        sample_band_piece, block_bar = block_pair
        overall_answer, reverse_sweep = jax.vjp(lambda state_argument, stencil_argument: predicted_samples(state_argument, stencil_argument, ocean_share), sample_band_piece, stencil_factors)
        return reverse_sweep(block_bar)
    prior_bar, coef_parts = lax.map(block_grad, (gathered_samples, field_bar.reshape(SAMPLE_TOTAL // 64, 64, MESH_LATITUDES, MESH_LONGITUDES)))
    return (prior_bar.reshape(SAMPLE_TOTAL, MESH_LATITUDES, MESH_LONGITUDES), lax.optimization_barrier(jnp.sum(coef_parts, axis=0)) / jnp.sqrt(jnp.float32(SAMPLE_TOTAL)))
```

```python
import jax
import jax.numpy as jnp
from jax import lax
from jax.sharding import Mesh
from jax.sharding import PartitionSpec as P

SAMPLE_TOTAL = 512
BLOCK = 128
STRIPS = ("z", "y", "core")
GRAM_ROWS = 320
PULL_ROW = GRAM_ROWS + 512
PAYLOAD_ROWS = 896
P1, P2, P3, P4 = -2.4375, 1.6875, -0.5625, 0.0625

high = lax.Precision.HIGH
highest = lax.Precision.HIGHEST


def contract(left_side, right_side, left_dim=1, right_dim=0, precision=high):
    return lax.dot_general(
        left_side,
        right_side,
        (((left_dim,), (right_dim,)), ((), ())),
        precision=precision,
        preferred_element_type=jnp.float32,
    )


def edge_rows(block):
    count = lax.axis_size(STRIPS)
    forward = [(i, i + 1) for i in range(count - 1)]
    backward = [(target, source) for source, target in forward]
    north = lax.ppermute(block[:, -2:], STRIPS, forward)
    south = lax.ppermute(block[:, :2], STRIPS, backward)
    return jnp.concatenate([north, block, south], axis=1)


def shifted(center):
    border = jnp.zeros_like(center[..., :1])
    western = jnp.concatenate([border, center[..., :-1]], axis=-1)
    eastern = jnp.concatenate([center[..., 1:], border], axis=-1)
    return western, eastern


def neighbours(extended):
    center = extended[:, 1:-1]
    western, eastern = shifted(center)
    return center, extended[:, :-2], extended[:, 2:], western, eastern


def substep(extended, stencil_factors, ocean_share):
    center, northern, southern, western, eastern = neighbours(extended)
    advanced = (
        center
        + stencil_factors[0] * (northern - center)
        + stencil_factors[1] * (southern - center)
        + stencil_factors[2] * (western - center)
        + stencil_factors[3] * (eastern - center)
    )
    return ocean_share * advanced


def transpose_step(weight_ext, coef_ext):
    center = weight_ext[:, 1:-1]
    inner_coef = coef_ext[:, 1:-1]
    from_south = coef_ext[0, 2:] * weight_ext[:, 2:]
    from_north = coef_ext[1, :-2] * weight_ext[:, :-2]
    from_west, _ = shifted(inner_coef[3] * center)
    _, from_east = shifted(inner_coef[2] * center)
    keeping = 1.0 - inner_coef[0] - inner_coef[1] - inner_coef[2] - inner_coef[3]
    return center * keeping + from_south + from_north + from_east + from_west


def coef_terms(weight, extended):
    center, northern, southern, western, eastern = neighbours(extended)
    return jnp.stack(
        [
            jnp.sum(weight * (northern - center), axis=0),
            jnp.sum(weight * (southern - center), axis=0),
            jnp.sum(weight * (western - center), axis=0),
            jnp.sum(weight * (eastern - center), axis=0),
        ]
    )


def strip_sum(payload):
    part = PAYLOAD_ROWS // 8
    pieces = lax.all_to_all(
        payload.reshape(8, part, BLOCK), ("y", "core"), 0, 0, tiled=True
    )
    piece = jnp.sum(pieces, axis=0)
    summed = jnp.sum(lax.all_gather(piece, "z", axis=0), axis=0)
    spread = jnp.broadcast_to(summed[None], (16, part, BLOCK))
    mine = lax.all_to_all(spread, ("y", "x"), 0, 0, tiled=True)
    other = lax.ppermute(mine, "core", [(0, 1), (1, 0)])
    first = lax.axis_index("core") == 0
    even = jnp.where(first, mine, other).reshape(4, 4, part, BLOCK)
    odd = jnp.where(first, other, mine).reshape(4, 4, part, BLOCK)
    both = jnp.stack([even, odd], axis=1)
    return both.transpose(2, 0, 1, 3, 4).reshape(4, PAYLOAD_ROWS, BLOCK)


def gram_matrix(blocks):
    diag = [blocks[m, :BLOCK] for m in range(4)]
    following = [blocks[m, BLOCK : 2 * BLOCK] for m in range(4)]
    across = [
        jnp.concatenate(
            [blocks[m, 2 * BLOCK : GRAM_ROWS], blocks[m + 2, 2 * BLOCK : GRAM_ROWS]]
        )
        for m in range(2)
    ]
    rows = [
        [diag[0], following[0], across[0], following[3].T],
        [following[0].T, diag[1], following[1], across[1]],
        [across[0].T, following[1].T, diag[2], following[2]],
        [following[3], across[1].T, following[2].T, diag[3]],
    ]
    return jnp.concatenate([jnp.concatenate(row, axis=1) for row in rows], axis=0)


def local(
    prior_ensemble,
    stencil_factors,
    sea_mask,
    measured_site_positions,
    measured_data,
    measurement_precision,
    cotangent,
):
    members, strip_rows, strip_cols = prior_ensemble.shape
    cell_count = strip_rows * strip_cols
    own = lax.axis_index("x")
    offset = own * members
    cov = jnp.sqrt(jnp.float32(SAMPLE_TOTAL - 1))
    cot_full = lax.all_gather(
        cotangent.reshape(members, cell_count), "x", axis=0, tiled=True
    )

    ocean = sea_mask.astype(jnp.float32)
    stacked = jnp.concatenate([prior_ensemble, stencil_factors, ocean[None]], axis=0)
    extended = edge_rows(stacked)
    prior_ext = extended[:members]
    coef_ext = extended[members : members + 4]
    ocean_ext = extended[members + 4]
    first_ext = substep(prior_ext, coef_ext[:, 1:-1], ocean_ext[1:-1])
    second_state = substep(first_ext, stencil_factors, ocean)
    state = second_state.reshape(members, cell_count)

    onehot = (measured_site_positions[0][:, None] == jnp.arange(cell_count)[None, :]).astype(
        jnp.float32
    )
    picked = contract(state, onehot, 1, 1, highest)
    tanh_picked = jnp.tanh(picked)
    observed = picked + 0.5 * tanh_picked
    member_sums = jnp.sum(state, axis=0).reshape(strip_rows, strip_cols)
    gathered = lax.all_gather(
        jnp.concatenate([observed, member_sums, jnp.zeros((4, BLOCK), jnp.float32)]),
        "x",
        axis=0,
    )
    observed_full = gathered[:, :members].reshape(SAMPLE_TOTAL, BLOCK)
    sample_average = (
        jnp.sum(gathered[:, members : members + strip_rows], axis=0).reshape(cell_count)
        / SAMPLE_TOTAL
    )
    observed_mean = jnp.mean(observed_full, axis=0)
    deviations = (state - sample_average) / cov
    weight = measurement_precision / cov
    anom_full = (observed_full - observed_mean) * weight
    innovation = measurement_precision * (measured_data - observed_mean)

    twice = jnp.concatenate([anom_full, anom_full[:BLOCK]])
    pair = lax.dynamic_slice_in_dim(twice, offset, 2 * BLOCK, 0)
    anom_own = pair[:BLOCK]
    near = contract(anom_own, pair, 1, 1)
    half_start = (own % 2) * BLOCK + (own // 2) * (BLOCK // 2)
    far = contract(
        lax.dynamic_slice_in_dim(anom_full, half_start, BLOCK // 2, 0),
        lax.dynamic_slice_in_dim(anom_full, (own % 2) * BLOCK + 2 * BLOCK, BLOCK, 0),
        1,
        1,
    )
    cross_rows = contract(deviations, cot_full, 1, 1)
    pull_row = jnp.sum(anom_own * innovation, axis=1)[None]
    payload = jnp.concatenate(
        [near[:, :BLOCK], near[:, BLOCK:], far]
        + [cross_rows[:, n * BLOCK : (n + 1) * BLOCK] for n in range(4)]
        + [pull_row, jnp.zeros((PAYLOAD_ROWS - PULL_ROW - 1, BLOCK), jnp.float32)]
    )
    blocks = strip_sum(payload)

    identity = jnp.eye(SAMPLE_TOTAL, dtype=jnp.float32)
    system = identity + gram_matrix(blocks)
    cross = (
        blocks[:, GRAM_ROWS:PULL_ROW]
        .reshape(4, 4, BLOCK, BLOCK)
        .transpose(0, 2, 1, 3)
        .reshape(SAMPLE_TOTAL, SAMPLE_TOTAL)
    )
    obs_pull = blocks[:, PULL_ROW].reshape(SAMPLE_TOTAL)

    norm_scale = jnp.sqrt(jnp.sum(system * system))
    root = jnp.sqrt(norm_scale)
    approach = system / norm_scale
    square = contract(approach, approach)
    polar = (
        2.25 * identity
        + P1 * approach
        + contract(square, P2 * identity + P3 * approach + P4 * square)
    )
    transform = polar / root
    mean_bar = jnp.sum(cross, axis=1)
    mids = contract(transform, jnp.stack([obs_pull, mean_bar], axis=1))
    ends = contract(transform, mids)
    mid_pull, mid_bar = mids[:, 0], mids[:, 1]
    mean_weights, pull_bar = ends[:, 0], ends[:, 1]

    half_bar = (
        (0.5 * cov) * cross
        + 0.5 * mean_bar[:, None] * mid_pull[None, :]
        + 0.5 * mid_bar[:, None] * obs_pull[None, :]
    )
    weight_bar = half_bar + half_bar.T
    polar_bar = weight_bar / root
    left = contract(approach, polar_bar)
    left = left + left.T
    outer = contract(square, P3 * polar_bar + P4 * left)
    middle = contract(contract(approach, polar_bar), approach)
    approach_bar = P1 * polar_bar + P2 * left + (outer + outer.T) + P3 * middle
    scale_bar = (
        -0.5 * jnp.sum(weight_bar * transform) - jnp.sum(approach_bar * approach)
    ) / norm_scale
    sym_bar = (2.0 / norm_scale) * (approach_bar + scale_bar * system)

    def rows_of(matrix):
        return lax.dynamic_slice_in_dim(matrix, offset, members, 0)

    zero_rows = jnp.zeros((6, SAMPLE_TOTAL), jnp.float32)
    mixed = contract(
        jnp.concatenate(
            [rows_of(transform), jnp.sum(transform, axis=0)[None], zero_rows, zero_rows[:1]]
        ),
        cot_full,
    )
    cot_total = jnp.sum(cot_full, axis=0)
    anom_bar = mixed[:members] + (rows_of(mean_weights) / cov)[:, None] * cot_total
    anom_bar_total = mixed[members] + (jnp.sum(mean_weights) / cov) * cot_total
    pulled = contract(
        jnp.concatenate(
            [rows_of(sym_bar), jnp.sum(sym_bar, axis=0)[None], pull_bar[None], zero_rows]
        ),
        anom_full,
    )
    obs_anom_bar = pulled[:members] + rows_of(pull_bar)[:, None] * innovation[None, :]
    obs_anom_total = pulled[members] + jnp.sum(pull_bar) * innovation
    observed_mean_bar = -(obs_anom_total * weight) - measurement_precision * pulled[members + 1]
    observed_bar = obs_anom_bar * weight + observed_mean_bar / SAMPLE_TOTAL
    picked_bar = observed_bar * (1.0 + 0.5 * (1.0 - tanh_picked * tanh_picked))
    field_bar = (
        anom_bar + (cot_total - anom_bar_total) / SAMPLE_TOTAL + contract(picked_bar, onehot)
    )

    second_bar = ocean * field_bar.reshape(members, strip_rows, strip_cols)
    bar_ext = edge_rows(second_bar)
    first_bar = ocean_ext[1:-1] * transpose_step(bar_ext, coef_ext)
    coef_grad = coef_terms(second_bar, first_ext) + coef_terms(
        first_bar[:, 1:-1], prior_ext[:, 1:-1]
    )
    prior_grad = transpose_step(first_bar, coef_ext[:, 1:-1])
    coef_total = lax.psum(coef_grad.reshape(-1), "x")
    return (
        prior_grad,
        coef_total.reshape(4, strip_rows, strip_cols) / jnp.sqrt(jnp.float32(SAMPLE_TOTAL)),
    )


def solution(mesh):
    strips, parts = mesh.devices.shape
    grid = Mesh(mesh.devices.reshape(strips // 8, 4, 2, parts), STRIPS + ("x",))
    placed = (
        P("x", STRIPS, None),
        P(None, STRIPS, None),
        P(STRIPS, None),
        P(STRIPS, None),
        P(STRIPS),
        P(STRIPS),
        P("x", STRIPS, None),
    )
    return jax.shard_map(
        local,
        mesh=grid,
        in_specs=placed,
        out_specs=(P("x", STRIPS, None), P(None, STRIPS, None)),
        check_vma=False,
    )
```

```python
import jax
import jax.numpy as jnp
from jax import lax
from jax.experimental import pallas as pl
from jax.experimental.pallas import tpu as pltpu
from jax.sharding import Mesh
from jax.sharding import PartitionSpec as P

TOTAL = 512
B = 128
CELLS = 512
STRIPS = ("z", "y", "core")
GRAM_ROWS = 320
PULL_ROW = GRAM_ROWS + 512
PAYLOAD_ROWS = 896
PART = PAYLOAD_ROWS // 8
P1, P2, P3, P4 = -2.4375, 1.6875, -0.5625, 0.0625
NN = (((1,), (0,)), ((), ()))
NT = (((1,), (1,)), ((), ()))
TN = (((0,), (0,)), ((), ()))
f32 = jnp.float32


def split(value):
    upper = value.astype(jnp.bfloat16)
    return upper, (value - upper.astype(f32)).astype(jnp.bfloat16)


def dot(left, right, dims=NN):
    return lax.dot_general(left, right, dims, preferred_element_type=f32)


def dot3(left, right, dims=NN):
    lu, ll = left
    ru, rl = right
    return dot(lu, ru, dims) + (dot(lu, rl, dims) + dot(ll, ru, dims))


def total(value):
    return jnp.sum(jnp.sum(value, axis=0, keepdims=True), axis=1, keepdims=True)


def column_sum(value):
    return jnp.sum(value, axis=0, keepdims=True)


def row_block(value, row):
    return value[:, row * B : (row + 1) * B]


def west_of(center):
    column = lax.broadcasted_iota(jnp.int32, center.shape, 1)
    return jnp.where(column == 0, 0.0, pltpu.roll(center, 1, 1))


def east_of(center):
    column = lax.broadcasted_iota(jnp.int32, center.shape, 1)
    return jnp.where(column == B - 1, 0.0, pltpu.roll(center, B - 1, 1))


def substep_row(center, north, south, coef, ocean):
    kept = 1.0 - coef[0] - coef[1] - coef[2] - coef[3]
    return ocean * (
        kept * center
        + coef[0] * north
        + coef[1] * south
        + coef[2] * west_of(center)
        + coef[3] * east_of(center)
    )


def transpose_row(center, north, south, coef, coef_north, coef_south):
    kept = 1.0 - coef[0] - coef[1] - coef[2] - coef[3]
    return (
        kept * center
        + coef_south * south
        + coef_north * north
        + east_of(coef[2] * center)
        + west_of(coef[3] * center)
    )


def onehot_of(sites):
    cell = lax.broadcasted_iota(jnp.int32, (B, CELLS), 1)
    return jnp.where(cell == sites, 1.0, 0.0).astype(jnp.bfloat16)


def coef_rows(field_ref, row):
    return [field_ref[k : k + 1, row * B : (row + 1) * B] for k in range(4)]


def forecast_kernel(prior_ref, north_ref, south_ref, field_ref, sites_ref, first_ref, state_ref, tanh_ref, out_ref):
    prior = (
        [row_block(north_ref[...], r) for r in range(2)]
        + [row_block(prior_ref[...], r) for r in range(4)]
        + [row_block(south_ref[...], r) for r in range(2)]
    )
    first = []
    for row in range(1, 7):
        value = substep_row(
            prior[row],
            prior[row - 1],
            prior[row + 1],
            coef_rows(field_ref, row),
            field_ref[4:5, row * B : (row + 1) * B],
        )
        first_ref[:, (row - 1) * B : row * B] = value
        first.append(value)
    onehot = onehot_of(sites_ref[...])
    picked = jnp.zeros((B, B), f32)
    sums = []
    for row in range(4):
        value = substep_row(
            first[row + 1],
            first[row],
            first[row + 2],
            coef_rows(field_ref, row + 2),
            field_ref[4:5, (row + 2) * B : (row + 3) * B],
        )
        state_ref[:, row * B : (row + 1) * B] = value
        upper, rest = split(value)
        lower = (value - upper.astype(f32) - rest.astype(f32)).astype(jnp.bfloat16)
        here = row_block(onehot, row)
        picked += dot(upper, here, NT) + (dot(rest, here, NT) + dot(lower, here, NT))
        sums.append(column_sum(value))
    bent = jnp.tanh(picked)
    tanh_ref[...] = bent
    out_ref[:B] = picked + 0.5 * bent
    out_ref[B:] = jnp.concatenate(sums + [jnp.zeros((4, B), f32)], axis=0)


def partial_kernel(
    own_ref, gathered_ref, state_ref, cot0, cot1, cot2, cot3, data_ref, precision_ref,
    payload_ref, anom_ref, innovation_ref,
):
    own = own_ref[0]
    root = jnp.sqrt(jnp.full((1, 1), TOTAL - 1, f32))
    sums = column_sum(gathered_ref[0, :B])
    cells = gathered_ref[0, B:]
    for m in range(1, 4):
        sums += column_sum(gathered_ref[m, :B])
        cells += gathered_ref[m, B:]
    observed_mean = sums / TOTAL
    precision = precision_ref[...]
    weight = precision / root
    innovation = precision * (data_ref[...] - observed_mean)
    innovation_ref[...] = innovation
    for m in range(4):
        anom_ref[m * B : (m + 1) * B] = (gathered_ref[m, :B] - observed_mean) * weight

    def members(start, count):
        return anom_ref[pl.ds(pl.multiple_of(start, B // 2), count)]

    mine = members(own * B, B)
    mine_parts = split(mine)
    payload_ref[:B] = dot3(mine_parts, mine_parts, NT)
    after = lax.rem(own + 1, 4)
    payload_ref[B : 2 * B] = dot3(mine_parts, split(members(after * B, B)), NT)
    low = lax.rem(own, 2)
    half = members(low * B + (own // 2) * (B // 2), B // 2)
    payload_ref[2 * B : GRAM_ROWS] = dot3(split(half), split(members(low * B + 2 * B, B)), NT)
    deviations = jnp.concatenate(
        [
            (row_block(state_ref[...], r) - cells[r : r + 1] / TOTAL) / root
            for r in range(4)
        ],
        axis=1,
    )
    parts = split(deviations)
    for d, cot_ref in enumerate((cot0, cot1, cot2, cot3)):
        payload_ref[GRAM_ROWS + d * B : GRAM_ROWS + (d + 1) * B] = dot3(
            parts, split(cot_ref[...]), NT
        )
    rows = dot3(split(jnp.broadcast_to(innovation, (8, B))), mine_parts, NT)
    payload_ref[PULL_ROW : PULL_ROW + 8] = rows
    payload_ref[PULL_ROW + 8 :] = jnp.zeros((PAYLOAD_ROWS - PULL_ROW - 8, B), f32)


def assimilate_kernel(
    place_ref, mine_ref, other_ref, cot0, cot1, cot2, cot3, anom_ref, innovation_ref,
    precision_ref, tanh_ref, sites_ref, ocean_ref,
    out_ref,
    blocks, system, approach_ref, sym_ref, transform_ref, cot_upper, cot_lower,
):
    own, core = place_ref[0], place_ref[1]
    for y in range(4):
        for x in range(4):
            here = pl.multiple_of((y * 2 + core) * PART, 16)
            there = pl.multiple_of((y * 2 + 1 - core) * PART, 16)
            blocks[x, pl.ds(here, PART)] = mine_ref[y * 4 + x]
            blocks[x, pl.ds(there, PART)] = other_ref[y * 4 + x]

    def put(m, n, value):
        system[m * B : (m + 1) * B, n * B : (n + 1) * B] = value

    diagonal = (
        lax.broadcasted_iota(jnp.int32, (B, B), 0) == lax.broadcasted_iota(jnp.int32, (B, B), 1)
    )
    for m in range(4):
        put(m, m, blocks[m, :B] + jnp.where(diagonal, 1.0, 0.0))
        n = (m + 1) % 4
        following = blocks[m, B : 2 * B]
        put(m, n, following)
        put(n, m, following.T)
    for m in range(2):
        across = jnp.concatenate(
            [blocks[m, 2 * B : GRAM_ROWS], blocks[m + 2, 2 * B : GRAM_ROWS]], axis=0
        )
        put(m, m + 2, across)
        put(m + 2, m, across.T)

    sums = [jnp.zeros((1, B), f32) for _ in range(4)]

    def cross(m, n):
        d = (n - m) % 4
        return blocks[m, GRAM_ROWS + d * B : GRAM_ROWS + (d + 1) * B]

    for m in range(4):
        for n in range(m, 4):
            turned = cross(m, n).T
            sums[m] += column_sum(turned)
            if n == m:
                sym_ref[m * B : (m + 1) * B, m * B : (m + 1) * B] = cross(m, m) + turned
            else:
                back = cross(n, m)
                back_turned = back.T
                sums[n] += column_sum(back_turned)
                sym_ref[m * B : (m + 1) * B, n * B : (n + 1) * B] = cross(m, n) + back_turned
                sym_ref[n * B : (n + 1) * B, m * B : (m + 1) * B] = back + turned
    mean_bar = jnp.concatenate(sums, axis=1)
    obs_pull = jnp.concatenate([blocks[m, PULL_ROW : PULL_ROW + 1] for m in range(4)], axis=1)

    full = system[...]
    norm = jnp.sqrt(total(full * full))
    root = jnp.sqrt(norm)
    per_norm, per_root = 1.0 / norm, 1.0 / root
    cov = jnp.sqrt(jnp.full((1, 1), TOTAL - 1, f32))
    approach = full * per_norm
    approach_ref[...] = approach
    approach_parts = split(approach)
    square = dot3(approach_parts, approach_parts)
    square_parts = split(square)
    identity = jnp.where(
        lax.broadcasted_iota(jnp.int32, (TOTAL, TOTAL), 0)
        == lax.broadcasted_iota(jnp.int32, (TOTAL, TOTAL), 1),
        1.0,
        0.0,
    )
    inner = split(P2 * identity + P3 * approach + P4 * square)
    transform = (2.25 * identity + P1 * approach + dot3(square_parts, inner)) * per_root
    transform_ref[...] = transform
    transform_parts = split(transform)
    zeros = jnp.zeros((6, TOTAL), f32)
    mids = dot3(split(jnp.concatenate([obs_pull, mean_bar, zeros], axis=0)), transform_parts)
    ends = dot3(split(mids), transform_parts)
    mid_pull, mid_bar = mids[0:1], mids[1:2]
    pull_bar = ends[1:2]
    gap = jnp.zeros((4, TOTAL), f32)
    outer = dot3(
        split(jnp.concatenate([mean_bar, mid_pull, mid_bar, obs_pull, gap], axis=0)),
        split(jnp.concatenate([mid_pull, mean_bar, obs_pull, mid_bar, gap], axis=0)),
        TN,
    )
    weight_bar = (0.5 * cov) * sym_ref[...] + 0.5 * outer
    scale_bar = -0.5 * total(weight_bar * transform_ref[...])
    polar_bar = weight_bar * per_root
    left = dot3(approach_parts, split(polar_bar))
    middle = dot3(split(left), approach_parts)
    both = left + left.T
    product = dot3(square_parts, split(P3 * polar_bar + P4 * both))
    approach_bar = P1 * polar_bar + P2 * both + (product + product.T) + P3 * middle
    scale_bar = (scale_bar - total(approach_bar * approach_ref[...])) * per_norm
    sym_bar = (2.0 * per_norm) * (approach_bar + scale_bar * system[...])
    sym_ref[...] = sym_bar

    cot_total = jnp.zeros((1, CELLS), f32)
    for d, cot_ref in enumerate((cot0, cot1, cot2, cot3)):
        value = cot_ref[...]
        cot_total += column_sum(value)
        upper, lower = split(value)
        place = pl.ds(pl.multiple_of(lax.rem(own + d, 4) * B, B), B)
        cot_upper[place] = upper
        cot_lower[place] = lower
    mine = pl.ds(pl.multiple_of(own * B, B), B)
    rows = jnp.concatenate(
        [transform_ref[mine], column_sum(transform_ref[...]), jnp.zeros((7, TOTAL), f32)], axis=0
    )
    mixed = dot3(split(rows), (cot_upper[...], cot_lower[...]))
    columns = dot3(split(transform_ref[mine]), split(mids), NT)
    weight_sum = jnp.sum(ends[0:1], axis=1, keepdims=True)
    anom_total = mixed[B : B + 1] + (weight_sum / cov) * cot_total
    shared = (cot_total - anom_total) / TOTAL
    rows = jnp.concatenate([sym_ref[mine], column_sum(sym_bar), pull_bar, zeros], axis=0)
    pulled = dot3(split(rows), split(anom_ref[...]))
    innovation, precision = innovation_ref[...], precision_ref[...]
    weight = precision / cov
    pull_sum = jnp.sum(pull_bar, axis=1, keepdims=True)
    obs_total = pulled[B : B + 1] + pull_sum * innovation
    mean_part = -(obs_total * weight) - precision * pulled[B + 1 : B + 2]
    observed_bar = (pulled[:B] + columns[:, 1:2] * innovation) * weight + mean_part / TOTAL
    bent = tanh_ref[...]
    picked_bar = observed_bar * (1.0 + 0.5 * (1.0 - bent * bent))
    upper, lower = split(picked_bar)
    onehot = onehot_of(sites_ref[...])
    field = mixed[:B] + (columns[:, 0:1] / cov) * cot_total + shared
    out_ref[...] = ocean_ref[...] * (field + (dot(upper, onehot) + dot(lower, onehot)))


def coef_sums(weight, center, north, south):
    base = column_sum(weight * center)
    return [
        column_sum(weight * north) - base,
        column_sum(weight * south) - base,
        column_sum(weight * west_of(center)) - base,
        column_sum(weight * east_of(center)) - base,
    ]


def adjoint_kernel(
    bar_ref, north_ref, south_ref, field_ref, first_ref, prior_ref, prior_north_ref, prior_south_ref,
    grad_ref, coef_ref,
):
    bars = (
        [row_block(north_ref[...], r) for r in range(2)]
        + [row_block(bar_ref[...], r) for r in range(4)]
        + [row_block(south_ref[...], r) for r in range(2)]
    )
    prior = (
        [row_block(prior_north_ref[...], 1)]
        + [row_block(prior_ref[...], r) for r in range(4)]
        + [row_block(prior_south_ref[...], 0)]
    )

    def coef(k, row):
        return field_ref[k : k + 1, row * B : (row + 1) * B]

    def stepped(row, center, north, south):
        return transpose_row(
            center, north, south, coef_rows(field_ref, row), coef(1, row - 1), coef(0, row + 1)
        )

    first_bars = [
        field_ref[4:5, row * B : (row + 1) * B]
        * stepped(row, bars[row], bars[row - 1], bars[row + 1])
        for row in range(1, 7)
    ]
    for row in range(4):
        grad_ref[:, row * B : (row + 1) * B] = stepped(
            row + 2, first_bars[row + 1], first_bars[row], first_bars[row + 2]
        )
        second = coef_sums(
            bars[row + 2],
            row_block(first_ref[...], row + 1),
            row_block(first_ref[...], row),
            row_block(first_ref[...], row + 2),
        )
        first = coef_sums(first_bars[row + 1], prior[row + 1], prior[row], prior[row + 2])
        for k in range(4):
            coef_ref[k * 4 + row : k * 4 + row + 1] = second[k] + first[k]


def call(kernel, outs, scratch=(), smem=False):
    def shaped(s):
        return jax.ShapeDtypeStruct(s, f32)

    def run(*operands):
        specs = [pl.BlockSpec(memory_space=pltpu.VMEM)] * len(operands)
        if smem:
            specs[0] = pl.BlockSpec(memory_space=pltpu.SMEM)
        single = isinstance(outs[0], int)
        return pl.pallas_call(
            kernel,
            out_shape=shaped(outs) if single else [shaped(s) for s in outs],
            in_specs=specs,
            out_specs=pl.BlockSpec(memory_space=pltpu.VMEM)
            if single
            else [pl.BlockSpec(memory_space=pltpu.VMEM)] * len(outs),
            scratch_shapes=list(scratch),
            compiler_params=pltpu.CompilerParams(vmem_limit_bytes=40 * 1024 * 1024),
        )(*operands)

    return run


def edges(block):
    count = lax.axis_size(STRIPS)
    forward = [(i, i + 1) for i in range(count - 1)]
    backward = [(target, source) for source, target in forward]
    north = lax.ppermute(block[:, 2 * B :], STRIPS, forward)
    south = lax.ppermute(block[:, : 2 * B], STRIPS, backward)
    return north, south


def copies_over(value, axes, count):
    spread = jnp.broadcast_to(value[None], (count,) + value.shape)
    return lax.all_to_all(spread, axes, 0, 0, tiled=True)


def strip_sum(payload):
    pieces = lax.all_to_all(
        payload.reshape(8, PART, B), ("y", "core"), 0, 0, tiled=True
    )
    piece = jnp.sum(pieces, axis=0)
    summed = jnp.sum(lax.all_gather(piece, "z", axis=0), axis=0)
    mine = copies_over(summed, ("y", "x"), 16)
    other = lax.ppermute(mine, "core", [(0, 1), (1, 0)])
    return mine, other


def local(
    prior_ensemble,
    stencil_factors,
    sea_mask,
    measured_site_positions,
    measured_data,
    measurement_precision,
    cotangent,
):
    members = prior_ensemble.shape[0]
    own = lax.axis_index("x")
    place = jnp.stack([own, lax.axis_index("core")]).astype(jnp.int32)
    ocean = sea_mask.astype(f32).reshape(1, CELLS)
    stacked = jnp.concatenate(
        [
            prior_ensemble.reshape(members, CELLS),
            stencil_factors.reshape(4, CELLS),
            ocean,
            jnp.zeros((3, CELLS), f32),
        ]
    )
    north, south = edges(stacked)
    prior = stacked[:members]
    field = jnp.concatenate([north[members:], stacked[members:], south[members:]], axis=1)
    prior_north, prior_south = north[:members], south[:members]

    cot = cotangent.reshape(members, CELLS)
    cots = [cot] + [
        lax.ppermute(cot, "x", [((i + d) % 4, i) for i in range(4)]) for d in (1, 3, 2)
    ]
    cots = [cots[0], cots[1], cots[3], cots[2]]

    sites = measured_site_positions.reshape(B, 1)
    precision = measurement_precision.reshape(1, B)
    data = measured_data.reshape(1, B)

    first, state, bent, outgoing = call(
        forecast_kernel, [(members, 6 * B), (members, CELLS), (B, B), (B + 8, B)]
    )(prior, prior_north, prior_south, field, sites)
    gathered = copies_over(outgoing, "x", 4)
    payload, anom, innovation = call(
        partial_kernel, [(PAYLOAD_ROWS, B), (TOTAL, B), (1, B)], smem=True
    )(place, gathered, state, *cots, data, precision)
    mine, other = strip_sum(payload)
    square = (TOTAL, TOTAL)
    bar = call(
        assimilate_kernel,
        (members, CELLS),
        scratch=[pltpu.VMEM((4, PAYLOAD_ROWS, B), f32)]
        + [pltpu.VMEM(square, f32)] * 4
        + [pltpu.VMEM(square, jnp.bfloat16)] * 2,
        smem=True,
    )(place, mine, other, *cots, anom, innovation, precision, bent, sites, ocean)
    bar_north, bar_south = edges(bar)
    grad, coef = call(adjoint_kernel, [(members, CELLS), (16, B)])(
        bar, bar_north, bar_south, field, first, prior, prior_north, prior_south
    )
    coef = jnp.sum(copies_over(coef, "x", 4), axis=0)
    return (
        grad.reshape(prior_ensemble.shape),
        coef.reshape(4, 4, B) / jnp.sqrt(jnp.float32(TOTAL)),
    )


def solution(mesh):
    strips, parts = mesh.devices.shape
    grid = Mesh(mesh.devices.reshape(strips // 8, 4, 2, parts), STRIPS + ("x",))
    placed = (
        P("x", STRIPS, None),
        P(None, STRIPS, None),
        P(STRIPS, None),
        P(STRIPS, None),
        P(STRIPS),
        P(STRIPS),
        P("x", STRIPS, None),
    )
    return jax.shard_map(
        local,
        mesh=grid,
        in_specs=placed,
        out_specs=(P("x", STRIPS, None), P(None, STRIPS, None)),
        check_vma=False,
    )
```

```python
import jax
import jax.numpy as jnp
from jax import lax
from jax.experimental import pallas as pl
from jax.experimental.pallas import tpu as pltpu
from jax.sharding import Mesh
from jax.sharding import PartitionSpec as P

TOTAL = 512
B = 128
CELLS = 512
STRIPS = ("z", "y", "core")
FAR = 2
CROSS = 3
PARTS = 8
HALF = B // 2
P1, P2, P3, P4 = -2.4375, 1.6875, -0.5625, 0.0625
NN = (((1,), (0,)), ((), ()))
NT = (((1,), (1,)), ((), ()))
TN = (((0,), (0,)), ((), ()))
f32 = jnp.float32


def split(value):
    upper = value.astype(jnp.bfloat16)
    return upper, (value - upper.astype(f32)).astype(jnp.bfloat16)


def dot(left, right, dims=NN):
    return lax.dot_general(left, right, dims, preferred_element_type=f32)


def dot3(left, right, dims=NN):
    lu, ll = left
    ru, rl = right
    return dot(lu, ru, dims) + (dot(lu, rl, dims) + dot(ll, ru, dims))


def total(value):
    return jnp.sum(jnp.sum(value, axis=0, keepdims=True), axis=1, keepdims=True)


def column_sum(value):
    return jnp.sum(value, axis=0, keepdims=True)


def row_block(value, row):
    return value[:, row * B : (row + 1) * B]


def west_of(center):
    column = lax.broadcasted_iota(jnp.int32, center.shape, 1)
    return jnp.where(column == 0, 0.0, pltpu.roll(center, 1, 1))


def east_of(center):
    column = lax.broadcasted_iota(jnp.int32, center.shape, 1)
    return jnp.where(column == B - 1, 0.0, pltpu.roll(center, B - 1, 1))


def substep_row(center, north, south, coef, ocean):
    kept = 1.0 - coef[0] - coef[1] - coef[2] - coef[3]
    return ocean * (
        kept * center
        + coef[0] * north
        + coef[1] * south
        + coef[2] * west_of(center)
        + coef[3] * east_of(center)
    )


def transpose_row(center, north, south, coef, coef_north, coef_south):
    kept = 1.0 - coef[0] - coef[1] - coef[2] - coef[3]
    return (
        kept * center
        + coef_south * south
        + coef_north * north
        + east_of(coef[2] * center)
        + west_of(coef[3] * center)
    )


def onehot_of(sites):
    cell = lax.broadcasted_iota(jnp.int32, (B, CELLS), 1)
    return jnp.where(cell == sites, 1.0, 0.0).astype(jnp.bfloat16)


def coef_rows(field_ref, row):
    return [field_ref[k : k + 1, row * B : (row + 1) * B] for k in range(4)]


def forecast_kernel(prior_ref, north_ref, south_ref, field_ref, sites_ref, first_ref, state_ref, tanh_ref, out_ref):
    prior = (
        [row_block(north_ref[...], r) for r in range(2)]
        + [row_block(prior_ref[...], r) for r in range(4)]
        + [row_block(south_ref[...], r) for r in range(2)]
    )
    first = []
    for row in range(1, 7):
        value = substep_row(
            prior[row],
            prior[row - 1],
            prior[row + 1],
            coef_rows(field_ref, row),
            field_ref[4:5, row * B : (row + 1) * B],
        )
        first_ref[:, (row - 1) * B : row * B] = value
        first.append(value)
    onehot = onehot_of(sites_ref[...])
    picked = jnp.zeros((B, B), f32)
    sums = []
    for row in range(4):
        value = substep_row(
            first[row + 1],
            first[row],
            first[row + 2],
            coef_rows(field_ref, row + 2),
            field_ref[4:5, (row + 2) * B : (row + 3) * B],
        )
        state_ref[:, row * B : (row + 1) * B] = value
        upper, rest = split(value)
        lower = (value - upper.astype(f32) - rest.astype(f32)).astype(jnp.bfloat16)
        here = row_block(onehot, row)
        picked += dot(upper, here, NT) + (dot(rest, here, NT) + dot(lower, here, NT))
        sums.append(column_sum(value))
    bent = jnp.tanh(picked)
    tanh_ref[...] = bent
    observed = picked + 0.5 * bent
    sums = jnp.concatenate(sums + [jnp.zeros((4, B), f32)], axis=0)
    for copy in range(4):
        out_ref[copy, :B] = observed
        out_ref[copy, B:] = sums


def partial_kernel(
    own_ref, gathered_ref, state_ref, cot_ref, data_ref, precision_ref,
    payload_ref, anom_ref, innovation_ref,
):
    own = own_ref[0]
    root = jnp.sqrt(jnp.full((1, 1), TOTAL - 1, f32))
    sums = column_sum(gathered_ref[0, :B])
    cells = gathered_ref[0, B:]
    for m in range(1, 4):
        sums += column_sum(gathered_ref[m, :B])
        cells += gathered_ref[m, B:]
    observed_mean = sums / TOTAL
    precision = precision_ref[...]
    weight = precision / root
    innovation = precision * (data_ref[...] - observed_mean)
    innovation_ref[...] = innovation
    for m in range(4):
        anom_ref[m * B : (m + 1) * B] = (gathered_ref[m, :B] - observed_mean) * weight

    def members(start, count):
        return anom_ref[pl.ds(pl.multiple_of(start, B // 2), count)]

    mine = members(own * B, B)
    mine_parts = split(mine)
    payload_ref[0] = dot3(mine_parts, mine_parts, NT)
    after = lax.rem(own + 1, 4)
    payload_ref[1] = dot3(mine_parts, split(members(after * B, B)), NT)
    low = lax.rem(own, 2)
    half = members(low * B + (own // 2) * HALF, HALF)
    payload_ref[FAR, :HALF] = dot3(split(half), split(members(low * B + 2 * B, B)), NT)
    payload_ref[FAR, HALF : HALF + 8] = dot3(
        split(jnp.broadcast_to(innovation, (8, B))), mine_parts, NT
    )
    payload_ref[FAR, HALF + 8 :] = jnp.zeros((HALF - 8, B), f32)
    payload_ref[PARTS - 1] = jnp.zeros((B, B), f32)
    deviations = jnp.concatenate(
        [
            (row_block(state_ref[...], r) - cells[r : r + 1] / TOTAL) / root
            for r in range(4)
        ],
        axis=1,
    )
    parts = split(deviations)
    for n in range(4):
        payload_ref[CROSS + n] = dot3(parts, split(cot_ref[n]), NT)


def assimilate_kernel(
    place_ref, mine_ref, other_ref, cot_ref, anom_ref, innovation_ref,
    precision_ref, tanh_ref, sites_ref, ocean_ref,
    out_ref,
    blocks, system, approach_ref, sym_ref, transform_ref, cot_upper, cot_lower,
):
    own, core = place_ref[0], place_ref[1]
    for y in range(4):
        for x in range(4):
            blocks[x, y * 2 + core] = mine_ref[y * 4 + x]
            blocks[x, y * 2 + 1 - core] = other_ref[y * 4 + x]

    def put(m, n, value):
        system[m * B : (m + 1) * B, n * B : (n + 1) * B] = value

    diagonal = (
        lax.broadcasted_iota(jnp.int32, (B, B), 0) == lax.broadcasted_iota(jnp.int32, (B, B), 1)
    )
    for m in range(4):
        put(m, m, blocks[m, 0] + jnp.where(diagonal, 1.0, 0.0))
        n = (m + 1) % 4
        following = blocks[m, 1]
        put(m, n, following)
        put(n, m, following.T)
    for m in range(2):
        across = jnp.concatenate(
            [blocks[m, FAR, :HALF], blocks[m + 2, FAR, :HALF]], axis=0
        )
        put(m, m + 2, across)
        put(m + 2, m, across.T)

    sums = [jnp.zeros((1, B), f32) for _ in range(4)]

    def cross(m, n):
        return blocks[m, CROSS + n]

    for m in range(4):
        for n in range(m, 4):
            turned = cross(m, n).T
            sums[m] += column_sum(turned)
            if n == m:
                sym_ref[m * B : (m + 1) * B, m * B : (m + 1) * B] = cross(m, m) + turned
            else:
                back = cross(n, m)
                back_turned = back.T
                sums[n] += column_sum(back_turned)
                sym_ref[m * B : (m + 1) * B, n * B : (n + 1) * B] = cross(m, n) + back_turned
                sym_ref[n * B : (n + 1) * B, m * B : (m + 1) * B] = back + turned
    mean_bar = jnp.concatenate(sums, axis=1)
    obs_pull = jnp.concatenate([blocks[m, FAR, HALF : HALF + 1] for m in range(4)], axis=1)

    full = system[...]
    norm = jnp.sqrt(total(full * full))
    root = jnp.sqrt(norm)
    per_norm, per_root = 1.0 / norm, 1.0 / root
    cov = jnp.sqrt(jnp.full((1, 1), TOTAL - 1, f32))
    approach = full * per_norm
    approach_ref[...] = approach
    approach_parts = split(approach)
    square = dot3(approach_parts, approach_parts)
    square_parts = split(square)
    identity = jnp.where(
        lax.broadcasted_iota(jnp.int32, (TOTAL, TOTAL), 0)
        == lax.broadcasted_iota(jnp.int32, (TOTAL, TOTAL), 1),
        1.0,
        0.0,
    )
    inner = split(P2 * identity + P3 * approach + P4 * square)
    transform = (2.25 * identity + P1 * approach + dot3(square_parts, inner)) * per_root
    transform_ref[...] = transform
    transform_parts = split(transform)
    zeros = jnp.zeros((6, TOTAL), f32)
    mids = dot3(split(jnp.concatenate([obs_pull, mean_bar, zeros], axis=0)), transform_parts)
    ends = dot3(split(mids), transform_parts)
    mid_pull, mid_bar = mids[0:1], mids[1:2]
    pull_bar = ends[1:2]
    gap = jnp.zeros((4, TOTAL), f32)
    outer = dot3(
        split(jnp.concatenate([mean_bar, mid_pull, mid_bar, obs_pull, gap], axis=0)),
        split(jnp.concatenate([mid_pull, mean_bar, obs_pull, mid_bar, gap], axis=0)),
        TN,
    )
    weight_bar = (0.5 * cov) * sym_ref[...] + 0.5 * outer
    scale_bar = -0.5 * total(weight_bar * transform_ref[...])
    polar_bar = weight_bar * per_root
    left = dot3(approach_parts, split(polar_bar))
    middle = dot3(split(left), approach_parts)
    both = left + left.T
    product = dot3(square_parts, split(P3 * polar_bar + P4 * both))
    approach_bar = P1 * polar_bar + P2 * both + (product + product.T) + P3 * middle
    scale_bar = (scale_bar - total(approach_bar * approach_ref[...])) * per_norm
    sym_bar = (2.0 * per_norm) * (approach_bar + scale_bar * system[...])
    sym_ref[...] = sym_bar

    cot_total = jnp.zeros((1, CELLS), f32)
    for n in range(4):
        value = cot_ref[n]
        cot_total += column_sum(value)
        upper, lower = split(value)
        cot_upper[n * B : (n + 1) * B] = upper
        cot_lower[n * B : (n + 1) * B] = lower
    mine = pl.ds(pl.multiple_of(own * B, B), B)
    rows = jnp.concatenate(
        [transform_ref[mine], column_sum(transform_ref[...]), jnp.zeros((7, TOTAL), f32)], axis=0
    )
    mixed = dot3(split(rows), (cot_upper[...], cot_lower[...]))
    columns = dot3(split(transform_ref[mine]), split(mids), NT)
    weight_sum = jnp.sum(ends[0:1], axis=1, keepdims=True)
    anom_total = mixed[B : B + 1] + (weight_sum / cov) * cot_total
    shared = (cot_total - anom_total) / TOTAL
    rows = jnp.concatenate([sym_ref[mine], column_sum(sym_bar), pull_bar, zeros], axis=0)
    pulled = dot3(split(rows), split(anom_ref[...]))
    innovation, precision = innovation_ref[...], precision_ref[...]
    weight = precision / cov
    pull_sum = jnp.sum(pull_bar, axis=1, keepdims=True)
    obs_total = pulled[B : B + 1] + pull_sum * innovation
    mean_part = -(obs_total * weight) - precision * pulled[B + 1 : B + 2]
    observed_bar = (pulled[:B] + columns[:, 1:2] * innovation) * weight + mean_part / TOTAL
    bent = tanh_ref[...]
    picked_bar = observed_bar * (1.0 + 0.5 * (1.0 - bent * bent))
    upper, lower = split(picked_bar)
    onehot = onehot_of(sites_ref[...])
    field = mixed[:B] + (columns[:, 0:1] / cov) * cot_total + shared
    out_ref[...] = ocean_ref[...] * (field + (dot(upper, onehot) + dot(lower, onehot)))


def coef_sums(weight, center, north, south):
    base = column_sum(weight * center)
    return [
        column_sum(weight * north) - base,
        column_sum(weight * south) - base,
        column_sum(weight * west_of(center)) - base,
        column_sum(weight * east_of(center)) - base,
    ]


def adjoint_kernel(
    bar_ref, north_ref, south_ref, field_ref, first_ref, prior_ref, prior_north_ref, prior_south_ref,
    grad_ref, coef_ref,
):
    bars = (
        [row_block(north_ref[...], r) for r in range(2)]
        + [row_block(bar_ref[...], r) for r in range(4)]
        + [row_block(south_ref[...], r) for r in range(2)]
    )
    prior = (
        [row_block(prior_north_ref[...], 1)]
        + [row_block(prior_ref[...], r) for r in range(4)]
        + [row_block(prior_south_ref[...], 0)]
    )

    def coef(k, row):
        return field_ref[k : k + 1, row * B : (row + 1) * B]

    def stepped(row, center, north, south):
        return transpose_row(
            center, north, south, coef_rows(field_ref, row), coef(1, row - 1), coef(0, row + 1)
        )

    first_bars = [
        field_ref[4:5, row * B : (row + 1) * B]
        * stepped(row, bars[row], bars[row - 1], bars[row + 1])
        for row in range(1, 7)
    ]
    for row in range(4):
        grad_ref[:, row * B : (row + 1) * B] = stepped(
            row + 2, first_bars[row + 1], first_bars[row], first_bars[row + 2]
        )
        second = coef_sums(
            bars[row + 2],
            row_block(first_ref[...], row + 1),
            row_block(first_ref[...], row),
            row_block(first_ref[...], row + 2),
        )
        first = coef_sums(first_bars[row + 1], prior[row + 1], prior[row], prior[row + 2])
        for k in range(4):
            for copy in range(4):
                coef_ref[copy, k * 4 + row : k * 4 + row + 1] = second[k] + first[k]


def call(kernel, outs, scratch=(), smem=False):
    def shaped(s):
        return jax.ShapeDtypeStruct(s, f32)

    def run(*operands):
        specs = [pl.BlockSpec(memory_space=pltpu.VMEM)] * len(operands)
        if smem:
            specs[0] = pl.BlockSpec(memory_space=pltpu.SMEM)
        single = isinstance(outs[0], int)
        return pl.pallas_call(
            kernel,
            out_shape=shaped(outs) if single else [shaped(s) for s in outs],
            in_specs=specs,
            out_specs=pl.BlockSpec(memory_space=pltpu.VMEM)
            if single
            else [pl.BlockSpec(memory_space=pltpu.VMEM)] * len(outs),
            scratch_shapes=list(scratch),
            compiler_params=pltpu.CompilerParams(vmem_limit_bytes=40 * 1024 * 1024),
        )(*operands)

    return run


def edge_kernel(prior_ref, coef_ref, mask_ref, prior_out, field_ref, forward_ref, backward_ref):
    members = prior_ref.shape[0]
    mask = mask_ref[...].astype(f32)
    for row in range(4):
        cells = slice(row * B, (row + 1) * B)
        value = prior_ref[:, row, :]
        rows = jnp.concatenate(
            [coef_ref[k, row : row + 1, :] for k in range(4)]
            + [mask[row : row + 1], jnp.zeros((3, B), f32)],
            axis=0,
        )
        prior_out[:, cells] = value
        field_ref[:, cells] = rows
        side = backward_ref if row < 2 else forward_ref
        cells = slice((row % 2) * B, (row % 2 + 1) * B)
        side[:members, cells] = value
        side[members:, cells] = rows


def spread_kernel(cot_ref, out_ref):
    for row in range(4):
        value = cot_ref[:, row, :]
        for copy in range(4):
            out_ref[copy, :, row * B : (row + 1) * B] = value


def exchange(forward_edge, backward_edge):
    count = lax.axis_size(STRIPS)
    forward = [(i, i + 1) for i in range(count - 1)]
    backward = [(target, source) for source, target in forward]
    return lax.ppermute(forward_edge, STRIPS, forward), lax.ppermute(backward_edge, STRIPS, backward)


def trade(parts, axes):
    return lax.all_to_all(parts, axes, 0, 0, tiled=True)


def copies(value, count):
    return jnp.broadcast_to(value[None], (count,) + value.shape)


def strip_sum(payload):
    piece = jnp.sum(trade(payload, ("y", "core")), axis=0)
    depth = lax.axis_size("z")
    slices = trade(piece.reshape(depth, B // depth, B), "z")
    summed = trade(copies(jnp.sum(slices, axis=0), depth), "z")
    mine = trade(copies(summed.reshape(B, B), 16), ("y", "x"))
    return mine, lax.ppermute(mine, "core", [(0, 1), (1, 0)])


def local(
    prior_ensemble,
    stencil_factors,
    sea_mask,
    measured_site_positions,
    measured_data,
    measurement_precision,
    cotangent,
):
    members = prior_ensemble.shape[0]
    own = lax.axis_index("x")
    place = jnp.stack([own, lax.axis_index("core")]).astype(jnp.int32)
    prior, own_field, forward_edge, backward_edge = call(
        edge_kernel,
        [(members, CELLS), (8, CELLS), (members + 8, 2 * B), (members + 8, 2 * B)],
    )(prior_ensemble, stencil_factors, sea_mask)
    north, south = exchange(forward_edge, backward_edge)
    field = jnp.concatenate([north[members:], own_field, south[members:]], axis=1)
    prior_north, prior_south = north[:members], south[:members]
    ocean = own_field[4:5]
    cots = trade(call(spread_kernel, (4, members, CELLS))(cotangent), "x")

    sites = measured_site_positions.reshape(B, 1)
    precision = measurement_precision.reshape(1, B)
    data = measured_data.reshape(1, B)

    first, state, bent, outgoing = call(
        forecast_kernel, [(members, 6 * B), (members, CELLS), (B, B), (4, B + 8, B)]
    )(prior, prior_north, prior_south, field, sites)
    gathered = trade(outgoing, "x")
    payload, anom, innovation = call(
        partial_kernel, [(PARTS, B, B), (TOTAL, B), (1, B)], smem=True
    )(place, gathered, state, cots, data, precision)
    mine, other = strip_sum(payload)
    square = (TOTAL, TOTAL)
    bar = call(
        assimilate_kernel,
        (members, CELLS),
        scratch=[pltpu.VMEM((4, PARTS, B, B), f32)]
        + [pltpu.VMEM(square, f32)] * 4
        + [pltpu.VMEM(square, jnp.bfloat16)] * 2,
        smem=True,
    )(place, mine, other, cots, anom, innovation, precision, bent, sites, ocean)
    bar_north, bar_south = exchange(bar[:, 2 * B :], bar[:, : 2 * B])
    grad, coef = call(adjoint_kernel, [(members, CELLS), (4, 16, B)])(
        bar, bar_north, bar_south, field, first, prior, prior_north, prior_south
    )
    coef = jnp.sum(trade(coef, "x"), axis=0)
    return (
        grad.reshape(prior_ensemble.shape),
        coef.reshape(4, 4, B) / jnp.sqrt(jnp.float32(TOTAL)),
    )


def solution(mesh):
    strips, parts = mesh.devices.shape
    grid = Mesh(mesh.devices.reshape(strips // 8, 4, 2, parts), STRIPS + ("x",))
    placed = (
        P("x", STRIPS, None),
        P(None, STRIPS, None),
        P(STRIPS, None),
        P(STRIPS, None),
        P(STRIPS),
        P(STRIPS),
        P("x", STRIPS, None),
    )
    return jax.shard_map(
        local,
        mesh=grid,
        in_specs=placed,
        out_specs=(P("x", STRIPS, None), P(None, STRIPS, None)),
        check_vma=False,
    )
```

```python
import jax
import jax.numpy as jnp
from jax import lax
from jax.experimental import pallas as pl
from jax.experimental.pallas import tpu as pltpu
from jax.sharding import Mesh
from jax.sharding import PartitionSpec as P

TOTAL = 512
B = 128
CELLS = 512
STRIPS = ("z", "z_low", "y", "core")
GRAM_ROWS = 320
PULL_ROW = GRAM_ROWS + 512
PAYLOAD_ROWS = 896
PART = PAYLOAD_ROWS // 16
HALF = B // 2
OBS_ROWS = B + 8
P1, P2, P3, P4 = -2.4375, 1.6875, -0.5625, 0.0625
NN = (((1,), (0,)), ((), ()))
NT = (((1,), (1,)), ((), ()))
TN = (((0,), (0,)), ((), ()))
f32 = jnp.float32


def split(value):
    upper = value.astype(jnp.bfloat16)
    return upper, (value - upper.astype(f32)).astype(jnp.bfloat16)


def dot(left, right, dims=NN):
    return lax.dot_general(left, right, dims, preferred_element_type=f32)


def dot3(left, right, dims=NN):
    lu, ll = left
    ru, rl = right
    return dot(lu, ru, dims) + (dot(lu, rl, dims) + dot(ll, ru, dims))


def total(value):
    return jnp.sum(jnp.sum(value, axis=0, keepdims=True), axis=1, keepdims=True)


def column_sum(value):
    return jnp.sum(value, axis=0, keepdims=True)


def row_block(value, row):
    return value[:, row * B : (row + 1) * B]


def west_of(center):
    column = lax.broadcasted_iota(jnp.int32, center.shape, 1)
    return jnp.where(column == 0, 0.0, pltpu.roll(center, 1, 1))


def east_of(center):
    column = lax.broadcasted_iota(jnp.int32, center.shape, 1)
    return jnp.where(column == B - 1, 0.0, pltpu.roll(center, B - 1, 1))


def substep_row(center, north, south, coef, ocean):
    kept = 1.0 - coef[0] - coef[1] - coef[2] - coef[3]
    return ocean * (
        kept * center
        + coef[0] * north
        + coef[1] * south
        + coef[2] * west_of(center)
        + coef[3] * east_of(center)
    )


def transpose_row(center, north, south, coef, coef_north, coef_south):
    kept = 1.0 - coef[0] - coef[1] - coef[2] - coef[3]
    return (
        kept * center
        + coef_south * south
        + coef_north * north
        + east_of(coef[2] * center)
        + west_of(coef[3] * center)
    )


def onehot_of(sites):
    cell = lax.broadcasted_iota(jnp.int32, (B, CELLS), 1)
    return jnp.where(cell == sites, 1.0, 0.0).astype(jnp.bfloat16)


def coef_rows(field_ref, row):
    return [field_ref[k : k + 1, row * B : (row + 1) * B] for k in range(4)]


def forecast_kernel(prior_ref, north_ref, south_ref, field_ref, sites_ref, cot_ref, first_ref, state_ref, tanh_ref, out_ref):
    prior = (
        [row_block(north_ref[...], r) for r in range(2)]
        + [row_block(prior_ref[...], r) for r in range(4)]
        + [row_block(south_ref[...], r) for r in range(2)]
    )
    first = []
    for row in range(1, 7):
        value = substep_row(
            prior[row],
            prior[row - 1],
            prior[row + 1],
            coef_rows(field_ref, row),
            field_ref[4:5, row * B : (row + 1) * B],
        )
        first_ref[:, (row - 1) * B : row * B] = value
        first.append(value)
    onehot = onehot_of(sites_ref[...])
    picked = jnp.zeros((B, B), f32)
    sums = []
    for row in range(4):
        value = substep_row(
            first[row + 1],
            first[row],
            first[row + 2],
            coef_rows(field_ref, row + 2),
            field_ref[4:5, (row + 2) * B : (row + 3) * B],
        )
        state_ref[:, row * B : (row + 1) * B] = value
        upper, rest = split(value)
        lower = (value - upper.astype(f32) - rest.astype(f32)).astype(jnp.bfloat16)
        here = row_block(onehot, row)
        picked += dot(upper, here, NT) + (dot(rest, here, NT) + dot(lower, here, NT))
        sums.append(column_sum(value))
    bent = jnp.tanh(picked)
    tanh_ref[...] = bent
    observed = picked + 0.5 * bent
    sums = jnp.concatenate(sums + [jnp.zeros((4, B), f32)], axis=0)
    for copy in range(4):
        out_ref[copy, :B] = observed
        out_ref[copy, B:OBS_ROWS] = sums
        out_ref[copy, OBS_ROWS:] = cot_ref[...]


def cot_block(gathered_ref, m):
    return jnp.concatenate(
        [gathered_ref[m, OBS_ROWS + r * B : OBS_ROWS + (r + 1) * B] for r in range(4)], axis=1
    )


def partial_kernel(
    own_ref, gathered_ref, state_ref, data_ref, precision_ref,
    payload_ref, anom_ref, innovation_ref,
):
    own = own_ref[0]
    root = jnp.sqrt(jnp.full((1, 1), TOTAL - 1, f32))
    sums = column_sum(gathered_ref[0, :B])
    cells = gathered_ref[0, B:OBS_ROWS]
    for m in range(1, 4):
        sums += column_sum(gathered_ref[m, :B])
        cells += gathered_ref[m, B:OBS_ROWS]
    observed_mean = sums / TOTAL
    precision = precision_ref[...]
    weight = precision / root
    innovation = precision * (data_ref[...] - observed_mean)
    innovation_ref[...] = innovation
    for m in range(4):
        anom_ref[m * B : (m + 1) * B] = (gathered_ref[m, :B] - observed_mean) * weight

    def members(start, count):
        return anom_ref[pl.ds(pl.multiple_of(start, B // 2), count)]

    mine = members(own * B, B)
    mine_parts = split(mine)
    payload_ref[:B] = dot3(mine_parts, mine_parts, NT)
    after = lax.rem(own + 1, 4)
    payload_ref[B : 2 * B] = dot3(mine_parts, split(members(after * B, B)), NT)
    low = lax.rem(own, 2)
    half = members(low * B + (own // 2) * HALF, HALF)
    payload_ref[2 * B : GRAM_ROWS] = dot3(split(half), split(members(low * B + 2 * B, B)), NT)
    payload_ref[PULL_ROW : PULL_ROW + 8] = dot3(
        split(jnp.broadcast_to(innovation, (8, B))), mine_parts, NT
    )
    payload_ref[PULL_ROW + 8 :] = jnp.zeros((PAYLOAD_ROWS - PULL_ROW - 8, B), f32)
    deviations = jnp.concatenate(
        [
            (row_block(state_ref[...], r) - cells[r : r + 1] / TOTAL) / root
            for r in range(4)
        ],
        axis=1,
    )
    parts = split(deviations)
    for n in range(4):
        payload_ref[GRAM_ROWS + n * B : GRAM_ROWS + (n + 1) * B] = dot3(
            parts, split(cot_block(gathered_ref, n)), NT
        )


def assimilate_kernel(
    place_ref, mine_ref, other_ref, gathered_ref, anom_ref, innovation_ref,
    precision_ref, tanh_ref, sites_ref, ocean_ref,
    out_ref,
    blocks, system, approach_ref, sym_ref, transform_ref, cot_upper, cot_lower,
):
    own, core = place_ref[0], place_ref[1]
    for p in range(8):
        here = pl.ds(pl.multiple_of((p * 2 + core) * PART, 8), PART)
        there = pl.ds(pl.multiple_of((p * 2 + 1 - core) * PART, 8), PART)
        spot = ((p % 2) * 4 + p // 2) * 4
        for x in range(4):
            blocks[x, here] = mine_ref[spot + x]
            blocks[x, there] = other_ref[spot + x]

    def put(m, n, value):
        system[m * B : (m + 1) * B, n * B : (n + 1) * B] = value

    diagonal = (
        lax.broadcasted_iota(jnp.int32, (B, B), 0) == lax.broadcasted_iota(jnp.int32, (B, B), 1)
    )
    for m in range(4):
        put(m, m, blocks[m, :B] + jnp.where(diagonal, 1.0, 0.0))
        n = (m + 1) % 4
        following = blocks[m, B : 2 * B]
        put(m, n, following)
        put(n, m, following.T)
    for m in range(2):
        across = jnp.concatenate(
            [blocks[m, 2 * B : GRAM_ROWS], blocks[m + 2, 2 * B : GRAM_ROWS]], axis=0
        )
        put(m, m + 2, across)
        put(m + 2, m, across.T)

    sums = [jnp.zeros((1, B), f32) for _ in range(4)]

    def cross(m, n):
        return blocks[m, GRAM_ROWS + n * B : GRAM_ROWS + (n + 1) * B]

    for m in range(4):
        for n in range(m, 4):
            turned = cross(m, n).T
            sums[m] += column_sum(turned)
            if n == m:
                sym_ref[m * B : (m + 1) * B, m * B : (m + 1) * B] = cross(m, m) + turned
            else:
                back = cross(n, m)
                back_turned = back.T
                sums[n] += column_sum(back_turned)
                sym_ref[m * B : (m + 1) * B, n * B : (n + 1) * B] = cross(m, n) + back_turned
                sym_ref[n * B : (n + 1) * B, m * B : (m + 1) * B] = back + turned
    mean_bar = jnp.concatenate(sums, axis=1)
    obs_pull = jnp.concatenate([blocks[m, PULL_ROW : PULL_ROW + 1] for m in range(4)], axis=1)

    full = system[...]
    norm = jnp.sqrt(total(full * full))
    root = jnp.sqrt(norm)
    per_norm, per_root = 1.0 / norm, 1.0 / root
    cov = jnp.sqrt(jnp.full((1, 1), TOTAL - 1, f32))
    approach = full * per_norm
    approach_ref[...] = approach
    approach_parts = split(approach)
    square = dot3(approach_parts, approach_parts)
    square_parts = split(square)
    identity = jnp.where(
        lax.broadcasted_iota(jnp.int32, (TOTAL, TOTAL), 0)
        == lax.broadcasted_iota(jnp.int32, (TOTAL, TOTAL), 1),
        1.0,
        0.0,
    )
    inner = split(P2 * identity + P3 * approach + P4 * square)
    transform = (2.25 * identity + P1 * approach + dot3(square_parts, inner)) * per_root
    transform_ref[...] = transform
    transform_parts = split(transform)
    zeros = jnp.zeros((6, TOTAL), f32)
    mids = dot3(split(jnp.concatenate([obs_pull, mean_bar, zeros], axis=0)), transform_parts)
    ends = dot3(split(mids), transform_parts)
    mid_pull, mid_bar = mids[0:1], mids[1:2]
    pull_bar = ends[1:2]
    gap = jnp.zeros((4, TOTAL), f32)
    outer = dot3(
        split(jnp.concatenate([mean_bar, mid_pull, mid_bar, obs_pull, gap], axis=0)),
        split(jnp.concatenate([mid_pull, mean_bar, obs_pull, mid_bar, gap], axis=0)),
        TN,
    )
    weight_bar = (0.5 * cov) * sym_ref[...] + 0.5 * outer
    scale_bar = -0.5 * total(weight_bar * transform_ref[...])
    polar_bar = weight_bar * per_root
    left = dot3(approach_parts, split(polar_bar))
    both = left + left.T
    approach = approach_ref[...]
    approach_bar = (
        P1 * polar_bar
        + P2 * both
        + dot3(square_parts, split(P3 * polar_bar + P4 * both))
        + dot3(split(both), split(P3 * approach + P4 * square))
    )
    scale_bar = (scale_bar - total(approach_bar * approach_ref[...])) * per_norm
    sym_bar = (2.0 * per_norm) * (approach_bar + scale_bar * system[...])
    sym_ref[...] = sym_bar

    cot_total = jnp.zeros((1, CELLS), f32)
    for n in range(4):
        value = cot_block(gathered_ref, n)
        cot_total += column_sum(value)
        upper, lower = split(value)
        cot_upper[n * B : (n + 1) * B] = upper
        cot_lower[n * B : (n + 1) * B] = lower
    mine = pl.ds(pl.multiple_of(own * B, B), B)
    rows = jnp.concatenate(
        [transform_ref[mine], column_sum(transform_ref[...]), jnp.zeros((7, TOTAL), f32)], axis=0
    )
    mixed = dot3(split(rows), (cot_upper[...], cot_lower[...]))
    columns = dot3(split(transform_ref[mine]), split(mids), NT)
    weight_sum = jnp.sum(ends[0:1], axis=1, keepdims=True)
    anom_total = mixed[B : B + 1] + (weight_sum / cov) * cot_total
    shared = (cot_total - anom_total) / TOTAL
    rows = jnp.concatenate([sym_ref[mine], column_sum(sym_bar), pull_bar, zeros], axis=0)
    pulled = dot3(split(rows), split(anom_ref[...]))
    innovation, precision = innovation_ref[...], precision_ref[...]
    weight = precision / cov
    pull_sum = jnp.sum(pull_bar, axis=1, keepdims=True)
    obs_total = pulled[B : B + 1] + pull_sum * innovation
    mean_part = -(obs_total * weight) - precision * pulled[B + 1 : B + 2]
    observed_bar = (pulled[:B] + columns[:, 1:2] * innovation) * weight + mean_part / TOTAL
    bent = tanh_ref[...]
    picked_bar = observed_bar * (1.0 + 0.5 * (1.0 - bent * bent))
    upper, lower = split(picked_bar)
    onehot = onehot_of(sites_ref[...])
    field = mixed[:B] + (columns[:, 0:1] / cov) * cot_total + shared
    out_ref[...] = ocean_ref[...] * (field + (dot(upper, onehot) + dot(lower, onehot)))


def coef_sums(weight, center, north, south):
    base = column_sum(weight * center)
    return [
        column_sum(weight * north) - base,
        column_sum(weight * south) - base,
        column_sum(weight * west_of(center)) - base,
        column_sum(weight * east_of(center)) - base,
    ]


def coef_kernel(
    bar_ref, north_ref, south_ref, field_ref, first_ref, prior_ref, prior_north_ref, prior_south_ref,
    first_bar_ref, coef_ref,
):
    bars = (
        [row_block(north_ref[...], r) for r in range(2)]
        + [row_block(bar_ref[...], r) for r in range(4)]
        + [row_block(south_ref[...], r) for r in range(2)]
    )
    prior = (
        [row_block(prior_north_ref[...], 1)]
        + [row_block(prior_ref[...], r) for r in range(4)]
        + [row_block(prior_south_ref[...], 0)]
    )
    first_bars = []
    for row in range(1, 7):
        value = field_ref[4:5, row * B : (row + 1) * B] * transposed(
            field_ref, row, bars[row], bars[row - 1], bars[row + 1]
        )
        first_bar_ref[:, (row - 1) * B : row * B] = value
        first_bars.append(value)
    for row in range(4):
        second = coef_sums(
            bars[row + 2],
            row_block(first_ref[...], row + 1),
            row_block(first_ref[...], row),
            row_block(first_ref[...], row + 2),
        )
        first = coef_sums(first_bars[row + 1], prior[row + 1], prior[row], prior[row + 2])
        for k in range(4):
            for copy in range(4):
                coef_ref[copy, k * 4 + row : k * 4 + row + 1] = second[k] + first[k]


def transposed(field_ref, row, center, north, south):
    return transpose_row(
        center,
        north,
        south,
        coef_rows(field_ref, row),
        field_ref[1:2, (row - 1) * B : row * B],
        field_ref[0:1, (row + 1) * B : (row + 2) * B],
    )


def grad_kernel(first_bar_ref, field_ref, grad_ref):
    bars = [row_block(first_bar_ref[...], row) for row in range(6)]
    for row in range(4):
        grad_ref[:, row, :] = transposed(
            field_ref, row + 2, bars[row + 1], bars[row], bars[row + 2]
        )


def call(kernel, outs, scratch=(), smem=False, place=pltpu.VMEM):
    def shaped(s):
        return jax.ShapeDtypeStruct(s, f32)

    def run(*operands):
        specs = [pl.BlockSpec(memory_space=place)] * len(operands)
        if smem:
            specs[0] = pl.BlockSpec(memory_space=pltpu.SMEM)
        single = isinstance(outs[0], int)
        return pl.pallas_call(
            kernel,
            out_shape=shaped(outs) if single else [shaped(s) for s in outs],
            in_specs=specs,
            out_specs=pl.BlockSpec(memory_space=pltpu.VMEM)
            if single
            else [pl.BlockSpec(memory_space=pltpu.VMEM)] * len(outs),
            scratch_shapes=list(scratch),
            compiler_params=pltpu.CompilerParams(vmem_limit_bytes=40 * 1024 * 1024),
        )(*operands)

    return run


def edge_kernel(
    prior_any, coef_any, mask_any, prior_out, field_ref, forward_ref, backward_ref,
    prior_ref, coef_ref, mask_ref, sems,
):
    moves = [
        pltpu.make_async_copy(source, target, sems.at[i])
        for i, (source, target) in enumerate(
            ((prior_any, prior_ref), (coef_any, coef_ref), (mask_any, mask_ref))
        )
    ]
    for move in moves:
        move.start()
    for move in moves:
        move.wait()
    members = prior_ref.shape[0]
    mask = mask_ref[...].astype(f32)
    for row in range(4):
        cells = slice(row * B, (row + 1) * B)
        value = prior_ref[:, row, :]
        rows = jnp.concatenate(
            [coef_ref[k, row : row + 1, :] for k in range(4)]
            + [mask[row : row + 1], jnp.zeros((3, B), f32)],
            axis=0,
        )
        prior_out[:, cells] = value
        field_ref[:, cells] = rows
        side = backward_ref if row < 2 else forward_ref
        cells = slice((row % 2) * B, (row % 2 + 1) * B)
        side[:members, cells] = value
        side[members:, cells] = rows


def rows_kernel(cot_ref, out_ref):
    for row in range(4):
        out_ref[row * B : (row + 1) * B] = cot_ref[:, row, :]


def exchange(forward_edge, backward_edge):
    count = lax.axis_size(STRIPS)
    forward = [(i, i + 1) for i in range(count - 1)]
    backward = [(target, source) for source, target in forward]
    return lax.ppermute(forward_edge, STRIPS, forward), lax.ppermute(backward_edge, STRIPS, backward)


def trade(parts, axes):
    return lax.all_to_all(parts, axes, 0, 0, tiled=True)


def copies(value, count):
    return jnp.broadcast_to(value[None], (count,) + value.shape)


def strip_sum(payload):
    piece = jnp.sum(trade(payload.reshape(16, PART, B), ("y", "z_low", "core")), axis=0)
    summed = jnp.sum(trade(copies(piece, lax.axis_size("z")), "z"), axis=0)
    mine = trade(copies(summed, 32), ("z_low", "y", "x"))
    return mine, lax.ppermute(mine, "core", [(0, 1), (1, 0)])


def local(
    prior_ensemble,
    stencil_factors,
    sea_mask,
    measured_site_positions,
    measured_data,
    measurement_precision,
    cotangent,
):
    members = prior_ensemble.shape[0]
    own = lax.axis_index("x")
    place = jnp.stack([own, lax.axis_index("core")]).astype(jnp.int32)
    prior, own_field, forward_edge, backward_edge = call(
        edge_kernel,
        [(members, CELLS), (8, CELLS), (members + 8, 2 * B), (members + 8, 2 * B)],
        scratch=[
            pltpu.VMEM((members, 4, B), f32),
            pltpu.VMEM((4, 4, B), f32),
            pltpu.VMEM((4, B), jnp.int32),
            pltpu.SemaphoreType.DMA((3,)),
        ],
        place=pl.ANY,
    )(prior_ensemble, stencil_factors, sea_mask)
    north, south = exchange(forward_edge, backward_edge)
    field = jnp.concatenate([north[members:], own_field, south[members:]], axis=1)
    prior_north, prior_south = north[:members], south[:members]
    ocean = own_field[4:5]
    cot_rows = call(rows_kernel, (4 * members, B))(cotangent)

    sites = measured_site_positions.reshape(B, 1)
    precision = measurement_precision.reshape(1, B)
    data = measured_data.reshape(1, B)

    first, state, bent, outgoing = call(
        forecast_kernel, [(members, 6 * B), (members, CELLS), (B, B), (4, OBS_ROWS + 4 * members, B)]
    )(prior, prior_north, prior_south, field, sites, cot_rows)
    gathered = trade(outgoing, "x")
    payload, anom, innovation = call(
        partial_kernel, [(PAYLOAD_ROWS, B), (TOTAL, B), (1, B)], smem=True
    )(place, gathered, state, data, precision)
    mine, other = strip_sum(payload)
    square = (TOTAL, TOTAL)
    bar = call(
        assimilate_kernel,
        (members, CELLS),
        scratch=[pltpu.VMEM((4, PAYLOAD_ROWS, B), f32)]
        + [pltpu.VMEM(square, f32)] * 4
        + [pltpu.VMEM(square, jnp.bfloat16)] * 2,
        smem=True,
    )(place, mine, other, gathered, anom, innovation, precision, bent, sites, ocean)
    bar_north, bar_south = exchange(bar[:, 2 * B :], bar[:, : 2 * B])
    first_bar, coef = call(coef_kernel, [(members, 6 * B), (4, 16, B)])(
        bar, bar_north, bar_south, field, first, prior, prior_north, prior_south
    )
    grad = call(grad_kernel, (members, 4, B))(first_bar, field)
    coef = jnp.sum(trade(coef, "x"), axis=0)
    return (
        grad,
        coef.reshape(4, 4, B) / jnp.sqrt(jnp.float32(TOTAL)),
    )


def solution(mesh):
    strips, parts = mesh.devices.shape
    grid = Mesh(mesh.devices.reshape(strips // 16, 2, 4, 2, parts), STRIPS + ("x",))
    placed = (
        P("x", STRIPS, None),
        P(None, STRIPS, None),
        P(STRIPS, None),
        P(STRIPS, None),
        P(STRIPS),
        P(STRIPS),
        P("x", STRIPS, None),
    )
    return jax.shard_map(
        local,
        mesh=grid,
        in_specs=placed,
        out_specs=(P("x", STRIPS, None), P(None, STRIPS, None)),
        check_vma=False,
    )
```

```python
import jax
import jax.numpy as jnp
from jax import lax
from jax.experimental import pallas as pl
from jax.experimental.pallas import tpu as pltpu
from jax.sharding import Mesh
from jax.sharding import PartitionSpec as P

TOTAL = 512
B = 128
CELLS = 512
STRIPS = ("z", "z_low", "y", "core")
GRAM_ROWS = 320
PULL_ROW = GRAM_ROWS + 512
PAYLOAD_ROWS = 896
PART = PAYLOAD_ROWS // 16
HALF = B // 2
OBS_ROWS = B + 8
VMEM_BYTES = 40 * 1024 * 1024
P1, P2, P3, P4 = -2.4375, 1.6875, -0.5625, 0.0625
NN = (((1,), (0,)), ((), ()))
NT = (((1,), (1,)), ((), ()))
TN = (((0,), (0,)), ((), ()))
f32 = jnp.float32


def split(value):
    upper = value.astype(jnp.bfloat16)
    return upper, (value - upper.astype(f32)).astype(jnp.bfloat16)


def dot(left, right, dims=NN):
    return lax.dot_general(left, right, dims, preferred_element_type=f32)


def dot3(left, right, dims=NN):
    lu, ll = left
    ru, rl = right
    return dot(lu, ru, dims) + (dot(lu, rl, dims) + dot(ll, ru, dims))


def total(value):
    return jnp.sum(jnp.sum(value, axis=0, keepdims=True), axis=1, keepdims=True)


def column_sum(value):
    return jnp.sum(value, axis=0, keepdims=True)


def row_block(value, row):
    return value[:, row * B : (row + 1) * B]


def west_of(center):
    column = lax.broadcasted_iota(jnp.int32, center.shape, 1)
    return jnp.where(column == 0, 0.0, pltpu.roll(center, 1, 1))


def east_of(center):
    column = lax.broadcasted_iota(jnp.int32, center.shape, 1)
    return jnp.where(column == B - 1, 0.0, pltpu.roll(center, B - 1, 1))


def substep_row(center, north, south, coef, ocean):
    kept = 1.0 - coef[0] - coef[1] - coef[2] - coef[3]
    return ocean * (
        kept * center
        + coef[0] * north
        + coef[1] * south
        + coef[2] * west_of(center)
        + coef[3] * east_of(center)
    )


def transpose_row(center, north, south, coef, coef_north, coef_south):
    kept = 1.0 - coef[0] - coef[1] - coef[2] - coef[3]
    return (
        kept * center
        + coef_south * south
        + coef_north * north
        + east_of(coef[2] * center)
        + west_of(coef[3] * center)
    )


def onehot_of(sites):
    cell = lax.broadcasted_iota(jnp.int32, (CELLS, B), 0)
    return jnp.where(cell == sites, 1.0, 0.0).astype(jnp.bfloat16)


def coef_rows(field_ref, row):
    return [field_ref[k : k + 1, row * B : (row + 1) * B] for k in range(4)]


def forecast_kernel(prior_ref, north_ref, south_ref, field_ref, sites_ref, first_ref, state_ref, tanh_ref, out_ref):
    prior = (
        [row_block(north_ref[...], r) for r in range(2)]
        + [row_block(prior_ref[...], r) for r in range(4)]
        + [row_block(south_ref[...], r) for r in range(2)]
    )
    first = []
    for row in range(1, 7):
        value = substep_row(
            prior[row],
            prior[row - 1],
            prior[row + 1],
            coef_rows(field_ref, row),
            field_ref[4:5, row * B : (row + 1) * B],
        )
        first_ref[:, (row - 1) * B : row * B] = value
        first.append(value)
    onehot = onehot_of(sites_ref[...])
    picked = jnp.zeros((B, B), f32)
    sums = []
    for row in range(4):
        value = substep_row(
            first[row + 1],
            first[row],
            first[row + 2],
            coef_rows(field_ref, row + 2),
            field_ref[4:5, (row + 2) * B : (row + 3) * B],
        )
        state_ref[:, row * B : (row + 1) * B] = value
        upper, rest = split(value)
        lower = (value - upper.astype(f32) - rest.astype(f32)).astype(jnp.bfloat16)
        here = onehot[row * B : (row + 1) * B]
        picked += dot(upper, here) + (dot(rest, here) + dot(lower, here))
        sums.append(column_sum(value))
    bent = jnp.tanh(picked)
    tanh_ref[...] = bent
    observed = picked + 0.5 * bent
    sums = jnp.concatenate(sums + [jnp.zeros((4, B), f32)], axis=0)
    for copy in range(4):
        out_ref[copy, :B] = observed
        out_ref[copy, B:] = sums


def partial_kernel(
    own_ref, gathered_ref, state_ref, cot_ref, data_ref, precision_ref,
    payload_ref, anom_ref, innovation_ref,
):
    own = own_ref[0]
    root = jnp.sqrt(jnp.full((1, 1), TOTAL - 1, f32))
    sums = column_sum(gathered_ref[0, :B])
    cells = gathered_ref[0, B:]
    for m in range(1, 4):
        sums += column_sum(gathered_ref[m, :B])
        cells += gathered_ref[m, B:]
    observed_mean = sums / TOTAL
    precision = precision_ref[...]
    weight = precision / root
    innovation = precision * (data_ref[...] - observed_mean)
    innovation_ref[...] = innovation
    for m in range(4):
        anom_ref[m * B : (m + 1) * B] = (gathered_ref[m, :B] - observed_mean) * weight

    def members(start, count):
        return anom_ref[pl.ds(pl.multiple_of(start, B // 2), count)]

    mine = members(own * B, B)
    mine_parts = split(mine)
    payload_ref[:B] = dot3(mine_parts, mine_parts, NT)
    after = lax.rem(own + 1, 4)
    payload_ref[B : 2 * B] = dot3(mine_parts, split(members(after * B, B)), NT)
    low = lax.rem(own, 2)
    half = members(low * B + (own // 2) * HALF, HALF)
    payload_ref[2 * B : GRAM_ROWS] = dot3(split(half), split(members(low * B + 2 * B, B)), NT)
    payload_ref[PULL_ROW : PULL_ROW + 8] = dot3(
        split(jnp.broadcast_to(innovation, (8, B))), mine_parts, NT
    )
    payload_ref[PULL_ROW + 8 :] = jnp.zeros((PAYLOAD_ROWS - PULL_ROW - 8, B), f32)
    deviations = jnp.concatenate(
        [
            (row_block(state_ref[...], r) - cells[r : r + 1] / TOTAL) / root
            for r in range(4)
        ],
        axis=1,
    )
    parts = split(deviations)
    for n in range(4):
        payload_ref[GRAM_ROWS + n * B : GRAM_ROWS + (n + 1) * B] = dot3(
            parts, split(cot_ref[n]), NT
        )


def assimilate_kernel(
    place_ref, mine_ref, other_ref, cot_ref, anom_ref, innovation_ref,
    precision_ref, tanh_ref, sites_ref, ocean_ref,
    out_ref,
    blocks, system, approach_ref, sym_ref, transform_ref, cot_upper, cot_lower,
):
    own, core = place_ref[0], place_ref[1]
    for p in range(8):
        here = pl.ds(pl.multiple_of((p * 2 + core) * PART, 8), PART)
        there = pl.ds(pl.multiple_of((p * 2 + 1 - core) * PART, 8), PART)
        spot = ((p % 2) * 4 + p // 2) * 4
        for x in range(4):
            blocks[x, here] = mine_ref[spot + x]
            blocks[x, there] = other_ref[spot + x]

    def put(m, n, value):
        system[m * B : (m + 1) * B, n * B : (n + 1) * B] = value

    diagonal = (
        lax.broadcasted_iota(jnp.int32, (B, B), 0) == lax.broadcasted_iota(jnp.int32, (B, B), 1)
    )
    for m in range(4):
        put(m, m, blocks[m, :B] + jnp.where(diagonal, 1.0, 0.0))
        n = (m + 1) % 4
        following = blocks[m, B : 2 * B]
        put(m, n, following)
        put(n, m, following.T)
    for m in range(2):
        across = jnp.concatenate(
            [blocks[m, 2 * B : GRAM_ROWS], blocks[m + 2, 2 * B : GRAM_ROWS]], axis=0
        )
        put(m, m + 2, across)
        put(m + 2, m, across.T)

    sums = [jnp.zeros((1, B), f32) for _ in range(4)]

    def cross(m, n):
        return blocks[m, GRAM_ROWS + n * B : GRAM_ROWS + (n + 1) * B]

    for m in range(4):
        for n in range(m, 4):
            turned = cross(m, n).T
            sums[m] += column_sum(turned)
            if n == m:
                sym_ref[m * B : (m + 1) * B, m * B : (m + 1) * B] = cross(m, m) + turned
            else:
                back = cross(n, m)
                back_turned = back.T
                sums[n] += column_sum(back_turned)
                sym_ref[m * B : (m + 1) * B, n * B : (n + 1) * B] = cross(m, n) + back_turned
                sym_ref[n * B : (n + 1) * B, m * B : (m + 1) * B] = back + turned
    mean_bar = jnp.concatenate(sums, axis=1)
    obs_pull = jnp.concatenate([blocks[m, PULL_ROW : PULL_ROW + 1] for m in range(4)], axis=1)

    full = system[...]
    norm = jnp.sqrt(total(full * full))
    root = jnp.sqrt(norm)
    per_norm, per_root = 1.0 / norm, 1.0 / root
    cov = jnp.sqrt(jnp.full((1, 1), TOTAL - 1, f32))
    approach = full * per_norm
    approach_ref[...] = approach
    approach_parts = split(approach)
    square = dot3(approach_parts, approach_parts)
    square_parts = split(square)
    identity = jnp.where(
        lax.broadcasted_iota(jnp.int32, (TOTAL, TOTAL), 0)
        == lax.broadcasted_iota(jnp.int32, (TOTAL, TOTAL), 1),
        1.0,
        0.0,
    )
    inner = split(P2 * identity + P3 * approach + P4 * square)
    transform = (2.25 * identity + P1 * approach + dot3(square_parts, inner)) * per_root
    transform_ref[...] = transform
    transform_parts = split(transform)
    zeros = jnp.zeros((6, TOTAL), f32)
    mids = dot3(split(jnp.concatenate([obs_pull, mean_bar, zeros], axis=0)), transform_parts)
    ends = dot3(split(mids), transform_parts)
    mid_pull, mid_bar = mids[0:1], mids[1:2]
    pull_bar = ends[1:2]
    gap = jnp.zeros((4, TOTAL), f32)
    outer = dot3(
        split(jnp.concatenate([mean_bar, mid_pull, mid_bar, obs_pull, gap], axis=0)),
        split(jnp.concatenate([mid_pull, mean_bar, obs_pull, mid_bar, gap], axis=0)),
        TN,
    )
    weight_bar = (0.5 * cov) * sym_ref[...] + 0.5 * outer
    scale_bar = -0.5 * total(weight_bar * transform_ref[...])
    polar_bar = weight_bar * per_root
    left = dot3(approach_parts, split(polar_bar))
    both = left + left.T
    approach = approach_ref[...]
    approach_bar = (
        P1 * polar_bar
        + P2 * both
        + dot3(square_parts, split(P3 * polar_bar + P4 * both))
        + dot3(split(both), split(P3 * approach + P4 * square))
    )
    scale_bar = (scale_bar - total(approach_bar * approach_ref[...])) * per_norm
    sym_bar = (2.0 * per_norm) * (approach_bar + scale_bar * system[...])
    sym_ref[...] = sym_bar

    cot_total = jnp.zeros((1, CELLS), f32)
    for n in range(4):
        value = cot_ref[n]
        cot_total += column_sum(value)
        upper, lower = split(value)
        cot_upper[n * B : (n + 1) * B] = upper
        cot_lower[n * B : (n + 1) * B] = lower
    mine = pl.ds(pl.multiple_of(own * B, B), B)
    rows = jnp.concatenate(
        [transform_ref[mine], column_sum(transform_ref[...]), jnp.zeros((7, TOTAL), f32)], axis=0
    )
    mixed = dot3(split(rows), (cot_upper[...], cot_lower[...]))
    columns = dot3(split(transform_ref[mine]), split(mids), NT)
    weight_sum = jnp.sum(ends[0:1], axis=1, keepdims=True)
    anom_total = mixed[B : B + 1] + (weight_sum / cov) * cot_total
    shared = (cot_total - anom_total) / TOTAL
    rows = jnp.concatenate([sym_ref[mine], column_sum(sym_bar), pull_bar, zeros], axis=0)
    pulled = dot3(split(rows), split(anom_ref[...]))
    innovation, precision = innovation_ref[...], precision_ref[...]
    weight = precision / cov
    pull_sum = jnp.sum(pull_bar, axis=1, keepdims=True)
    obs_total = pulled[B : B + 1] + pull_sum * innovation
    mean_part = -(obs_total * weight) - precision * pulled[B + 1 : B + 2]
    observed_bar = (pulled[:B] + columns[:, 1:2] * innovation) * weight + mean_part / TOTAL
    bent = tanh_ref[...]
    picked_bar = observed_bar * (1.0 + 0.5 * (1.0 - bent * bent))
    upper, lower = split(picked_bar)
    onehot = onehot_of(sites_ref[...])
    field = mixed[:B] + (columns[:, 0:1] / cov) * cot_total + shared
    out_ref[...] = ocean_ref[...] * (field + (dot(upper, onehot, NT) + dot(lower, onehot, NT)))


def coef_sums(weight, center, north, south):
    base = column_sum(weight * center)
    return [
        column_sum(weight * north) - base,
        column_sum(weight * south) - base,
        column_sum(weight * west_of(center)) - base,
        column_sum(weight * east_of(center)) - base,
    ]


def coef_kernel(
    bar_ref, north_ref, south_ref, field_ref, first_ref, prior_ref, prior_north_ref, prior_south_ref,
    first_bar_ref, coef_ref,
):
    bars = (
        [row_block(north_ref[...], r) for r in range(2)]
        + [row_block(bar_ref[...], r) for r in range(4)]
        + [row_block(south_ref[...], r) for r in range(2)]
    )
    prior = (
        [row_block(prior_north_ref[...], 1)]
        + [row_block(prior_ref[...], r) for r in range(4)]
        + [row_block(prior_south_ref[...], 0)]
    )
    first_bars = []
    for row in range(1, 7):
        value = field_ref[4:5, row * B : (row + 1) * B] * transposed(
            field_ref, row, bars[row], bars[row - 1], bars[row + 1]
        )
        first_bar_ref[:, (row - 1) * B : row * B] = value
        first_bars.append(value)
    for row in range(4):
        second = coef_sums(
            bars[row + 2],
            row_block(first_ref[...], row + 1),
            row_block(first_ref[...], row),
            row_block(first_ref[...], row + 2),
        )
        first = coef_sums(first_bars[row + 1], prior[row + 1], prior[row], prior[row + 2])
        for k in range(4):
            for copy in range(4):
                coef_ref[copy, k * 4 + row : k * 4 + row + 1] = second[k] + first[k]


def transposed(field_ref, row, center, north, south):
    return transpose_row(
        center,
        north,
        south,
        coef_rows(field_ref, row),
        field_ref[1:2, (row - 1) * B : row * B],
        field_ref[0:1, (row + 1) * B : (row + 2) * B],
    )


def grad_kernel(first_bar_ref, field_ref, grad_ref):
    bars = [row_block(first_bar_ref[...], row) for row in range(6)]
    for row in range(4):
        grad_ref[:, row, :] = transposed(
            field_ref, row + 2, bars[row + 1], bars[row], bars[row + 2]
        )


def call(kernel, outs, scratch=(), smem=False, place=pltpu.VMEM):
    def shaped(s):
        return jax.ShapeDtypeStruct(s, f32)

    def run(*operands):
        specs = [pl.BlockSpec(memory_space=place)] * len(operands)
        if smem:
            specs[0] = pl.BlockSpec(memory_space=pltpu.SMEM)
        single = isinstance(outs[0], int)
        return pl.pallas_call(
            kernel,
            out_shape=shaped(outs) if single else [shaped(s) for s in outs],
            in_specs=specs,
            out_specs=pl.BlockSpec(memory_space=pltpu.VMEM)
            if single
            else [pl.BlockSpec(memory_space=pltpu.VMEM)] * len(outs),
            scratch_shapes=list(scratch),
            compiler_params=None if place is pl.ANY else pltpu.CompilerParams(vmem_limit_bytes=VMEM_BYTES),
        )(*operands)

    return run


def edge_kernel(
    prior_any, coef_any, mask_any, prior_out, field_ref, forward_ref, backward_ref,
    prior_ref, coef_ref, mask_ref, sems,
):
    moves = [
        pltpu.make_async_copy(source, target, sems.at[i])
        for i, (source, target) in enumerate(
            ((prior_any, prior_ref), (coef_any, coef_ref), (mask_any, mask_ref))
        )
    ]
    for move in moves:
        move.start()
    for move in moves:
        move.wait()
    members = prior_ref.shape[0]
    mask = mask_ref[...].astype(f32)
    for row in range(4):
        cells = slice(row * B, (row + 1) * B)
        value = prior_ref[:, row, :]
        rows = jnp.concatenate(
            [coef_ref[k, row : row + 1, :] for k in range(4)]
            + [mask[row : row + 1], jnp.zeros((3, B), f32)],
            axis=0,
        )
        prior_out[:, cells] = value
        field_ref[:, cells] = rows
        side = backward_ref if row < 2 else forward_ref
        cells = slice((row % 2) * B, (row % 2 + 1) * B)
        side[:members, cells] = value
        side[members:, cells] = rows


def spread_kernel(cot_ref, out_ref):
    for row in range(4):
        value = cot_ref[:, row, :]
        for copy in range(4):
            out_ref[copy, :, row * B : (row + 1) * B] = value


def exchange(forward_edge, backward_edge):
    count = lax.axis_size(STRIPS)
    forward = [(i, i + 1) for i in range(count - 1)]
    backward = [(target, source) for source, target in forward]
    return lax.ppermute(forward_edge, STRIPS, forward), lax.ppermute(backward_edge, STRIPS, backward)


def trade(parts, axes):
    return lax.all_to_all(parts, axes, 0, 0, tiled=True)


def copies(value, count):
    return jnp.broadcast_to(value[None], (count,) + value.shape)


def strip_sum(payload):
    piece = jnp.sum(trade(payload.reshape(16, PART, B), ("y", "z_low", "core")), axis=0)
    summed = jnp.sum(trade(copies(piece, lax.axis_size("z")), "z"), axis=0)
    mine = trade(copies(summed, 32), ("z_low", "y", "x"))
    return mine, lax.ppermute(mine, "core", [(0, 1), (1, 0)])


def local(
    prior_ensemble,
    stencil_factors,
    sea_mask,
    measured_site_positions,
    measured_data,
    measurement_precision,
    cotangent,
):
    members = prior_ensemble.shape[0]
    own = lax.axis_index("x")
    place = jnp.stack([own, lax.axis_index("core")]).astype(jnp.int32)
    prior, own_field, forward_edge, backward_edge = call(
        edge_kernel,
        [(members, CELLS), (8, CELLS), (members + 8, 2 * B), (members + 8, 2 * B)],
        scratch=[
            pltpu.VMEM((members, 4, B), f32),
            pltpu.VMEM((4, 4, B), f32),
            pltpu.VMEM((4, B), jnp.int32),
            pltpu.SemaphoreType.DMA((3,)),
        ],
        place=pl.ANY,
    )(prior_ensemble, stencil_factors, sea_mask)
    north, south = exchange(forward_edge, backward_edge)
    field = jnp.concatenate([north[members:], own_field, south[members:]], axis=1)
    prior_north, prior_south = north[:members], south[:members]
    ocean = own_field[4:5]
    cots = trade(call(spread_kernel, (4, members, CELLS))(cotangent), "x")

    sites = measured_site_positions
    precision = measurement_precision.reshape(1, B)
    data = measured_data.reshape(1, B)

    first, state, bent, outgoing = call(
        forecast_kernel, [(members, 6 * B), (members, CELLS), (B, B), (4, OBS_ROWS, B)]
    )(prior, prior_north, prior_south, field, sites)
    outgoing, cots = lax.optimization_barrier((outgoing, cots))
    gathered = trade(outgoing, "x")
    payload, anom, innovation = call(
        partial_kernel, [(PAYLOAD_ROWS, B), (TOTAL, B), (1, B)], smem=True
    )(place, gathered, state, cots, data, precision)
    mine, other = strip_sum(payload)
    square = (TOTAL, TOTAL)
    bar = call(
        assimilate_kernel,
        (members, CELLS),
        scratch=[pltpu.VMEM((4, PAYLOAD_ROWS, B), f32)]
        + [pltpu.VMEM(square, f32)] * 4
        + [pltpu.VMEM(square, jnp.bfloat16)] * 2,
        smem=True,
    )(place, mine, other, cots, anom, innovation, precision, bent, sites, ocean)
    bar_north, bar_south = exchange(bar[:, 2 * B :], bar[:, : 2 * B])
    first_bar, coef = call(coef_kernel, [(members, 6 * B), (4, 16, B)])(
        bar, bar_north, bar_south, field, first, prior, prior_north, prior_south
    )
    grad = call(grad_kernel, (members, 4, B))(first_bar, field)
    coef = jnp.sum(trade(coef, "x"), axis=0)
    return (
        grad,
        coef.reshape(4, 4, B) / jnp.sqrt(jnp.float32(TOTAL)),
    )


def solution(mesh):
    strips, parts = mesh.devices.shape
    grid = Mesh(mesh.devices.reshape(strips // 16, 2, 4, 2, parts), STRIPS + ("x",))
    placed = (
        P("x", STRIPS, None),
        P(None, STRIPS, None),
        P(STRIPS, None),
        P(STRIPS, None),
        P(STRIPS),
        P(STRIPS),
        P("x", STRIPS, None),
    )
    return jax.shard_map(
        local,
        mesh=grid,
        in_specs=placed,
        out_specs=(P("x", STRIPS, None), P(None, STRIPS, None)),
        check_vma=False,
    )
```

```python
import jax
import jax.numpy as jnp
from jax import lax
from jax.experimental import pallas as pl
from jax.experimental.pallas import tpu as pltpu
from jax.sharding import Mesh
from jax.sharding import PartitionSpec as P

TOTAL = 512
B = 128
CELLS = 512
STRIPS = ("z", "z_low", "y", "core")
GRAM_ROWS = 320
PULL_ROW = GRAM_ROWS + 512
PAYLOAD_ROWS = 896
PART = PAYLOAD_ROWS // 16
HALF = B // 2
OBS_ROWS = B + 8
VMEM_BYTES = 24 * 1024 * 1024
P1, P2, P3, P4 = -2.4375, 1.6875, -0.5625, 0.0625
NN = (((1,), (0,)), ((), ()))
NT = (((1,), (1,)), ((), ()))
TN = (((0,), (0,)), ((), ()))
f32 = jnp.float32


def split(value):
    upper = value.astype(jnp.bfloat16)
    return upper, (value - upper.astype(f32)).astype(jnp.bfloat16)


def dot(left, right, dims=NN):
    return lax.dot_general(left, right, dims, preferred_element_type=f32)


def dot3(left, right, dims=NN):
    lu, ll = left
    ru, rl = right
    return dot(lu, ru, dims) + (dot(lu, rl, dims) + dot(ll, ru, dims))


def total(value):
    return jnp.sum(jnp.sum(value, axis=0, keepdims=True), axis=1, keepdims=True)


def column_sum(value):
    return jnp.sum(value, axis=0, keepdims=True)


def row_block(value, row):
    return value[:, row * B : (row + 1) * B]


def west_of(center):
    column = lax.broadcasted_iota(jnp.int32, center.shape, 1)
    return jnp.where(column == 0, 0.0, pltpu.roll(center, 1, 1))


def east_of(center):
    column = lax.broadcasted_iota(jnp.int32, center.shape, 1)
    return jnp.where(column == B - 1, 0.0, pltpu.roll(center, B - 1, 1))


def substep_row(center, north, south, coef, ocean):
    kept = 1.0 - coef[0] - coef[1] - coef[2] - coef[3]
    return ocean * (
        kept * center
        + coef[0] * north
        + coef[1] * south
        + coef[2] * west_of(center)
        + coef[3] * east_of(center)
    )


def transpose_row(center, north, south, coef, coef_north, coef_south):
    kept = 1.0 - coef[0] - coef[1] - coef[2] - coef[3]
    return (
        kept * center
        + coef_south * south
        + coef_north * north
        + east_of(coef[2] * center)
        + west_of(coef[3] * center)
    )


def onehot_of(sites):
    cell = lax.broadcasted_iota(jnp.int32, (CELLS, B), 0)
    return jnp.where(cell == sites, 1.0, 0.0).astype(jnp.bfloat16)


def coef_rows(fields, row):
    return [fields[row][k : k + 1] for k in range(4)]


def field_rows(own_ref, north_ref, south_ref):
    members = north_ref.shape[0] - 8
    return (
        [row_block(north_ref[members:], r) for r in range(2)]
        + [row_block(own_ref[...], r) for r in range(4)]
        + [row_block(south_ref[members:], r) for r in range(2)]
    )


def forecast_kernel(prior_ref, north_ref, south_ref, own_ref, sites_ref, first_ref, state_ref, tanh_ref, out_ref):
    fields = field_rows(own_ref, north_ref, south_ref)
    prior = (
        [row_block(north_ref[:B], r) for r in range(2)]
        + [row_block(prior_ref[...], r) for r in range(4)]
        + [row_block(south_ref[:B], r) for r in range(2)]
    )
    first = []
    for row in range(1, 7):
        value = substep_row(
            prior[row],
            prior[row - 1],
            prior[row + 1],
            coef_rows(fields, row),
            fields[row][4:5],
        )
        first_ref[:, (row - 1) * B : row * B] = value
        first.append(value)
    onehot = onehot_of(sites_ref[...])
    picked = jnp.zeros((B, B), f32)
    sums = []
    for row in range(4):
        value = substep_row(
            first[row + 1],
            first[row],
            first[row + 2],
            coef_rows(fields, row + 2),
            fields[row + 2][4:5],
        )
        state_ref[:, row * B : (row + 1) * B] = value
        upper, rest = split(value)
        lower = (value - upper.astype(f32) - rest.astype(f32)).astype(jnp.bfloat16)
        here = onehot[row * B : (row + 1) * B]
        picked += dot(upper, here) + (dot(rest, here) + dot(lower, here))
        sums.append(column_sum(value))
    bent = jnp.tanh(picked)
    tanh_ref[...] = bent
    observed = picked + 0.5 * bent
    sums = jnp.concatenate(sums + [jnp.zeros((4, B), f32)], axis=0)
    for copy in range(4):
        out_ref[copy, :B] = observed
        out_ref[copy, B:] = sums


def partial_kernel(
    own_ref, gathered_ref, state_ref, cot_ref, data_ref, precision_ref,
    payload_ref, anom_ref, innovation_ref,
):
    own = own_ref[0]
    root = jnp.sqrt(jnp.full((1, 1), TOTAL - 1, f32))
    sums = column_sum(gathered_ref[0, :B])
    cells = gathered_ref[0, B:]
    for m in range(1, 4):
        sums += column_sum(gathered_ref[m, :B])
        cells += gathered_ref[m, B:]
    observed_mean = sums / TOTAL
    precision = precision_ref[...]
    weight = precision / root
    innovation = precision * (data_ref[...] - observed_mean)
    innovation_ref[...] = innovation
    for m in range(4):
        anom_ref[m * B : (m + 1) * B] = (gathered_ref[m, :B] - observed_mean) * weight

    def members(start, count):
        return anom_ref[pl.ds(pl.multiple_of(start, B // 2), count)]

    mine = members(own * B, B)
    mine_parts = split(mine)
    payload_ref[:B] = dot3(mine_parts, mine_parts, NT)
    after = lax.rem(own + 1, 4)
    payload_ref[B : 2 * B] = dot3(mine_parts, split(members(after * B, B)), NT)
    low = lax.rem(own, 2)
    half = members(low * B + (own // 2) * HALF, HALF)
    payload_ref[2 * B : GRAM_ROWS] = dot3(split(half), split(members(low * B + 2 * B, B)), NT)
    payload_ref[PULL_ROW : PULL_ROW + 8] = dot3(
        split(jnp.broadcast_to(innovation, (8, B))), mine_parts, NT
    )
    payload_ref[PULL_ROW + 8 :] = jnp.zeros((PAYLOAD_ROWS - PULL_ROW - 8, B), f32)
    deviations = jnp.concatenate(
        [
            (row_block(state_ref[...], r) - cells[r : r + 1] / TOTAL) / root
            for r in range(4)
        ],
        axis=1,
    )
    parts = split(deviations)
    for n in range(4):
        payload_ref[GRAM_ROWS + n * B : GRAM_ROWS + (n + 1) * B] = dot3(
            parts, split(cot_ref[n]), NT
        )


def assimilate_kernel(
    place_ref, mine_ref, other_ref, cot_ref, anom_ref, innovation_ref,
    precision_ref, tanh_ref, sites_ref, ocean_ref,
    out_ref, forward_ref, backward_ref,
    blocks, system, approach_ref, sym_ref, transform_ref, cot_upper, cot_lower,
):
    own, core = place_ref[0], place_ref[1]
    for p in range(8):
        here = pl.ds(pl.multiple_of((p * 2 + core) * PART, 8), PART)
        there = pl.ds(pl.multiple_of((p * 2 + 1 - core) * PART, 8), PART)
        spot = ((p % 2) * 4 + p // 2) * 4
        for x in range(4):
            blocks[x, here] = mine_ref[spot + x]
            blocks[x, there] = other_ref[spot + x]

    def put(m, n, value):
        system[m * B : (m + 1) * B, n * B : (n + 1) * B] = value

    diagonal = (
        lax.broadcasted_iota(jnp.int32, (B, B), 0) == lax.broadcasted_iota(jnp.int32, (B, B), 1)
    )
    for m in range(4):
        put(m, m, blocks[m, :B] + jnp.where(diagonal, 1.0, 0.0))
        n = (m + 1) % 4
        following = blocks[m, B : 2 * B]
        put(m, n, following)
        put(n, m, following.T)
    for m in range(2):
        across = jnp.concatenate(
            [blocks[m, 2 * B : GRAM_ROWS], blocks[m + 2, 2 * B : GRAM_ROWS]], axis=0
        )
        put(m, m + 2, across)
        put(m + 2, m, across.T)

    sums = [jnp.zeros((1, B), f32) for _ in range(4)]

    def cross(m, n):
        return blocks[m, GRAM_ROWS + n * B : GRAM_ROWS + (n + 1) * B]

    for m in range(4):
        for n in range(m, 4):
            turned = cross(m, n).T
            sums[m] += column_sum(turned)
            if n == m:
                sym_ref[m * B : (m + 1) * B, m * B : (m + 1) * B] = cross(m, m) + turned
            else:
                back = cross(n, m)
                back_turned = back.T
                sums[n] += column_sum(back_turned)
                sym_ref[m * B : (m + 1) * B, n * B : (n + 1) * B] = cross(m, n) + back_turned
                sym_ref[n * B : (n + 1) * B, m * B : (m + 1) * B] = back + turned
    mean_bar = jnp.concatenate(sums, axis=1)
    obs_pull = jnp.concatenate([blocks[m, PULL_ROW : PULL_ROW + 1] for m in range(4)], axis=1)

    full = system[...]
    norm = jnp.sqrt(total(full * full))
    root = jnp.sqrt(norm)
    per_norm, per_root = 1.0 / norm, 1.0 / root
    cov = jnp.sqrt(jnp.full((1, 1), TOTAL - 1, f32))
    approach = full * per_norm
    approach_ref[...] = approach
    approach_parts = split(approach)
    square = dot3(approach_parts, approach_parts)
    square_parts = split(square)
    identity = jnp.where(
        lax.broadcasted_iota(jnp.int32, (TOTAL, TOTAL), 0)
        == lax.broadcasted_iota(jnp.int32, (TOTAL, TOTAL), 1),
        1.0,
        0.0,
    )
    inner = split(P2 * identity + P3 * approach + P4 * square)
    transform = (2.25 * identity + P1 * approach + dot3(square_parts, inner)) * per_root
    transform_ref[...] = transform
    transform_parts = split(transform)
    zeros = jnp.zeros((6, TOTAL), f32)
    mids = dot3(split(jnp.concatenate([obs_pull, mean_bar, zeros], axis=0)), transform_parts)
    ends = dot3(split(mids), transform_parts)
    mid_pull, mid_bar = mids[0:1], mids[1:2]
    pull_bar = ends[1:2]
    gap = jnp.zeros((4, TOTAL), f32)
    outer = dot3(
        split(jnp.concatenate([mean_bar, mid_pull, mid_bar, obs_pull, gap], axis=0)),
        split(jnp.concatenate([mid_pull, mean_bar, obs_pull, mid_bar, gap], axis=0)),
        TN,
    )
    weight_bar = (0.5 * cov) * sym_ref[...] + 0.5 * outer
    scale_bar = -0.5 * total(weight_bar * transform_ref[...])
    polar_bar = weight_bar * per_root
    left = dot3(approach_parts, split(polar_bar))
    both = left + left.T
    approach = approach_ref[...]
    approach_bar = (
        P1 * polar_bar
        + P2 * both
        + dot3(square_parts, split(P3 * polar_bar + P4 * both))
        + dot3(split(both), split(P3 * approach + P4 * square))
    )
    scale_bar = (scale_bar - total(approach_bar * approach_ref[...])) * per_norm
    sym_bar = (2.0 * per_norm) * (approach_bar + scale_bar * system[...])
    sym_ref[...] = sym_bar

    cot_total = jnp.zeros((1, CELLS), f32)
    for n in range(4):
        value = cot_ref[n]
        cot_total += column_sum(value)
        upper, lower = split(value)
        cot_upper[n * B : (n + 1) * B] = upper
        cot_lower[n * B : (n + 1) * B] = lower
    mine = pl.ds(pl.multiple_of(own * B, B), B)
    rows = jnp.concatenate(
        [transform_ref[mine], column_sum(transform_ref[...]), jnp.zeros((7, TOTAL), f32)], axis=0
    )
    mixed = dot3(split(rows), (cot_upper[...], cot_lower[...]))
    columns = dot3(split(transform_ref[mine]), split(mids), NT)
    weight_sum = jnp.sum(ends[0:1], axis=1, keepdims=True)
    anom_total = mixed[B : B + 1] + (weight_sum / cov) * cot_total
    shared = (cot_total - anom_total) / TOTAL
    rows = jnp.concatenate([sym_ref[mine], column_sum(sym_bar), pull_bar, zeros], axis=0)
    pulled = dot3(split(rows), split(anom_ref[...]))
    innovation, precision = innovation_ref[...], precision_ref[...]
    weight = precision / cov
    pull_sum = jnp.sum(pull_bar, axis=1, keepdims=True)
    obs_total = pulled[B : B + 1] + pull_sum * innovation
    mean_part = -(obs_total * weight) - precision * pulled[B + 1 : B + 2]
    observed_bar = (pulled[:B] + columns[:, 1:2] * innovation) * weight + mean_part / TOTAL
    bent = tanh_ref[...]
    picked_bar = observed_bar * (1.0 + 0.5 * (1.0 - bent * bent))
    upper, lower = split(picked_bar)
    onehot = onehot_of(sites_ref[...])
    field = mixed[:B] + (columns[:, 0:1] / cov) * cot_total + shared
    field = field + (dot(upper, onehot, NT) + dot(lower, onehot, NT))
    for row in range(4):
        bar = ocean_ref[4:5, row * B : (row + 1) * B] * row_block(field, row)
        out_ref[:, row * B : (row + 1) * B] = bar
        side = backward_ref if row < 2 else forward_ref
        side[:, (row % 2) * B : (row % 2 + 1) * B] = bar


def coef_sums(weight, center, north, south):
    base = column_sum(weight * center)
    return [
        column_sum(weight * north) - base,
        column_sum(weight * south) - base,
        column_sum(weight * west_of(center)) - base,
        column_sum(weight * east_of(center)) - base,
    ]


def coef_kernel(
    bar_ref, north_ref, south_ref, own_ref, first_ref, prior_ref, prior_north_ref, prior_south_ref,
    first_bar_ref, coef_ref,
):
    fields = field_rows(own_ref, prior_north_ref, prior_south_ref)
    bars = (
        [row_block(north_ref[...], r) for r in range(2)]
        + [row_block(bar_ref[...], r) for r in range(4)]
        + [row_block(south_ref[...], r) for r in range(2)]
    )
    prior = (
        [row_block(prior_north_ref[:B], 1)]
        + [row_block(prior_ref[...], r) for r in range(4)]
        + [row_block(prior_south_ref[:B], 0)]
    )
    first_bars = []
    for row in range(1, 7):
        value = fields[row][4:5] * transposed(
            fields, row, bars[row], bars[row - 1], bars[row + 1]
        )
        first_bar_ref[:, (row - 1) * B : row * B] = value
        first_bars.append(value)
    for row in range(4):
        second = coef_sums(
            bars[row + 2],
            row_block(first_ref[...], row + 1),
            row_block(first_ref[...], row),
            row_block(first_ref[...], row + 2),
        )
        first = coef_sums(first_bars[row + 1], prior[row + 1], prior[row], prior[row + 2])
        for k in range(4):
            for copy in range(4):
                coef_ref[copy, k * 4 + row : k * 4 + row + 1] = second[k] + first[k]


def transposed(fields, row, center, north, south):
    return transpose_row(
        center,
        north,
        south,
        coef_rows(fields, row),
        fields[row - 1][1:2],
        fields[row + 1][0:1],
    )


def grad_kernel(first_bar_ref, own_ref, prior_north_ref, prior_south_ref, grad_ref):
    fields = field_rows(own_ref, prior_north_ref, prior_south_ref)
    bars = [row_block(first_bar_ref[...], row) for row in range(6)]
    for row in range(4):
        grad_ref[:, row, :] = transposed(
            fields, row + 2, bars[row + 1], bars[row], bars[row + 2]
        )


def call(kernel, outs, scratch=(), smem=False):
    def shaped(s):
        return jax.ShapeDtypeStruct(s, f32)

    def run(*operands):
        specs = [pl.BlockSpec(memory_space=pltpu.VMEM)] * len(operands)
        if smem:
            specs[0] = pl.BlockSpec(memory_space=pltpu.SMEM)
        single = isinstance(outs[0], int)
        return pl.pallas_call(
            kernel,
            out_shape=shaped(outs) if single else [shaped(s) for s in outs],
            in_specs=specs,
            out_specs=pl.BlockSpec(memory_space=pltpu.VMEM)
            if single
            else [pl.BlockSpec(memory_space=pltpu.VMEM)] * len(outs),
            scratch_shapes=list(scratch),
            compiler_params=pltpu.CompilerParams(vmem_limit_bytes=VMEM_BYTES),
        )(*operands)

    return run


def edge_kernel(prior_ref, coef_ref, mask_ref, prior_out, field_ref, forward_ref, backward_ref):
    members = prior_ref.shape[0]
    mask = mask_ref[...].astype(f32)
    for row in range(4):
        cells = slice(row * B, (row + 1) * B)
        value = prior_ref[:, row, :]
        rows = jnp.concatenate(
            [coef_ref[k, row : row + 1, :] for k in range(4)]
            + [mask[row : row + 1], jnp.zeros((3, B), f32)],
            axis=0,
        )
        prior_out[:, cells] = value
        field_ref[:, cells] = rows
        side = backward_ref if row < 2 else forward_ref
        cells = slice((row % 2) * B, (row % 2 + 1) * B)
        side[:members, cells] = value
        side[members:, cells] = rows


def spread_kernel(cot_ref, after_ref, out_ref):
    for row in range(4):
        value = cot_ref[:, row, :]
        for copy in range(4):
            out_ref[copy, :, row * B : (row + 1) * B] = value


def exchange(forward_edge, backward_edge):
    count = lax.axis_size(STRIPS)
    forward = [(i, i + 1) for i in range(count - 1)]
    backward = [(target, source) for source, target in forward]
    return lax.ppermute(forward_edge, STRIPS, forward), lax.ppermute(backward_edge, STRIPS, backward)


def trade(parts, axes):
    return lax.all_to_all(parts, axes, 0, 0, tiled=True)


def sum_kernel(parts_ref, out_ref):
    value = parts_ref[0]
    for i in range(1, parts_ref.shape[0]):
        value += parts_ref[i]
    for copy in range(out_ref.shape[0]):
        out_ref[copy] = value


def summed_copies(parts, count):
    return call(sum_kernel, (count,) + parts.shape[1:])(parts)


def strip_sum(payload):
    pieces = trade(payload.reshape(16, PART, B), ("y", "z_low", "core"))
    pairs = trade(summed_copies(pieces, lax.axis_size("z")), "z")
    mine = trade(summed_copies(pairs, 32), ("z_low", "y", "x"))
    return mine, lax.ppermute(mine, "core", [(0, 1), (1, 0)])


def coef_total_kernel(parts_ref, out_ref):
    value = parts_ref[0] + parts_ref[1] + parts_ref[2] + parts_ref[3]
    out_ref[...] = value / jnp.sqrt(jnp.full((1, 1), TOTAL, f32))


def local(
    prior_ensemble,
    stencil_factors,
    sea_mask,
    measured_site_positions,
    measured_data,
    measurement_precision,
    cotangent,
):
    members = prior_ensemble.shape[0]
    own = lax.axis_index("x")
    place = jnp.stack([own, lax.axis_index("core")]).astype(jnp.int32)
    prior, own_field, forward_edge, backward_edge = call(
        edge_kernel,
        [(members, CELLS), (8, CELLS), (members + 8, 2 * B), (members + 8, 2 * B)],
    )(prior_ensemble, stencil_factors, sea_mask)
    north, south = exchange(forward_edge, backward_edge)
    cots = trade(call(spread_kernel, (4, members, CELLS))(cotangent, own_field), "x")

    sites = measured_site_positions
    precision = measurement_precision.reshape(1, B)
    data = measured_data.reshape(1, B)

    first, state, bent, outgoing = call(
        forecast_kernel, [(members, 6 * B), (members, CELLS), (B, B), (4, OBS_ROWS, B)]
    )(prior, north, south, own_field, sites)
    outgoing, cots = lax.optimization_barrier((outgoing, cots))
    gathered = trade(outgoing, "x")
    payload, anom, innovation = call(
        partial_kernel, [(PAYLOAD_ROWS, B), (TOTAL, B), (1, B)], smem=True
    )(place, gathered, state, cots, data, precision)
    mine, other = strip_sum(payload)
    square = (TOTAL, TOTAL)
    bar, bar_forward, bar_backward = call(
        assimilate_kernel,
        [(members, CELLS), (members, 2 * B), (members, 2 * B)],
        scratch=[pltpu.VMEM((4, PAYLOAD_ROWS, B), f32)]
        + [pltpu.VMEM(square, f32)] * 4
        + [pltpu.VMEM(square, jnp.bfloat16)] * 2,
        smem=True,
    )(place, mine, other, cots, anom, innovation, precision, bent, sites, own_field)
    bar_north, bar_south = exchange(bar_forward, bar_backward)
    first_bar, coef = call(coef_kernel, [(members, 6 * B), (4, 16, B)])(
        bar, bar_north, bar_south, own_field, first, prior, north, south
    )
    grad = call(grad_kernel, (members, 4, B))(first_bar, own_field, north, south)
    coef = call(coef_total_kernel, (16, B))(trade(coef, "x"))
    return (
        grad,
        coef.reshape(4, 4, B),
    )


def solution(mesh):
    strips, parts = mesh.devices.shape
    grid = Mesh(mesh.devices.reshape(strips // 16, 2, 4, 2, parts), STRIPS + ("x",))
    placed = (
        P("x", STRIPS, None),
        P(None, STRIPS, None),
        P(STRIPS, None),
        P(STRIPS, None),
        P(STRIPS),
        P(STRIPS),
        P("x", STRIPS, None),
    )
    return jax.shard_map(
        local,
        mesh=grid,
        in_specs=placed,
        out_specs=(P("x", STRIPS, None), P(None, STRIPS, None)),
        check_vma=False,
    )
```

```python
import jax
import jax.numpy as jnp
from jax import lax
from jax.experimental import pallas as pl
from jax.experimental.pallas import tpu as pltpu
from jax.sharding import Mesh
from jax.sharding import PartitionSpec as P

TOTAL = 512
B = 128
CELLS = 512
STRIPS = ("z", "z_low", "y", "core")
GRAM_ROWS = 320
PULL_ROW = GRAM_ROWS + 512
PAYLOAD_ROWS = 896
PART = PAYLOAD_ROWS // 16
HALF = B // 2
OBS_ROWS = B + 8
VMEM_BYTES = 24 * 1024 * 1024
P1, P2, P3, P4 = -2.4375, 1.6875, -0.5625, 0.0625
NN = (((1,), (0,)), ((), ()))
NT = (((1,), (1,)), ((), ()))
TN = (((0,), (0,)), ((), ()))
f32 = jnp.float32


def split(value):
    upper = value.astype(jnp.bfloat16)
    return upper, (value - upper.astype(f32)).astype(jnp.bfloat16)


def dot(left, right, dims=NN):
    return lax.dot_general(left, right, dims, preferred_element_type=f32)


def dot3(left, right, dims=NN):
    lu, ll = left
    ru, rl = right
    return dot(lu, ru, dims) + (dot(lu, rl, dims) + dot(ll, ru, dims))


def total(value):
    return jnp.sum(jnp.sum(value, axis=0, keepdims=True), axis=1, keepdims=True)


def column_sum(value):
    return jnp.sum(value, axis=0, keepdims=True)


def row_block(value, row):
    return value[:, row * B : (row + 1) * B]


def west_of(center):
    column = lax.broadcasted_iota(jnp.int32, center.shape, 1)
    return jnp.where(column == 0, 0.0, pltpu.roll(center, 1, 1))


def east_of(center):
    column = lax.broadcasted_iota(jnp.int32, center.shape, 1)
    return jnp.where(column == B - 1, 0.0, pltpu.roll(center, B - 1, 1))


def substep_row(center, north, south, coef, ocean):
    kept = 1.0 - coef[0] - coef[1] - coef[2] - coef[3]
    return ocean * (
        kept * center
        + coef[0] * north
        + coef[1] * south
        + coef[2] * west_of(center)
        + coef[3] * east_of(center)
    )


def transpose_row(center, north, south, coef, coef_north, coef_south):
    kept = 1.0 - coef[0] - coef[1] - coef[2] - coef[3]
    return (
        kept * center
        + coef_south * south
        + coef_north * north
        + east_of(coef[2] * center)
        + west_of(coef[3] * center)
    )


def onehot_of(sites):
    cell = lax.broadcasted_iota(jnp.int32, (CELLS, B), 0)
    return jnp.where(cell == sites, 1.0, 0.0).astype(jnp.bfloat16)


def coef_rows(fields, row):
    return [fields[row][k : k + 1] for k in range(4)]


def field_rows(own_ref, north_ref, south_ref):
    members = north_ref.shape[0] - 8
    return (
        [row_block(north_ref[members:], r) for r in range(2)]
        + [row_block(own_ref[...], r) for r in range(4)]
        + [row_block(south_ref[members:], r) for r in range(2)]
    )


def forecast_kernel(
    prior_ref, north_ref, south_ref, own_ref, sites_ref, data_ref, precision_ref,
    first_ref, state_ref, tanh_ref, out_ref, data_out, precision_out,
):
    data_out[...] = data_ref[...]
    precision_out[...] = precision_ref[...]
    fields = field_rows(own_ref, north_ref, south_ref)
    prior = (
        [row_block(north_ref[:B], r) for r in range(2)]
        + [row_block(prior_ref[...], r) for r in range(4)]
        + [row_block(south_ref[:B], r) for r in range(2)]
    )
    first = []
    for row in range(1, 7):
        value = substep_row(
            prior[row],
            prior[row - 1],
            prior[row + 1],
            coef_rows(fields, row),
            fields[row][4:5],
        )
        first_ref[:, (row - 1) * B : row * B] = value
        first.append(value)
    onehot = onehot_of(sites_ref[...])
    picked = jnp.zeros((B, B), f32)
    sums = []
    for row in range(4):
        value = substep_row(
            first[row + 1],
            first[row],
            first[row + 2],
            coef_rows(fields, row + 2),
            fields[row + 2][4:5],
        )
        state_ref[:, row * B : (row + 1) * B] = value
        upper, rest = split(value)
        lower = (value - upper.astype(f32) - rest.astype(f32)).astype(jnp.bfloat16)
        here = onehot[row * B : (row + 1) * B]
        picked += dot(upper, here) + (dot(rest, here) + dot(lower, here))
        sums.append(column_sum(value))
    bent = jnp.tanh(picked)
    tanh_ref[...] = bent
    observed = picked + 0.5 * bent
    sums = jnp.concatenate(sums + [jnp.zeros((4, B), f32)], axis=0)
    for copy in range(4):
        out_ref[copy, :B] = observed
        out_ref[copy, B:] = sums


def partial_kernel(
    own_ref, gathered_ref, state_ref, cot_ref, data_ref, precision_ref,
    payload_ref, anom_ref, innovation_ref,
):
    own = own_ref[0]
    root = jnp.sqrt(jnp.full((1, 1), TOTAL - 1, f32))
    sums = column_sum(gathered_ref[0, :B])
    cells = gathered_ref[0, B:]
    for m in range(1, 4):
        sums += column_sum(gathered_ref[m, :B])
        cells += gathered_ref[m, B:]
    observed_mean = sums / TOTAL
    precision = precision_ref[...]
    weight = precision / root
    innovation = precision * (data_ref[...] - observed_mean)
    innovation_ref[...] = innovation
    for m in range(4):
        anom_ref[m * B : (m + 1) * B] = (gathered_ref[m, :B] - observed_mean) * weight

    def members(start, count):
        return anom_ref[pl.ds(pl.multiple_of(start, B // 2), count)]

    mine = members(own * B, B)
    mine_parts = split(mine)
    payload_ref[:B] = dot3(mine_parts, mine_parts, NT)
    after = lax.rem(own + 1, 4)
    payload_ref[B : 2 * B] = dot3(mine_parts, split(members(after * B, B)), NT)
    low = lax.rem(own, 2)
    half = members(low * B + (own // 2) * HALF, HALF)
    payload_ref[2 * B : GRAM_ROWS] = dot3(split(half), split(members(low * B + 2 * B, B)), NT)
    payload_ref[PULL_ROW : PULL_ROW + 8] = dot3(
        split(jnp.broadcast_to(innovation, (8, B))), mine_parts, NT
    )
    payload_ref[PULL_ROW + 8 :] = jnp.zeros((PAYLOAD_ROWS - PULL_ROW - 8, B), f32)
    deviations = jnp.concatenate(
        [
            (row_block(state_ref[...], r) - cells[r : r + 1] / TOTAL) / root
            for r in range(4)
        ],
        axis=1,
    )
    parts = split(deviations)
    for n in range(4):
        payload_ref[GRAM_ROWS + n * B : GRAM_ROWS + (n + 1) * B] = dot3(
            parts, split(cot_ref[n]), NT
        )


def assimilate_kernel(
    place_ref, mine_ref, other_ref, cot_ref, anom_ref, innovation_ref,
    precision_ref, tanh_ref, sites_ref, ocean_ref,
    out_ref, forward_ref, backward_ref,
    blocks, system, approach_ref, sym_ref, transform_ref, cot_upper, cot_lower,
):
    own, core = place_ref[0], place_ref[1]
    for p in range(8):
        here = pl.ds(pl.multiple_of((p * 2 + core) * PART, 8), PART)
        there = pl.ds(pl.multiple_of((p * 2 + 1 - core) * PART, 8), PART)
        spot = ((p % 2) * 4 + p // 2) * 4
        for x in range(4):
            blocks[x, here] = mine_ref[spot + x]
            blocks[x, there] = other_ref[spot + x]

    def put(m, n, value):
        system[m * B : (m + 1) * B, n * B : (n + 1) * B] = value

    diagonal = (
        lax.broadcasted_iota(jnp.int32, (B, B), 0) == lax.broadcasted_iota(jnp.int32, (B, B), 1)
    )
    for m in range(4):
        put(m, m, blocks[m, :B] + jnp.where(diagonal, 1.0, 0.0))
        n = (m + 1) % 4
        following = blocks[m, B : 2 * B]
        put(m, n, following)
        put(n, m, following.T)
    for m in range(2):
        across = jnp.concatenate(
            [blocks[m, 2 * B : GRAM_ROWS], blocks[m + 2, 2 * B : GRAM_ROWS]], axis=0
        )
        put(m, m + 2, across)
        put(m + 2, m, across.T)

    sums = [jnp.zeros((1, B), f32) for _ in range(4)]

    def cross(m, n):
        return blocks[m, GRAM_ROWS + n * B : GRAM_ROWS + (n + 1) * B]

    for m in range(4):
        for n in range(m, 4):
            turned = cross(m, n).T
            sums[m] += column_sum(turned)
            if n == m:
                sym_ref[m * B : (m + 1) * B, m * B : (m + 1) * B] = cross(m, m) + turned
            else:
                back = cross(n, m)
                back_turned = back.T
                sums[n] += column_sum(back_turned)
                sym_ref[m * B : (m + 1) * B, n * B : (n + 1) * B] = cross(m, n) + back_turned
                sym_ref[n * B : (n + 1) * B, m * B : (m + 1) * B] = back + turned
    mean_bar = jnp.concatenate(sums, axis=1)
    obs_pull = jnp.concatenate([blocks[m, PULL_ROW : PULL_ROW + 1] for m in range(4)], axis=1)

    full = system[...]
    norm = jnp.sqrt(total(full * full))
    root = jnp.sqrt(norm)
    per_norm, per_root = 1.0 / norm, 1.0 / root
    cov = jnp.sqrt(jnp.full((1, 1), TOTAL - 1, f32))
    approach = full * per_norm
    approach_ref[...] = approach
    approach_parts = split(approach)
    square = dot3(approach_parts, approach_parts)
    square_parts = split(square)
    identity = jnp.where(
        lax.broadcasted_iota(jnp.int32, (TOTAL, TOTAL), 0)
        == lax.broadcasted_iota(jnp.int32, (TOTAL, TOTAL), 1),
        1.0,
        0.0,
    )
    inner = split(P2 * identity + P3 * approach + P4 * square)
    transform = (2.25 * identity + P1 * approach + dot3(square_parts, inner)) * per_root
    transform_ref[...] = transform
    transform_parts = split(transform)
    zeros = jnp.zeros((6, TOTAL), f32)
    mids = dot3(split(jnp.concatenate([obs_pull, mean_bar, zeros], axis=0)), transform_parts)
    ends = dot3(split(mids), transform_parts)
    mid_pull, mid_bar = mids[0:1], mids[1:2]
    pull_bar = ends[1:2]
    gap = jnp.zeros((4, TOTAL), f32)
    outer = dot3(
        split(jnp.concatenate([mean_bar, mid_pull, mid_bar, obs_pull, gap], axis=0)),
        split(jnp.concatenate([mid_pull, mean_bar, obs_pull, mid_bar, gap], axis=0)),
        TN,
    )
    weight_bar = (0.5 * cov) * sym_ref[...] + 0.5 * outer
    scale_bar = -0.5 * total(weight_bar * transform_ref[...])
    polar_bar = weight_bar * per_root
    left = dot3(approach_parts, split(polar_bar))
    both = left + left.T
    approach = approach_ref[...]
    approach_bar = (
        P1 * polar_bar
        + P2 * both
        + dot3(square_parts, split(P3 * polar_bar + P4 * both))
        + dot3(split(both), split(P3 * approach + P4 * square))
    )
    scale_bar = (scale_bar - total(approach_bar * approach_ref[...])) * per_norm
    sym_bar = (2.0 * per_norm) * (approach_bar + scale_bar * system[...])
    sym_ref[...] = sym_bar

    cot_total = jnp.zeros((1, CELLS), f32)
    for n in range(4):
        value = cot_ref[n]
        cot_total += column_sum(value)
        upper, lower = split(value)
        cot_upper[n * B : (n + 1) * B] = upper
        cot_lower[n * B : (n + 1) * B] = lower
    mine = pl.ds(pl.multiple_of(own * B, B), B)
    rows = jnp.concatenate(
        [transform_ref[mine], column_sum(transform_ref[...]), jnp.zeros((7, TOTAL), f32)], axis=0
    )
    mixed = dot3(split(rows), (cot_upper[...], cot_lower[...]))
    columns = dot3(split(transform_ref[mine]), split(mids), NT)
    weight_sum = jnp.sum(ends[0:1], axis=1, keepdims=True)
    anom_total = mixed[B : B + 1] + (weight_sum / cov) * cot_total
    shared = (cot_total - anom_total) / TOTAL
    rows = jnp.concatenate([sym_ref[mine], column_sum(sym_bar), pull_bar, zeros], axis=0)
    pulled = dot3(split(rows), split(anom_ref[...]))
    innovation, precision = innovation_ref[...], precision_ref[...]
    weight = precision / cov
    pull_sum = jnp.sum(pull_bar, axis=1, keepdims=True)
    obs_total = pulled[B : B + 1] + pull_sum * innovation
    mean_part = -(obs_total * weight) - precision * pulled[B + 1 : B + 2]
    observed_bar = (pulled[:B] + columns[:, 1:2] * innovation) * weight + mean_part / TOTAL
    bent = tanh_ref[...]
    picked_bar = observed_bar * (1.0 + 0.5 * (1.0 - bent * bent))
    upper, lower = split(picked_bar)
    onehot = onehot_of(sites_ref[...])
    field = mixed[:B] + (columns[:, 0:1] / cov) * cot_total + shared
    field = field + (dot(upper, onehot, NT) + dot(lower, onehot, NT))
    for row in range(4):
        bar = ocean_ref[4:5, row * B : (row + 1) * B] * row_block(field, row)
        out_ref[:, row * B : (row + 1) * B] = bar
        side = backward_ref if row < 2 else forward_ref
        side[:, (row % 2) * B : (row % 2 + 1) * B] = bar


def coef_sums(weight, center, north, south):
    base = column_sum(weight * center)
    return [
        column_sum(weight * north) - base,
        column_sum(weight * south) - base,
        column_sum(weight * west_of(center)) - base,
        column_sum(weight * east_of(center)) - base,
    ]


def coef_kernel(
    bar_ref, north_ref, south_ref, own_ref, first_ref, prior_ref, prior_north_ref, prior_south_ref,
    first_bar_ref, coef_ref,
):
    fields = field_rows(own_ref, prior_north_ref, prior_south_ref)
    bars = (
        [row_block(north_ref[...], r) for r in range(2)]
        + [row_block(bar_ref[...], r) for r in range(4)]
        + [row_block(south_ref[...], r) for r in range(2)]
    )
    prior = (
        [row_block(prior_north_ref[:B], 1)]
        + [row_block(prior_ref[...], r) for r in range(4)]
        + [row_block(prior_south_ref[:B], 0)]
    )
    first_bars = []
    for row in range(1, 7):
        value = fields[row][4:5] * transposed(
            fields, row, bars[row], bars[row - 1], bars[row + 1]
        )
        first_bar_ref[:, (row - 1) * B : row * B] = value
        first_bars.append(value)
    for row in range(4):
        second = coef_sums(
            bars[row + 2],
            row_block(first_ref[...], row + 1),
            row_block(first_ref[...], row),
            row_block(first_ref[...], row + 2),
        )
        first = coef_sums(first_bars[row + 1], prior[row + 1], prior[row], prior[row + 2])
        for k in range(4):
            for copy in range(4):
                coef_ref[copy, k * 4 + row : k * 4 + row + 1] = second[k] + first[k]


def transposed(fields, row, center, north, south):
    return transpose_row(
        center,
        north,
        south,
        coef_rows(fields, row),
        fields[row - 1][1:2],
        fields[row + 1][0:1],
    )


def grad_kernel(first_bar_ref, own_ref, prior_north_ref, prior_south_ref, grad_ref):
    fields = field_rows(own_ref, prior_north_ref, prior_south_ref)
    bars = [row_block(first_bar_ref[...], row) for row in range(6)]
    for row in range(4):
        grad_ref[:, row, :] = transposed(
            fields, row + 2, bars[row + 1], bars[row], bars[row + 2]
        )


def call(kernel, outs, scratch=(), smem=False):
    def shaped(s):
        return jax.ShapeDtypeStruct(s, f32)

    def run(*operands):
        specs = [pl.BlockSpec(memory_space=pltpu.VMEM)] * len(operands)
        if smem:
            specs[0] = pl.BlockSpec(memory_space=pltpu.SMEM)
        single = isinstance(outs[0], int)
        return pl.pallas_call(
            kernel,
            out_shape=shaped(outs) if single else [shaped(s) for s in outs],
            in_specs=specs,
            out_specs=pl.BlockSpec(memory_space=pltpu.VMEM)
            if single
            else [pl.BlockSpec(memory_space=pltpu.VMEM)] * len(outs),
            scratch_shapes=list(scratch),
            compiler_params=pltpu.CompilerParams(vmem_limit_bytes=VMEM_BYTES),
        )(*operands)

    return run


def edge_kernel(prior_ref, coef_ref, mask_ref, prior_out, field_ref, forward_ref, backward_ref):
    members = prior_ref.shape[0]
    mask = mask_ref[...].astype(f32)
    for row in range(4):
        cells = slice(row * B, (row + 1) * B)
        value = prior_ref[:, row, :]
        rows = jnp.concatenate(
            [coef_ref[k, row : row + 1, :] for k in range(4)]
            + [mask[row : row + 1], jnp.zeros((3, B), f32)],
            axis=0,
        )
        prior_out[:, cells] = value
        field_ref[:, cells] = rows
        side = backward_ref if row < 2 else forward_ref
        cells = slice((row % 2) * B, (row % 2 + 1) * B)
        side[:members, cells] = value
        side[members:, cells] = rows


def spread_kernel(cot_ref, out_ref):
    for row in range(4):
        value = cot_ref[:, row, :]
        for copy in range(4):
            out_ref[copy, :, row * B : (row + 1) * B] = value


def exchange(forward_edge, backward_edge):
    count = lax.axis_size(STRIPS)
    forward = [(i, i + 1) for i in range(count - 1)]
    backward = [(target, source) for source, target in forward]
    return lax.ppermute(forward_edge, STRIPS, forward), lax.ppermute(backward_edge, STRIPS, backward)


def trade(parts, axes):
    return lax.all_to_all(parts, axes, 0, 0, tiled=True)


def sum_kernel(parts_ref, out_ref):
    value = parts_ref[0]
    for i in range(1, parts_ref.shape[0]):
        value += parts_ref[i]
    for copy in range(out_ref.shape[0]):
        out_ref[copy] = value


def summed_copies(parts, count):
    return call(sum_kernel, (count,) + parts.shape[1:])(parts)


def strip_sum(payload):
    pieces = trade(payload.reshape(16, PART, B), ("y", "z_low", "core"))
    pairs = trade(summed_copies(pieces, lax.axis_size("z")), "z")
    mine = trade(summed_copies(pairs, 32), ("z_low", "y", "x"))
    return mine, lax.ppermute(mine, "core", [(0, 1), (1, 0)])


def coef_total_kernel(parts_ref, out_ref):
    value = parts_ref[0] + parts_ref[1] + parts_ref[2] + parts_ref[3]
    out_ref[...] = value / jnp.sqrt(jnp.full((1, 1), TOTAL, f32))


def local(
    prior_ensemble,
    stencil_factors,
    sea_mask,
    measured_site_positions,
    measured_data,
    measurement_precision,
    cotangent,
):
    members = prior_ensemble.shape[0]
    own = lax.axis_index("x")
    place = jnp.stack([own, lax.axis_index("core")]).astype(jnp.int32)
    prior, own_field, forward_edge, backward_edge = call(
        edge_kernel,
        [(members, CELLS), (8, CELLS), (members + 8, 2 * B), (members + 8, 2 * B)],
    )(prior_ensemble, stencil_factors, sea_mask)
    north, south = exchange(forward_edge, backward_edge)
    cots = trade(call(spread_kernel, (4, members, CELLS))(cotangent), "x")

    sites = measured_site_positions
    precision = measurement_precision.reshape(1, B)
    data = measured_data.reshape(1, B)

    first, state, bent, outgoing, data, precision = call(
        forecast_kernel, [(members, 6 * B), (members, CELLS), (B, B), (4, OBS_ROWS, B), (1, B), (1, B)]
    )(prior, north, south, own_field, sites, data, precision)
    outgoing, cots = lax.optimization_barrier((outgoing, cots))
    gathered = trade(outgoing, "x")
    payload, anom, innovation = call(
        partial_kernel, [(PAYLOAD_ROWS, B), (TOTAL, B), (1, B)], smem=True
    )(place, gathered, state, cots, data, precision)
    mine, other = strip_sum(payload)
    square = (TOTAL, TOTAL)
    bar, bar_forward, bar_backward = call(
        assimilate_kernel,
        [(members, CELLS), (members, 2 * B), (members, 2 * B)],
        scratch=[pltpu.VMEM((4, PAYLOAD_ROWS, B), f32)]
        + [pltpu.VMEM(square, f32)] * 4
        + [pltpu.VMEM(square, jnp.bfloat16)] * 2,
        smem=True,
    )(place, mine, other, cots, anom, innovation, precision, bent, sites, own_field)
    bar_north, bar_south = exchange(bar_forward, bar_backward)
    first_bar, coef = call(coef_kernel, [(members, 6 * B), (4, 16, B)])(
        bar, bar_north, bar_south, own_field, first, prior, north, south
    )
    grad = call(grad_kernel, (members, 4, B))(first_bar, own_field, north, south)
    coef = call(coef_total_kernel, (16, B))(trade(coef, "x"))
    return (
        grad,
        coef.reshape(4, 4, B),
    )


def solution(mesh):
    strips, parts = mesh.devices.shape
    grid = Mesh(mesh.devices.reshape(strips // 16, 2, 4, 2, parts), STRIPS + ("x",))
    placed = (
        P("x", STRIPS, None),
        P(None, STRIPS, None),
        P(STRIPS, None),
        P(STRIPS, None),
        P(STRIPS),
        P(STRIPS),
        P("x", STRIPS, None),
    )
    return jax.shard_map(
        local,
        mesh=grid,
        in_specs=placed,
        out_specs=(P("x", STRIPS, None), P(None, STRIPS, None)),
        check_vma=False,
    )
```

```python
import jax
import jax.numpy as jnp
from jax import lax
from jax.experimental import pallas as pl
from jax.experimental.pallas import tpu as pltpu
from jax.sharding import Mesh
from jax.sharding import PartitionSpec as P

TOTAL = 512
B = 128
CELLS = 512
STRIPS = ("z", "z_low", "y", "core")
GRAM_ROWS = 320
PULL_ROW = GRAM_ROWS + 512
PAYLOAD_ROWS = 896
PART = PAYLOAD_ROWS // 16
HALF = B // 2
OBS_ROWS = B + 8
VMEM_BYTES = 24 * 1024 * 1024
P1, P2, P3, P4 = -2.4375, 1.6875, -0.5625, 0.0625
NN = (((1,), (0,)), ((), ()))
NT = (((1,), (1,)), ((), ()))
TN = (((0,), (0,)), ((), ()))
f32 = jnp.float32


def split(value):
    upper = value.astype(jnp.bfloat16)
    return upper, (value - upper.astype(f32)).astype(jnp.bfloat16)


def dot(left, right, dims=NN):
    return lax.dot_general(left, right, dims, preferred_element_type=f32)


def dot3(left, right, dims=NN):
    lu, ll = left
    ru, rl = right
    return dot(lu, ru, dims) + (dot(lu, rl, dims) + dot(ll, ru, dims))


def total(value):
    return jnp.sum(jnp.sum(value, axis=0, keepdims=True), axis=1, keepdims=True)


def column_sum(value):
    return jnp.sum(value, axis=0, keepdims=True)


def row_block(value, row):
    return value[:, row * B : (row + 1) * B]


def west_of(center):
    column = lax.broadcasted_iota(jnp.int32, center.shape, 1)
    return jnp.where(column == 0, 0.0, pltpu.roll(center, 1, 1))


def east_of(center):
    column = lax.broadcasted_iota(jnp.int32, center.shape, 1)
    return jnp.where(column == B - 1, 0.0, pltpu.roll(center, B - 1, 1))


def substep_row(center, north, south, coef, ocean):
    kept = 1.0 - coef[0] - coef[1] - coef[2] - coef[3]
    return ocean * (
        kept * center
        + coef[0] * north
        + coef[1] * south
        + coef[2] * west_of(center)
        + coef[3] * east_of(center)
    )


def transpose_row(center, north, south, coef, coef_north, coef_south):
    kept = 1.0 - coef[0] - coef[1] - coef[2] - coef[3]
    return (
        kept * center
        + coef_south * south
        + coef_north * north
        + east_of(coef[2] * center)
        + west_of(coef[3] * center)
    )


def onehot_of(sites):
    cell = lax.broadcasted_iota(jnp.int32, (CELLS, B), 0)
    return jnp.where(cell == sites, 1.0, 0.0).astype(jnp.bfloat16)


def coef_rows(fields, row):
    return [fields[row][k : k + 1] for k in range(4)]


def field_rows(own_ref, north_ref, south_ref):
    members = north_ref.shape[0] - 8
    return (
        [row_block(north_ref[members:], r) for r in range(2)]
        + [row_block(own_ref[...], r) for r in range(4)]
        + [row_block(south_ref[members:], r) for r in range(2)]
    )


def forecast_kernel(
    prior_ref, north_ref, south_ref, own_ref, sites_ref, data_ref, precision_ref,
    first_ref, state_ref, tanh_ref, out_ref, data_out, precision_out,
):
    data_out[...] = data_ref[...]
    precision_out[...] = precision_ref[...]
    fields = field_rows(own_ref, north_ref, south_ref)
    prior = (
        [row_block(north_ref[:B], r) for r in range(2)]
        + [row_block(prior_ref[...], r) for r in range(4)]
        + [row_block(south_ref[:B], r) for r in range(2)]
    )
    first = []
    for row in range(1, 7):
        value = substep_row(
            prior[row],
            prior[row - 1],
            prior[row + 1],
            coef_rows(fields, row),
            fields[row][4:5],
        )
        first_ref[:, (row - 1) * B : row * B] = value
        first.append(value)
    onehot = onehot_of(sites_ref[...])
    picked = jnp.zeros((B, B), f32)
    sums = []
    for row in range(4):
        value = substep_row(
            first[row + 1],
            first[row],
            first[row + 2],
            coef_rows(fields, row + 2),
            fields[row + 2][4:5],
        )
        state_ref[:, row * B : (row + 1) * B] = value
        upper, rest = split(value)
        lower = (value - upper.astype(f32) - rest.astype(f32)).astype(jnp.bfloat16)
        here = onehot[row * B : (row + 1) * B]
        picked += dot(upper, here) + (dot(rest, here) + dot(lower, here))
        sums.append(column_sum(value))
    bent = jnp.tanh(picked)
    tanh_ref[...] = bent
    observed = picked + 0.5 * bent
    sums = jnp.concatenate(sums + [jnp.zeros((4, B), f32)], axis=0)
    for copy in range(4):
        out_ref[copy, :B] = observed
        out_ref[copy, B:] = sums


def partial_kernel(
    own_ref, gathered_ref, state_ref, cot_ref, data_ref, precision_ref,
    payload_ref, anom_ref, innovation_ref,
):
    own = own_ref[0]
    root = jnp.sqrt(jnp.full((1, 1), TOTAL - 1, f32))
    sums = column_sum(gathered_ref[0, :B])
    cells = gathered_ref[0, B:]
    for m in range(1, 4):
        sums += column_sum(gathered_ref[m, :B])
        cells += gathered_ref[m, B:]
    observed_mean = sums / TOTAL
    precision = precision_ref[...]
    weight = precision / root
    innovation = precision * (data_ref[...] - observed_mean)
    innovation_ref[...] = innovation
    for m in range(4):
        anom_ref[m * B : (m + 1) * B] = (gathered_ref[m, :B] - observed_mean) * weight

    def members(start, count):
        return anom_ref[pl.ds(pl.multiple_of(start, B // 2), count)]

    mine = members(own * B, B)
    mine_parts = split(mine)
    payload_ref[:B] = dot3(mine_parts, mine_parts, NT)
    after = lax.rem(own + 1, 4)
    payload_ref[B : 2 * B] = dot3(mine_parts, split(members(after * B, B)), NT)
    low = lax.rem(own, 2)
    half = members(low * B + (own // 2) * HALF, HALF)
    payload_ref[2 * B : GRAM_ROWS] = dot3(split(half), split(members(low * B + 2 * B, B)), NT)
    payload_ref[PULL_ROW : PULL_ROW + 8] = dot3(
        split(jnp.broadcast_to(innovation, (8, B))), mine_parts, NT
    )
    payload_ref[PULL_ROW + 8 :] = jnp.zeros((PAYLOAD_ROWS - PULL_ROW - 8, B), f32)
    deviations = jnp.concatenate(
        [
            (row_block(state_ref[...], r) - cells[r : r + 1] / TOTAL) / root
            for r in range(4)
        ],
        axis=1,
    )
    parts = split(deviations)
    for n in range(4):
        payload_ref[GRAM_ROWS + n * B : GRAM_ROWS + (n + 1) * B] = dot3(
            parts, split(cot_ref[n]), NT
        )


def assimilate_kernel(
    place_ref, mine_ref, other_ref, cot_ref, anom_ref, innovation_ref,
    precision_ref, tanh_ref, sites_ref, ocean_ref,
    out_ref, forward_ref, backward_ref,
    blocks, system, approach_ref, sym_ref, transform_ref, cot_upper, cot_lower,
):
    own, core = place_ref[0], place_ref[1]
    for p in range(8):
        here = pl.ds(pl.multiple_of((p * 2 + core) * PART, 8), PART)
        there = pl.ds(pl.multiple_of((p * 2 + 1 - core) * PART, 8), PART)
        spot = ((p % 2) * 4 + p // 2) * 4
        for x in range(4):
            blocks[x, here] = mine_ref[spot + x]
            blocks[x, there] = other_ref[spot + x]

    def put(m, n, value):
        system[m * B : (m + 1) * B, n * B : (n + 1) * B] = value

    diagonal = (
        lax.broadcasted_iota(jnp.int32, (B, B), 0) == lax.broadcasted_iota(jnp.int32, (B, B), 1)
    )
    for m in range(4):
        put(m, m, blocks[m, :B] + jnp.where(diagonal, 1.0, 0.0))
        n = (m + 1) % 4
        following = blocks[m, B : 2 * B]
        put(m, n, following)
        put(n, m, following.T)
    for m in range(2):
        across = jnp.concatenate(
            [blocks[m, 2 * B : GRAM_ROWS], blocks[m + 2, 2 * B : GRAM_ROWS]], axis=0
        )
        put(m, m + 2, across)
        put(m + 2, m, across.T)

    sums = [jnp.zeros((1, B), f32) for _ in range(4)]

    def cross(m, n):
        return blocks[m, GRAM_ROWS + n * B : GRAM_ROWS + (n + 1) * B]

    for m in range(4):
        for n in range(m, 4):
            turned = cross(m, n).T
            sums[m] += column_sum(turned)
            if n == m:
                sym_ref[m * B : (m + 1) * B, m * B : (m + 1) * B] = cross(m, m) + turned
            else:
                back = cross(n, m)
                back_turned = back.T
                sums[n] += column_sum(back_turned)
                sym_ref[m * B : (m + 1) * B, n * B : (n + 1) * B] = cross(m, n) + back_turned
                sym_ref[n * B : (n + 1) * B, m * B : (m + 1) * B] = back + turned
    mean_bar = jnp.concatenate(sums, axis=1)
    obs_pull = jnp.concatenate([blocks[m, PULL_ROW : PULL_ROW + 1] for m in range(4)], axis=1)

    full = system[...]
    norm = jnp.sqrt(total(full * full))
    root = jnp.sqrt(norm)
    per_norm, per_root = 1.0 / norm, 1.0 / root
    cov = jnp.sqrt(jnp.full((1, 1), TOTAL - 1, f32))
    approach = full * per_norm
    approach_ref[...] = approach
    approach_parts = split(approach)
    square = dot3(approach_parts, approach_parts)
    square_parts = split(square)
    identity = jnp.where(
        lax.broadcasted_iota(jnp.int32, (TOTAL, TOTAL), 0)
        == lax.broadcasted_iota(jnp.int32, (TOTAL, TOTAL), 1),
        1.0,
        0.0,
    )
    inner = split(P2 * identity + P3 * approach + P4 * square)
    transform = (2.25 * identity + P1 * approach + dot3(square_parts, inner)) * per_root
    transform_ref[...] = transform
    transform_parts = split(transform)
    zeros = jnp.zeros((6, TOTAL), f32)
    mids = dot3(split(jnp.concatenate([obs_pull, mean_bar, zeros], axis=0)), transform_parts)
    ends = dot3(split(mids), transform_parts)
    mid_pull, mid_bar = mids[0:1], mids[1:2]
    pull_bar = ends[1:2]
    gap = jnp.zeros((4, TOTAL), f32)
    outer = dot3(
        split(jnp.concatenate([mean_bar, mid_pull, mid_bar, obs_pull, gap], axis=0)),
        split(jnp.concatenate([mid_pull, mean_bar, obs_pull, mid_bar, gap], axis=0)),
        TN,
    )
    weight_bar = (0.5 * cov) * sym_ref[...] + 0.5 * outer
    scale_bar = -0.5 * total(weight_bar * transform_ref[...])
    polar_bar = weight_bar * per_root
    left = dot3(approach_parts, split(polar_bar))
    both = left + left.T
    approach = approach_ref[...]
    approach_bar = (
        P1 * polar_bar
        + P2 * both
        + dot3(square_parts, split(P3 * polar_bar + P4 * both))
        + dot3(split(both), split(P3 * approach + P4 * square))
    )
    scale_bar = (scale_bar - total(approach_bar * approach_ref[...])) * per_norm
    sym_bar = (2.0 * per_norm) * (approach_bar + scale_bar * system[...])
    sym_ref[...] = sym_bar

    cot_total = jnp.zeros((1, CELLS), f32)
    for n in range(4):
        value = cot_ref[n]
        cot_total += column_sum(value)
        upper, lower = split(value)
        cot_upper[n * B : (n + 1) * B] = upper
        cot_lower[n * B : (n + 1) * B] = lower
    mine = pl.ds(pl.multiple_of(own * B, B), B)
    rows = jnp.concatenate(
        [transform_ref[mine], column_sum(transform_ref[...]), jnp.zeros((7, TOTAL), f32)], axis=0
    )
    mixed = dot3(split(rows), (cot_upper[...], cot_lower[...]))
    columns = dot3(split(transform_ref[mine]), split(mids), NT)
    weight_sum = jnp.sum(ends[0:1], axis=1, keepdims=True)
    anom_total = mixed[B : B + 1] + (weight_sum / cov) * cot_total
    shared = (cot_total - anom_total) / TOTAL
    rows = jnp.concatenate([sym_ref[mine], column_sum(sym_bar), pull_bar, zeros], axis=0)
    pulled = dot3(split(rows), split(anom_ref[...]))
    innovation, precision = innovation_ref[...], precision_ref[...]
    weight = precision / cov
    pull_sum = jnp.sum(pull_bar, axis=1, keepdims=True)
    obs_total = pulled[B : B + 1] + pull_sum * innovation
    mean_part = -(obs_total * weight) - precision * pulled[B + 1 : B + 2]
    observed_bar = (pulled[:B] + columns[:, 1:2] * innovation) * weight + mean_part / TOTAL
    bent = tanh_ref[...]
    picked_bar = observed_bar * (1.0 + 0.5 * (1.0 - bent * bent))
    upper, lower = split(picked_bar)
    onehot = onehot_of(sites_ref[...])
    field = mixed[:B] + (columns[:, 0:1] / cov) * cot_total + shared
    field = field + (dot(upper, onehot, NT) + dot(lower, onehot, NT))
    for row in range(4):
        bar = ocean_ref[4:5, row * B : (row + 1) * B] * row_block(field, row)
        out_ref[:, row * B : (row + 1) * B] = bar
        side = backward_ref if row < 2 else forward_ref
        side[:, (row % 2) * B : (row % 2 + 1) * B] = bar


def coef_sums(weight, center, north, south):
    base = column_sum(weight * center)
    return [
        column_sum(weight * north) - base,
        column_sum(weight * south) - base,
        column_sum(weight * west_of(center)) - base,
        column_sum(weight * east_of(center)) - base,
    ]


def coef_kernel(
    bar_ref, north_ref, south_ref, own_ref, first_ref, prior_ref, prior_north_ref, prior_south_ref,
    first_bar_ref, coef_ref,
):
    fields = field_rows(own_ref, prior_north_ref, prior_south_ref)
    bars = (
        [row_block(north_ref[...], r) for r in range(2)]
        + [row_block(bar_ref[...], r) for r in range(4)]
        + [row_block(south_ref[...], r) for r in range(2)]
    )
    prior = (
        [row_block(prior_north_ref[:B], 1)]
        + [row_block(prior_ref[...], r) for r in range(4)]
        + [row_block(prior_south_ref[:B], 0)]
    )
    first_bars = []
    for row in range(1, 7):
        value = fields[row][4:5] * transposed(
            fields, row, bars[row], bars[row - 1], bars[row + 1]
        )
        first_bar_ref[:, (row - 1) * B : row * B] = value
        first_bars.append(value)
    for row in range(4):
        second = coef_sums(
            bars[row + 2],
            row_block(first_ref[...], row + 1),
            row_block(first_ref[...], row),
            row_block(first_ref[...], row + 2),
        )
        first = coef_sums(first_bars[row + 1], prior[row + 1], prior[row], prior[row + 2])
        for k in range(4):
            for copy in range(4):
                coef_ref[copy, k * 4 + row : k * 4 + row + 1] = second[k] + first[k]


def transposed(fields, row, center, north, south):
    return transpose_row(
        center,
        north,
        south,
        coef_rows(fields, row),
        fields[row - 1][1:2],
        fields[row + 1][0:1],
    )


def grad_kernel(first_bar_ref, own_ref, prior_north_ref, prior_south_ref, grad_ref):
    fields = field_rows(own_ref, prior_north_ref, prior_south_ref)
    bars = [row_block(first_bar_ref[...], row) for row in range(6)]
    for row in range(4):
        grad_ref[:, row, :] = transposed(
            fields, row + 2, bars[row + 1], bars[row], bars[row + 2]
        )


def call(kernel, outs, scratch=(), smem=False):
    def shaped(s):
        return jax.ShapeDtypeStruct(s, f32)

    def run(*operands):
        specs = [pl.BlockSpec(memory_space=pltpu.VMEM)] * len(operands)
        if smem:
            specs[0] = pl.BlockSpec(memory_space=pltpu.SMEM)
        single = isinstance(outs[0], int)
        return pl.pallas_call(
            kernel,
            out_shape=shaped(outs) if single else [shaped(s) for s in outs],
            in_specs=specs,
            out_specs=pl.BlockSpec(memory_space=pltpu.VMEM)
            if single
            else [pl.BlockSpec(memory_space=pltpu.VMEM)] * len(outs),
            scratch_shapes=list(scratch),
            compiler_params=pltpu.CompilerParams(vmem_limit_bytes=VMEM_BYTES),
        )(*operands)

    return run


def edge_kernel(prior_ref, coef_ref, mask_ref, prior_out, field_ref, forward_ref, backward_ref):
    members = prior_ref.shape[0]
    mask = mask_ref[...].astype(f32)
    for row in range(4):
        cells = slice(row * B, (row + 1) * B)
        value = prior_ref[:, row, :]
        rows = jnp.concatenate(
            [coef_ref[k, row : row + 1, :] for k in range(4)]
            + [mask[row : row + 1], jnp.zeros((3, B), f32)],
            axis=0,
        )
        prior_out[:, cells] = value
        field_ref[:, cells] = rows
        side = backward_ref if row < 2 else forward_ref
        cells = slice((row % 2) * B, (row % 2 + 1) * B)
        side[:members, cells] = value
        side[members:, cells] = rows


def spread_kernel(cot_ref, out_ref):
    for row in range(4):
        value = cot_ref[:, row, :]
        for copy in range(4):
            out_ref[copy, :, row * B : (row + 1) * B] = value


def exchange(forward_edge, backward_edge, backward_first=False):
    count = lax.axis_size(STRIPS)
    forward = [(i, i + 1) for i in range(count - 1)]
    backward = [(target, source) for source, target in forward]
    if backward_first:
        south = lax.ppermute(backward_edge, STRIPS, backward)
        return lax.ppermute(forward_edge, STRIPS, forward), south
    north = lax.ppermute(forward_edge, STRIPS, forward)
    return north, lax.ppermute(backward_edge, STRIPS, backward)


def trade(parts, axes):
    return lax.all_to_all(parts, axes, 0, 0, tiled=True)


def sum_kernel(parts_ref, out_ref):
    value = parts_ref[0]
    for i in range(1, parts_ref.shape[0]):
        value += parts_ref[i]
    for copy in range(out_ref.shape[0]):
        out_ref[copy] = value


def summed_copies(parts, count):
    return call(sum_kernel, (count,) + parts.shape[1:])(parts)


def strip_sum(payload):
    pieces = trade(payload.reshape(16, PART, B), ("y", "z_low", "core"))
    pairs = trade(summed_copies(pieces, lax.axis_size("z")), "z")
    mine = trade(summed_copies(pairs, 32), ("z_low", "y", "x"))
    return mine, lax.ppermute(mine, "core", [(0, 1), (1, 0)])


def coef_total_kernel(parts_ref, out_ref):
    value = parts_ref[0] + parts_ref[1] + parts_ref[2] + parts_ref[3]
    out_ref[...] = value / jnp.sqrt(jnp.full((1, 1), TOTAL, f32))


def local(
    prior_ensemble,
    stencil_factors,
    sea_mask,
    measured_site_positions,
    measured_data,
    measurement_precision,
    cotangent,
):
    members = prior_ensemble.shape[0]
    own = lax.axis_index("x")
    place = jnp.stack([own, lax.axis_index("core")]).astype(jnp.int32)
    prior, own_field, forward_edge, backward_edge = call(
        edge_kernel,
        [(members, CELLS), (8, CELLS), (members + 8, 2 * B), (members + 8, 2 * B)],
    )(prior_ensemble, stencil_factors, sea_mask)
    north, south = exchange(forward_edge, backward_edge)
    cots = trade(call(spread_kernel, (4, members, CELLS))(cotangent), "x")

    sites = measured_site_positions
    precision = measurement_precision.reshape(1, B)
    data = measured_data.reshape(1, B)

    first, state, bent, outgoing, data, precision = call(
        forecast_kernel, [(members, 6 * B), (members, CELLS), (B, B), (4, OBS_ROWS, B), (1, B), (1, B)]
    )(prior, north, south, own_field, sites, data, precision)
    outgoing, cots = lax.optimization_barrier((outgoing, cots))
    gathered = trade(outgoing, "x")
    payload, anom, innovation = call(
        partial_kernel, [(PAYLOAD_ROWS, B), (TOTAL, B), (1, B)], smem=True
    )(place, gathered, state, cots, data, precision)
    mine, other = strip_sum(payload)
    square = (TOTAL, TOTAL)
    bar, bar_forward, bar_backward = call(
        assimilate_kernel,
        [(members, CELLS), (members, 2 * B), (members, 2 * B)],
        scratch=[pltpu.VMEM((4, PAYLOAD_ROWS, B), f32)]
        + [pltpu.VMEM(square, f32)] * 4
        + [pltpu.VMEM(square, jnp.bfloat16)] * 2,
        smem=True,
    )(place, mine, other, cots, anom, innovation, precision, bent, sites, own_field)
    bar_north, bar_south = exchange(bar_forward, bar_backward, backward_first=True)
    first_bar, coef = call(coef_kernel, [(members, 6 * B), (4, 16, B)])(
        bar, bar_north, bar_south, own_field, first, prior, north, south
    )
    grad = call(grad_kernel, (members, 4, B))(first_bar, own_field, north, south)
    coef = call(coef_total_kernel, (16, B))(trade(coef, "x"))
    return (
        grad,
        coef.reshape(4, 4, B),
    )


def solution(mesh):
    strips, parts = mesh.devices.shape
    grid = Mesh(mesh.devices.reshape(strips // 16, 2, 4, 2, parts), STRIPS + ("x",))
    placed = (
        P("x", STRIPS, None),
        P(None, STRIPS, None),
        P(STRIPS, None),
        P(STRIPS, None),
        P(STRIPS),
        P(STRIPS),
        P("x", STRIPS, None),
    )
    return jax.shard_map(
        local,
        mesh=grid,
        in_specs=placed,
        out_specs=(P("x", STRIPS, None), P(None, STRIPS, None)),
        check_vma=False,
    )
```

```python
import jax
import jax.numpy as jnp
from jax import lax
from jax.experimental import pallas as pl
from jax.experimental.pallas import tpu as pltpu
from jax.sharding import Mesh
from jax.sharding import PartitionSpec as P

TOTAL = 512
B = 128
CELLS = 512
STRIPS = ("z", "z_low", "y", "core")
GRAM_ROWS = 320
PULL_ROW = GRAM_ROWS + 512
PAYLOAD_ROWS = 896
PART = PAYLOAD_ROWS // 16
HALF = B // 2
OBS_ROWS = B + 8
VMEM_BYTES = 24 * 1024 * 1024
P1, P2, P3, P4 = -2.4375, 1.6875, -0.5625, 0.0625
NN = (((1,), (0,)), ((), ()))
NT = (((1,), (1,)), ((), ()))
TN = (((0,), (0,)), ((), ()))
f32 = jnp.float32


def split(value):
    upper = value.astype(jnp.bfloat16)
    return upper, (value - upper.astype(f32)).astype(jnp.bfloat16)


def dot(left, right, dims=NN):
    return lax.dot_general(left, right, dims, preferred_element_type=f32)


def dot3(left, right, dims=NN):
    lu, ll = left
    ru, rl = right
    return dot(lu, ru, dims) + (dot(lu, rl, dims) + dot(ll, ru, dims))


def total(value):
    return jnp.sum(jnp.sum(value, axis=0, keepdims=True), axis=1, keepdims=True)


def column_sum(value):
    return jnp.sum(value, axis=0, keepdims=True)


def row_block(value, row):
    return value[:, row * B : (row + 1) * B]


def west_of(center):
    column = lax.broadcasted_iota(jnp.int32, center.shape, 1)
    return jnp.where(column == 0, 0.0, pltpu.roll(center, 1, 1))


def east_of(center):
    column = lax.broadcasted_iota(jnp.int32, center.shape, 1)
    return jnp.where(column == B - 1, 0.0, pltpu.roll(center, B - 1, 1))


def substep_row(center, north, south, coef, ocean):
    kept = 1.0 - coef[0] - coef[1] - coef[2] - coef[3]
    return ocean * (
        kept * center
        + coef[0] * north
        + coef[1] * south
        + coef[2] * west_of(center)
        + coef[3] * east_of(center)
    )


def transpose_row(center, north, south, coef, coef_north, coef_south):
    kept = 1.0 - coef[0] - coef[1] - coef[2] - coef[3]
    return (
        kept * center
        + coef_south * south
        + coef_north * north
        + east_of(coef[2] * center)
        + west_of(coef[3] * center)
    )


def onehot_of(sites):
    cell = lax.broadcasted_iota(jnp.int32, (CELLS, B), 0)
    return jnp.where(cell == sites, 1.0, 0.0).astype(jnp.bfloat16)


def coef_rows(fields, row):
    return [fields[row][k : k + 1] for k in range(4)]


def chosen(place_ref, even, odd):
    core = jnp.zeros(even.shape, jnp.int32) + place_ref[1]
    return jnp.where(core == 0, even, odd)


def sides(place_ref, on_ref, off_ref):
    on, off = on_ref[...], off_ref[...]
    return chosen(place_ref, off, on), chosen(place_ref, on, off)


def field_rows(own_ref, north_ref, south_ref):
    members = north_ref.shape[0] - 8
    return (
        [row_block(north_ref[members:], r) for r in range(2)]
        + [row_block(own_ref[...], r) for r in range(4)]
        + [row_block(south_ref[members:], r) for r in range(2)]
    )


def forecast_kernel(
    place_ref, prior_ref, on_ref, off_ref, own_ref, sites_ref, data_ref, precision_ref,
    first_ref, state_ref, tanh_ref, out_ref, data_out, precision_out,
):
    north_ref, south_ref = sides(place_ref, on_ref, off_ref)
    data_out[...] = data_ref[...]
    precision_out[...] = precision_ref[...]
    fields = field_rows(own_ref, north_ref, south_ref)
    prior = (
        [row_block(north_ref[:B], r) for r in range(2)]
        + [row_block(prior_ref[...], r) for r in range(4)]
        + [row_block(south_ref[:B], r) for r in range(2)]
    )
    first = []
    for row in range(1, 7):
        value = substep_row(
            prior[row],
            prior[row - 1],
            prior[row + 1],
            coef_rows(fields, row),
            fields[row][4:5],
        )
        first_ref[:, (row - 1) * B : row * B] = value
        first.append(value)
    onehot = onehot_of(sites_ref[...])
    picked = jnp.zeros((B, B), f32)
    sums = []
    for row in range(4):
        value = substep_row(
            first[row + 1],
            first[row],
            first[row + 2],
            coef_rows(fields, row + 2),
            fields[row + 2][4:5],
        )
        state_ref[:, row * B : (row + 1) * B] = value
        upper, rest = split(value)
        lower = (value - upper.astype(f32) - rest.astype(f32)).astype(jnp.bfloat16)
        here = onehot[row * B : (row + 1) * B]
        picked += dot(upper, here) + (dot(rest, here) + dot(lower, here))
        sums.append(column_sum(value))
    bent = jnp.tanh(picked)
    tanh_ref[...] = bent
    observed = picked + 0.5 * bent
    sums = jnp.concatenate(sums + [jnp.zeros((4, B), f32)], axis=0)
    for copy in range(4):
        out_ref[copy, :B] = observed
        out_ref[copy, B:] = sums


def partial_kernel(
    own_ref, gathered_ref, state_ref, cot_ref, data_ref, precision_ref,
    payload_ref, anom_ref, innovation_ref,
):
    own = own_ref[0]
    root = jnp.sqrt(jnp.full((1, 1), TOTAL - 1, f32))
    sums = column_sum(gathered_ref[0, :B])
    cells = gathered_ref[0, B:]
    for m in range(1, 4):
        sums += column_sum(gathered_ref[m, :B])
        cells += gathered_ref[m, B:]
    observed_mean = sums / TOTAL
    precision = precision_ref[...]
    weight = precision / root
    innovation = precision * (data_ref[...] - observed_mean)
    innovation_ref[...] = innovation
    for m in range(4):
        anom_ref[m * B : (m + 1) * B] = (gathered_ref[m, :B] - observed_mean) * weight

    def members(start, count):
        return anom_ref[pl.ds(pl.multiple_of(start, B // 2), count)]

    mine = members(own * B, B)
    mine_parts = split(mine)
    payload_ref[:B] = dot3(mine_parts, mine_parts, NT)
    after = lax.rem(own + 1, 4)
    payload_ref[B : 2 * B] = dot3(mine_parts, split(members(after * B, B)), NT)
    low = lax.rem(own, 2)
    half = members(low * B + (own // 2) * HALF, HALF)
    payload_ref[2 * B : GRAM_ROWS] = dot3(split(half), split(members(low * B + 2 * B, B)), NT)
    payload_ref[PULL_ROW : PULL_ROW + 8] = dot3(
        split(jnp.broadcast_to(innovation, (8, B))), mine_parts, NT
    )
    payload_ref[PULL_ROW + 8 :] = jnp.zeros((PAYLOAD_ROWS - PULL_ROW - 8, B), f32)
    deviations = jnp.concatenate(
        [
            (row_block(state_ref[...], r) - cells[r : r + 1] / TOTAL) / root
            for r in range(4)
        ],
        axis=1,
    )
    parts = split(deviations)
    for n in range(4):
        payload_ref[GRAM_ROWS + n * B : GRAM_ROWS + (n + 1) * B] = dot3(
            parts, split(cot_ref[n]), NT
        )


def assimilate_kernel(
    place_ref, mine_ref, other_ref, cot_ref, anom_ref, innovation_ref,
    precision_ref, tanh_ref, sites_ref, ocean_ref,
    out_ref, on_edge_ref, off_edge_ref,
    blocks, system, approach_ref, sym_ref, transform_ref, cot_upper, cot_lower,
):
    own, core = place_ref[0], place_ref[1]
    for p in range(8):
        here = pl.ds(pl.multiple_of((p * 2 + core) * PART, 8), PART)
        there = pl.ds(pl.multiple_of((p * 2 + 1 - core) * PART, 8), PART)
        spot = ((p % 2) * 4 + p // 2) * 4
        for x in range(4):
            blocks[x, here] = mine_ref[spot + x]
            blocks[x, there] = other_ref[spot + x]

    def put(m, n, value):
        system[m * B : (m + 1) * B, n * B : (n + 1) * B] = value

    diagonal = (
        lax.broadcasted_iota(jnp.int32, (B, B), 0) == lax.broadcasted_iota(jnp.int32, (B, B), 1)
    )
    for m in range(4):
        put(m, m, blocks[m, :B] + jnp.where(diagonal, 1.0, 0.0))
        n = (m + 1) % 4
        following = blocks[m, B : 2 * B]
        put(m, n, following)
        put(n, m, following.T)
    for m in range(2):
        across = jnp.concatenate(
            [blocks[m, 2 * B : GRAM_ROWS], blocks[m + 2, 2 * B : GRAM_ROWS]], axis=0
        )
        put(m, m + 2, across)
        put(m + 2, m, across.T)

    sums = [jnp.zeros((1, B), f32) for _ in range(4)]

    def cross(m, n):
        return blocks[m, GRAM_ROWS + n * B : GRAM_ROWS + (n + 1) * B]

    for m in range(4):
        for n in range(m, 4):
            turned = cross(m, n).T
            sums[m] += column_sum(turned)
            if n == m:
                sym_ref[m * B : (m + 1) * B, m * B : (m + 1) * B] = cross(m, m) + turned
            else:
                back = cross(n, m)
                back_turned = back.T
                sums[n] += column_sum(back_turned)
                sym_ref[m * B : (m + 1) * B, n * B : (n + 1) * B] = cross(m, n) + back_turned
                sym_ref[n * B : (n + 1) * B, m * B : (m + 1) * B] = back + turned
    mean_bar = jnp.concatenate(sums, axis=1)
    obs_pull = jnp.concatenate([blocks[m, PULL_ROW : PULL_ROW + 1] for m in range(4)], axis=1)

    full = system[...]
    norm = jnp.sqrt(total(full * full))
    root = jnp.sqrt(norm)
    per_norm, per_root = 1.0 / norm, 1.0 / root
    cov = jnp.sqrt(jnp.full((1, 1), TOTAL - 1, f32))
    approach = full * per_norm
    approach_ref[...] = approach
    approach_parts = split(approach)
    square = dot3(approach_parts, approach_parts)
    square_parts = split(square)
    identity = jnp.where(
        lax.broadcasted_iota(jnp.int32, (TOTAL, TOTAL), 0)
        == lax.broadcasted_iota(jnp.int32, (TOTAL, TOTAL), 1),
        1.0,
        0.0,
    )
    inner = split(P2 * identity + P3 * approach + P4 * square)
    transform = (2.25 * identity + P1 * approach + dot3(square_parts, inner)) * per_root
    transform_ref[...] = transform
    transform_parts = split(transform)
    zeros = jnp.zeros((6, TOTAL), f32)
    mids = dot3(split(jnp.concatenate([obs_pull, mean_bar, zeros], axis=0)), transform_parts)
    ends = dot3(split(mids), transform_parts)
    mid_pull, mid_bar = mids[0:1], mids[1:2]
    pull_bar = ends[1:2]
    gap = jnp.zeros((4, TOTAL), f32)
    outer = dot3(
        split(jnp.concatenate([mean_bar, mid_pull, mid_bar, obs_pull, gap], axis=0)),
        split(jnp.concatenate([mid_pull, mean_bar, obs_pull, mid_bar, gap], axis=0)),
        TN,
    )
    weight_bar = (0.5 * cov) * sym_ref[...] + 0.5 * outer
    scale_bar = -0.5 * total(weight_bar * transform_ref[...])
    polar_bar = weight_bar * per_root
    left = dot3(approach_parts, split(polar_bar))
    both = left + left.T
    approach = approach_ref[...]
    approach_bar = (
        P1 * polar_bar
        + P2 * both
        + dot3(square_parts, split(P3 * polar_bar + P4 * both))
        + dot3(split(both), split(P3 * approach + P4 * square))
    )
    scale_bar = (scale_bar - total(approach_bar * approach_ref[...])) * per_norm
    sym_bar = (2.0 * per_norm) * (approach_bar + scale_bar * system[...])
    sym_ref[...] = sym_bar

    cot_total = jnp.zeros((1, CELLS), f32)
    for n in range(4):
        value = cot_ref[n]
        cot_total += column_sum(value)
        upper, lower = split(value)
        cot_upper[n * B : (n + 1) * B] = upper
        cot_lower[n * B : (n + 1) * B] = lower
    mine = pl.ds(pl.multiple_of(own * B, B), B)
    rows = jnp.concatenate(
        [transform_ref[mine], column_sum(transform_ref[...]), jnp.zeros((7, TOTAL), f32)], axis=0
    )
    mixed = dot3(split(rows), (cot_upper[...], cot_lower[...]))
    columns = dot3(split(transform_ref[mine]), split(mids), NT)
    weight_sum = jnp.sum(ends[0:1], axis=1, keepdims=True)
    anom_total = mixed[B : B + 1] + (weight_sum / cov) * cot_total
    shared = (cot_total - anom_total) / TOTAL
    rows = jnp.concatenate([sym_ref[mine], column_sum(sym_bar), pull_bar, zeros], axis=0)
    pulled = dot3(split(rows), split(anom_ref[...]))
    innovation, precision = innovation_ref[...], precision_ref[...]
    weight = precision / cov
    pull_sum = jnp.sum(pull_bar, axis=1, keepdims=True)
    obs_total = pulled[B : B + 1] + pull_sum * innovation
    mean_part = -(obs_total * weight) - precision * pulled[B + 1 : B + 2]
    observed_bar = (pulled[:B] + columns[:, 1:2] * innovation) * weight + mean_part / TOTAL
    bent = tanh_ref[...]
    picked_bar = observed_bar * (1.0 + 0.5 * (1.0 - bent * bent))
    upper, lower = split(picked_bar)
    onehot = onehot_of(sites_ref[...])
    field = mixed[:B] + (columns[:, 0:1] / cov) * cot_total + shared
    field = field + (dot(upper, onehot, NT) + dot(lower, onehot, NT))
    for row in range(4):
        bar = ocean_ref[4:5, row * B : (row + 1) * B] * row_block(field, row)
        out_ref[:, row * B : (row + 1) * B] = bar
    for row in range(2):
        cells = slice(row * B, (row + 1) * B)
        backward, forward = out_ref[:, cells], out_ref[:, (row + 2) * B : (row + 3) * B]
        on_edge_ref[:, cells] = chosen(place_ref, forward, backward)
        off_edge_ref[:, cells] = chosen(place_ref, backward, forward)


def coef_sums(weight, center, north, south):
    base = column_sum(weight * center)
    return [
        column_sum(weight * north) - base,
        column_sum(weight * south) - base,
        column_sum(weight * west_of(center)) - base,
        column_sum(weight * east_of(center)) - base,
    ]


def coef_kernel(
    place_ref, bar_ref, bar_on_ref, bar_off_ref, own_ref, first_ref, prior_ref, on_ref, off_ref,
    first_bar_ref, coef_ref,
):
    north_ref, south_ref = sides(place_ref, bar_on_ref, bar_off_ref)
    prior_north_ref, prior_south_ref = sides(place_ref, on_ref, off_ref)
    fields = field_rows(own_ref, prior_north_ref, prior_south_ref)
    bars = (
        [row_block(north_ref[...], r) for r in range(2)]
        + [row_block(bar_ref[...], r) for r in range(4)]
        + [row_block(south_ref[...], r) for r in range(2)]
    )
    prior = (
        [row_block(prior_north_ref[:B], 1)]
        + [row_block(prior_ref[...], r) for r in range(4)]
        + [row_block(prior_south_ref[:B], 0)]
    )
    first_bars = []
    for row in range(1, 7):
        value = fields[row][4:5] * transposed(
            fields, row, bars[row], bars[row - 1], bars[row + 1]
        )
        first_bar_ref[:, (row - 1) * B : row * B] = value
        first_bars.append(value)
    for row in range(4):
        second = coef_sums(
            bars[row + 2],
            row_block(first_ref[...], row + 1),
            row_block(first_ref[...], row),
            row_block(first_ref[...], row + 2),
        )
        first = coef_sums(first_bars[row + 1], prior[row + 1], prior[row], prior[row + 2])
        for k in range(4):
            for copy in range(4):
                coef_ref[copy, k * 4 + row : k * 4 + row + 1] = second[k] + first[k]


def transposed(fields, row, center, north, south):
    return transpose_row(
        center,
        north,
        south,
        coef_rows(fields, row),
        fields[row - 1][1:2],
        fields[row + 1][0:1],
    )


def grad_kernel(place_ref, first_bar_ref, own_ref, on_ref, off_ref, grad_ref):
    prior_north_ref, prior_south_ref = sides(place_ref, on_ref, off_ref)
    fields = field_rows(own_ref, prior_north_ref, prior_south_ref)
    bars = [row_block(first_bar_ref[...], row) for row in range(6)]
    for row in range(4):
        grad_ref[:, row, :] = transposed(
            fields, row + 2, bars[row + 1], bars[row], bars[row + 2]
        )


def call(kernel, outs, scratch=(), smem=False):
    def shaped(s):
        return jax.ShapeDtypeStruct(s, f32)

    def run(*operands):
        specs = [pl.BlockSpec(memory_space=pltpu.VMEM)] * len(operands)
        if smem:
            specs[0] = pl.BlockSpec(memory_space=pltpu.SMEM)
        single = isinstance(outs[0], int)
        return pl.pallas_call(
            kernel,
            out_shape=shaped(outs) if single else [shaped(s) for s in outs],
            in_specs=specs,
            out_specs=pl.BlockSpec(memory_space=pltpu.VMEM)
            if single
            else [pl.BlockSpec(memory_space=pltpu.VMEM)] * len(outs),
            scratch_shapes=list(scratch),
            compiler_params=pltpu.CompilerParams(vmem_limit_bytes=VMEM_BYTES),
        )(*operands)

    return run


def edge_kernel(
    place_ref, prior_ref, coef_ref, mask_ref, prior_out, field_ref, on_edge_ref, off_edge_ref
):
    members = prior_ref.shape[0]
    mask = mask_ref[...].astype(f32)
    for row in range(4):
        cells = slice(row * B, (row + 1) * B)
        value = prior_ref[:, row, :]
        rows = jnp.concatenate(
            [coef_ref[k, row : row + 1, :] for k in range(4)]
            + [mask[row : row + 1], jnp.zeros((3, B), f32)],
            axis=0,
        )
        prior_out[:, cells] = value
        field_ref[:, cells] = rows
    for row in range(2):
        cells = slice(row * B, (row + 1) * B)
        later = slice((row + 2) * B, (row + 3) * B)
        for top, value_ref in ((0, prior_out), (members, field_ref)):
            backward, forward = value_ref[:, cells], value_ref[:, later]
            rows = slice(top, top + value_ref.shape[0])
            on_edge_ref[rows, cells] = chosen(place_ref, forward, backward)
            off_edge_ref[rows, cells] = chosen(place_ref, backward, forward)


def spread_kernel(cot_ref, out_ref):
    for row in range(4):
        value = cot_ref[:, row, :]
        for copy in range(4):
            out_ref[copy, :, row * B : (row + 1) * B] = value


def exchange(on_edge, off_edge):
    count = lax.axis_size(STRIPS)

    def pairs(start):
        low = [(i, i + 1) for i in range(start, count - 1, 2)]
        return low + [(target, source) for source, target in low]

    off = lax.ppermute(off_edge, STRIPS, pairs(1))
    return lax.ppermute(on_edge, STRIPS, pairs(0)), off


def trade(parts, axes):
    return lax.all_to_all(parts, axes, 0, 0, tiled=True)


def sum_kernel(parts_ref, out_ref):
    value = parts_ref[0]
    for i in range(1, parts_ref.shape[0]):
        value += parts_ref[i]
    for copy in range(out_ref.shape[0]):
        out_ref[copy] = value


def summed_copies(parts, count):
    return call(sum_kernel, (count,) + parts.shape[1:])(parts)


def strip_sum(payload):
    pieces = trade(payload.reshape(16, PART, B), ("y", "z_low", "core"))
    pairs = trade(summed_copies(pieces, lax.axis_size("z")), "z")
    mine = trade(summed_copies(pairs, 32), ("z_low", "y", "x"))
    return mine, lax.ppermute(mine, "core", [(0, 1), (1, 0)])


def coef_total_kernel(parts_ref, out_ref):
    value = parts_ref[0] + parts_ref[1] + parts_ref[2] + parts_ref[3]
    out_ref[...] = value / jnp.sqrt(jnp.full((1, 1), TOTAL, f32))


def local(
    prior_ensemble,
    stencil_factors,
    sea_mask,
    measured_site_positions,
    measured_data,
    measurement_precision,
    cotangent,
):
    members = prior_ensemble.shape[0]
    own = lax.axis_index("x")
    place = jnp.stack([own, lax.axis_index("core")]).astype(jnp.int32)
    prior, own_field, on_edge, off_edge = call(
        edge_kernel,
        [(members, CELLS), (8, CELLS), (members + 8, 2 * B), (members + 8, 2 * B)],
        smem=True,
    )(place, prior_ensemble, stencil_factors, sea_mask)
    on, off = exchange(on_edge, off_edge)
    cots = trade(call(spread_kernel, (4, members, CELLS))(cotangent), "x")

    sites = measured_site_positions
    precision = measurement_precision.reshape(1, B)
    data = measured_data.reshape(1, B)

    first, state, bent, outgoing, data, precision = call(
        forecast_kernel, [(members, 6 * B), (members, CELLS), (B, B), (4, OBS_ROWS, B), (1, B), (1, B)], smem=True
    )(place, prior, on, off, own_field, sites, data, precision)
    outgoing, cots = lax.optimization_barrier((outgoing, cots))
    gathered = trade(outgoing, "x")
    payload, anom, innovation = call(
        partial_kernel, [(PAYLOAD_ROWS, B), (TOTAL, B), (1, B)], smem=True
    )(place, gathered, state, cots, data, precision)
    mine, other = strip_sum(payload)
    square = (TOTAL, TOTAL)
    bar, bar_on_edge, bar_off_edge = call(
        assimilate_kernel,
        [(members, CELLS), (members, 2 * B), (members, 2 * B)],
        scratch=[pltpu.VMEM((4, PAYLOAD_ROWS, B), f32)]
        + [pltpu.VMEM(square, f32)] * 4
        + [pltpu.VMEM(square, jnp.bfloat16)] * 2,
        smem=True,
    )(place, mine, other, cots, anom, innovation, precision, bent, sites, own_field)
    bar_on, bar_off = exchange(bar_on_edge, bar_off_edge)
    first_bar, coef = call(coef_kernel, [(members, 6 * B), (4, 16, B)], smem=True)(
        place, bar, bar_on, bar_off, own_field, first, prior, on, off
    )
    grad = call(grad_kernel, (members, 4, B), smem=True)(
        place, first_bar, own_field, on, off
    )
    coef = call(coef_total_kernel, (16, B))(trade(coef, "x"))
    return (
        grad,
        coef.reshape(4, 4, B),
    )


def solution(mesh):
    strips, parts = mesh.devices.shape
    grid = Mesh(mesh.devices.reshape(strips // 16, 2, 4, 2, parts), STRIPS + ("x",))
    placed = (
        P("x", STRIPS, None),
        P(None, STRIPS, None),
        P(STRIPS, None),
        P(STRIPS, None),
        P(STRIPS),
        P(STRIPS),
        P("x", STRIPS, None),
    )
    return jax.shard_map(
        local,
        mesh=grid,
        in_specs=placed,
        out_specs=(P("x", STRIPS, None), P(None, STRIPS, None)),
        check_vma=False,
    )
```

```python
import jax
import jax.numpy as jnp
from jax import lax
from jax.experimental import pallas as pl
from jax.experimental.pallas import tpu as pltpu
from jax.sharding import Mesh
from jax.sharding import PartitionSpec as P

TOTAL = 512
B = 128
CELLS = 512
STRIPS = ("z", "z_low", "y", "core")
GRAM_ROWS = 320
PULL_ROW = GRAM_ROWS + 512
PAYLOAD_ROWS = 896
PART = PAYLOAD_ROWS // 16
HALF = B // 2
OBS_ROWS = B + 8
VMEM_BYTES = 24 * 1024 * 1024
P1, P2, P3, P4 = -2.4375, 1.6875, -0.5625, 0.0625
NN = (((1,), (0,)), ((), ()))
NT = (((1,), (1,)), ((), ()))
TN = (((0,), (0,)), ((), ()))
f32 = jnp.float32


def split(value):
    upper = value.astype(jnp.bfloat16)
    return upper, (value - upper.astype(f32)).astype(jnp.bfloat16)


def dot(left, right, dims=NN):
    return lax.dot_general(left, right, dims, preferred_element_type=f32)


def dot3(left, right, dims=NN):
    lu, ll = left
    ru, rl = right
    return dot(lu, ru, dims) + (dot(lu, rl, dims) + dot(ll, ru, dims))


def total(value):
    return jnp.sum(jnp.sum(value, axis=0, keepdims=True), axis=1, keepdims=True)


def column_sum(value):
    return jnp.sum(value, axis=0, keepdims=True)


def row_block(value, row):
    return value[:, row * B : (row + 1) * B]


def west_of(center):
    column = lax.broadcasted_iota(jnp.int32, center.shape, 1)
    return jnp.where(column == 0, 0.0, pltpu.roll(center, 1, 1))


def east_of(center):
    column = lax.broadcasted_iota(jnp.int32, center.shape, 1)
    return jnp.where(column == B - 1, 0.0, pltpu.roll(center, B - 1, 1))


def substep_row(center, north, south, coef, ocean):
    kept = 1.0 - coef[0] - coef[1] - coef[2] - coef[3]
    return ocean * (
        kept * center
        + coef[0] * north
        + coef[1] * south
        + coef[2] * west_of(center)
        + coef[3] * east_of(center)
    )


def transpose_row(center, north, south, coef, coef_north, coef_south):
    kept = 1.0 - coef[0] - coef[1] - coef[2] - coef[3]
    return (
        kept * center
        + coef_south * south
        + coef_north * north
        + east_of(coef[2] * center)
        + west_of(coef[3] * center)
    )


def onehot_of(sites):
    cell = lax.broadcasted_iota(jnp.int32, (CELLS, B), 0)
    return jnp.where(cell == sites, 1.0, 0.0).astype(jnp.bfloat16)


def coef_rows(fields, row):
    return [fields[row][k : k + 1] for k in range(4)]


def chosen(place_ref, even, odd):
    core = jnp.zeros(even.shape, jnp.int32) + place_ref[1]
    return jnp.where(core == 0, even, odd)


def sides(place_ref, on_ref, off_ref):
    on, off = on_ref[...], off_ref[...]
    return chosen(place_ref, off, on), chosen(place_ref, on, off)


def field_rows(own_ref, north_ref, south_ref):
    members = north_ref.shape[0] - 8
    return (
        [row_block(north_ref[members:], r) for r in range(2)]
        + [row_block(own_ref[...], r) for r in range(4)]
        + [row_block(south_ref[members:], r) for r in range(2)]
    )


def forecast_kernel(
    place_ref, off_ref, on_ref, prior_ref, own_ref, sites_ref, data_ref, precision_ref,
    first_ref, state_ref, tanh_ref, out_ref, data_out, precision_out, north_out, south_out,
):
    north_ref, south_ref = sides(place_ref, on_ref, off_ref)
    north_out[...] = north_ref
    south_out[...] = south_ref
    data_out[...] = data_ref[...]
    precision_out[...] = precision_ref[...]
    fields = field_rows(own_ref, north_ref, south_ref)
    prior = (
        [row_block(north_ref[:B], r) for r in range(2)]
        + [row_block(prior_ref[...], r) for r in range(4)]
        + [row_block(south_ref[:B], r) for r in range(2)]
    )
    first = []
    for row in range(1, 7):
        value = substep_row(
            prior[row],
            prior[row - 1],
            prior[row + 1],
            coef_rows(fields, row),
            fields[row][4:5],
        )
        first_ref[:, (row - 1) * B : row * B] = value
        first.append(value)
    onehot = onehot_of(sites_ref[...])
    picked = jnp.zeros((B, B), f32)
    sums = []
    for row in range(4):
        value = substep_row(
            first[row + 1],
            first[row],
            first[row + 2],
            coef_rows(fields, row + 2),
            fields[row + 2][4:5],
        )
        state_ref[:, row * B : (row + 1) * B] = value
        upper, rest = split(value)
        lower = (value - upper.astype(f32) - rest.astype(f32)).astype(jnp.bfloat16)
        here = onehot[row * B : (row + 1) * B]
        picked += dot(upper, here) + (dot(rest, here) + dot(lower, here))
        sums.append(column_sum(value))
    bent = jnp.tanh(picked)
    tanh_ref[...] = bent
    observed = picked + 0.5 * bent
    sums = jnp.concatenate(sums + [jnp.zeros((4, B), f32)], axis=0)
    for copy in range(4):
        out_ref[copy, :B] = observed
        out_ref[copy, B:] = sums


def partial_kernel(
    own_ref, gathered_ref, state_ref, cot_ref, data_ref, precision_ref,
    payload_ref, anom_ref, innovation_ref,
):
    own = own_ref[0]
    root = jnp.sqrt(jnp.full((1, 1), TOTAL - 1, f32))
    sums = column_sum(gathered_ref[0, :B])
    cells = gathered_ref[0, B:]
    for m in range(1, 4):
        sums += column_sum(gathered_ref[m, :B])
        cells += gathered_ref[m, B:]
    observed_mean = sums / TOTAL
    precision = precision_ref[...]
    weight = precision / root
    innovation = precision * (data_ref[...] - observed_mean)
    innovation_ref[...] = innovation
    for m in range(4):
        anom_ref[m * B : (m + 1) * B] = (gathered_ref[m, :B] - observed_mean) * weight

    def members(start, count):
        return anom_ref[pl.ds(pl.multiple_of(start, B // 2), count)]

    mine = members(own * B, B)
    mine_parts = split(mine)
    payload_ref[:B] = dot3(mine_parts, mine_parts, NT)
    after = lax.rem(own + 1, 4)
    payload_ref[B : 2 * B] = dot3(mine_parts, split(members(after * B, B)), NT)
    low = lax.rem(own, 2)
    half = members(low * B + (own // 2) * HALF, HALF)
    payload_ref[2 * B : GRAM_ROWS] = dot3(split(half), split(members(low * B + 2 * B, B)), NT)
    payload_ref[PULL_ROW : PULL_ROW + 8] = dot3(
        split(jnp.broadcast_to(innovation, (8, B))), mine_parts, NT
    )
    payload_ref[PULL_ROW + 8 :] = jnp.zeros((PAYLOAD_ROWS - PULL_ROW - 8, B), f32)
    deviations = jnp.concatenate(
        [
            (row_block(state_ref[...], r) - cells[r : r + 1] / TOTAL) / root
            for r in range(4)
        ],
        axis=1,
    )
    parts = split(deviations)
    for n in range(4):
        payload_ref[GRAM_ROWS + n * B : GRAM_ROWS + (n + 1) * B] = dot3(
            parts, split(cot_ref[n]), NT
        )


def assimilate_kernel(
    place_ref, mine_ref, other_ref, cot_ref, anom_ref, innovation_ref,
    precision_ref, tanh_ref, sites_ref, ocean_ref,
    off_edge_ref, on_edge_ref, out_ref,
    blocks, system, approach_ref, sym_ref, transform_ref, cot_upper, cot_lower,
):
    own, core = place_ref[0], place_ref[1]
    for p in range(8):
        here = pl.ds(pl.multiple_of((p * 2 + core) * PART, 8), PART)
        there = pl.ds(pl.multiple_of((p * 2 + 1 - core) * PART, 8), PART)
        spot = ((p % 2) * 4 + p // 2) * 4
        for x in range(4):
            blocks[x, here] = mine_ref[spot + x]
            blocks[x, there] = other_ref[spot + x]

    def put(m, n, value):
        system[m * B : (m + 1) * B, n * B : (n + 1) * B] = value

    diagonal = (
        lax.broadcasted_iota(jnp.int32, (B, B), 0) == lax.broadcasted_iota(jnp.int32, (B, B), 1)
    )
    for m in range(4):
        put(m, m, blocks[m, :B] + jnp.where(diagonal, 1.0, 0.0))
        n = (m + 1) % 4
        following = blocks[m, B : 2 * B]
        put(m, n, following)
        put(n, m, following.T)
    for m in range(2):
        across = jnp.concatenate(
            [blocks[m, 2 * B : GRAM_ROWS], blocks[m + 2, 2 * B : GRAM_ROWS]], axis=0
        )
        put(m, m + 2, across)
        put(m + 2, m, across.T)

    sums = [jnp.zeros((1, B), f32) for _ in range(4)]

    def cross(m, n):
        return blocks[m, GRAM_ROWS + n * B : GRAM_ROWS + (n + 1) * B]

    for m in range(4):
        for n in range(m, 4):
            turned = cross(m, n).T
            sums[m] += column_sum(turned)
            if n == m:
                sym_ref[m * B : (m + 1) * B, m * B : (m + 1) * B] = cross(m, m) + turned
            else:
                back = cross(n, m)
                back_turned = back.T
                sums[n] += column_sum(back_turned)
                sym_ref[m * B : (m + 1) * B, n * B : (n + 1) * B] = cross(m, n) + back_turned
                sym_ref[n * B : (n + 1) * B, m * B : (m + 1) * B] = back + turned
    mean_bar = jnp.concatenate(sums, axis=1)
    obs_pull = jnp.concatenate([blocks[m, PULL_ROW : PULL_ROW + 1] for m in range(4)], axis=1)

    full = system[...]
    norm = jnp.sqrt(total(full * full))
    root = jnp.sqrt(norm)
    per_norm, per_root = 1.0 / norm, 1.0 / root
    cov = jnp.sqrt(jnp.full((1, 1), TOTAL - 1, f32))
    approach = full * per_norm
    approach_ref[...] = approach
    approach_parts = split(approach)
    square = dot3(approach_parts, approach_parts)
    square_parts = split(square)
    identity = jnp.where(
        lax.broadcasted_iota(jnp.int32, (TOTAL, TOTAL), 0)
        == lax.broadcasted_iota(jnp.int32, (TOTAL, TOTAL), 1),
        1.0,
        0.0,
    )
    inner = split(P2 * identity + P3 * approach + P4 * square)
    transform = (2.25 * identity + P1 * approach + dot3(square_parts, inner)) * per_root
    transform_ref[...] = transform
    transform_parts = split(transform)
    zeros = jnp.zeros((6, TOTAL), f32)
    mids = dot3(split(jnp.concatenate([obs_pull, mean_bar, zeros], axis=0)), transform_parts)
    ends = dot3(split(mids), transform_parts)
    mid_pull, mid_bar = mids[0:1], mids[1:2]
    pull_bar = ends[1:2]
    gap = jnp.zeros((4, TOTAL), f32)
    outer = dot3(
        split(jnp.concatenate([mean_bar, mid_pull, mid_bar, obs_pull, gap], axis=0)),
        split(jnp.concatenate([mid_pull, mean_bar, obs_pull, mid_bar, gap], axis=0)),
        TN,
    )
    weight_bar = (0.5 * cov) * sym_ref[...] + 0.5 * outer
    scale_bar = -0.5 * total(weight_bar * transform_ref[...])
    polar_bar = weight_bar * per_root
    left = dot3(approach_parts, split(polar_bar))
    both = left + left.T
    approach = approach_ref[...]
    approach_bar = (
        P1 * polar_bar
        + P2 * both
        + dot3(square_parts, split(P3 * polar_bar + P4 * both))
        + dot3(split(both), split(P3 * approach + P4 * square))
    )
    scale_bar = (scale_bar - total(approach_bar * approach_ref[...])) * per_norm
    sym_bar = (2.0 * per_norm) * (approach_bar + scale_bar * system[...])
    sym_ref[...] = sym_bar

    cot_total = jnp.zeros((1, CELLS), f32)
    for n in range(4):
        value = cot_ref[n]
        cot_total += column_sum(value)
        upper, lower = split(value)
        cot_upper[n * B : (n + 1) * B] = upper
        cot_lower[n * B : (n + 1) * B] = lower
    mine = pl.ds(pl.multiple_of(own * B, B), B)
    rows = jnp.concatenate(
        [transform_ref[mine], column_sum(transform_ref[...]), jnp.zeros((7, TOTAL), f32)], axis=0
    )
    mixed = dot3(split(rows), (cot_upper[...], cot_lower[...]))
    columns = dot3(split(transform_ref[mine]), split(mids), NT)
    weight_sum = jnp.sum(ends[0:1], axis=1, keepdims=True)
    anom_total = mixed[B : B + 1] + (weight_sum / cov) * cot_total
    shared = (cot_total - anom_total) / TOTAL
    rows = jnp.concatenate([sym_ref[mine], column_sum(sym_bar), pull_bar, zeros], axis=0)
    pulled = dot3(split(rows), split(anom_ref[...]))
    innovation, precision = innovation_ref[...], precision_ref[...]
    weight = precision / cov
    pull_sum = jnp.sum(pull_bar, axis=1, keepdims=True)
    obs_total = pulled[B : B + 1] + pull_sum * innovation
    mean_part = -(obs_total * weight) - precision * pulled[B + 1 : B + 2]
    observed_bar = (pulled[:B] + columns[:, 1:2] * innovation) * weight + mean_part / TOTAL
    bent = tanh_ref[...]
    picked_bar = observed_bar * (1.0 + 0.5 * (1.0 - bent * bent))
    upper, lower = split(picked_bar)
    onehot = onehot_of(sites_ref[...])
    field = mixed[:B] + (columns[:, 0:1] / cov) * cot_total + shared
    field = field + (dot(upper, onehot, NT) + dot(lower, onehot, NT))
    for row in range(4):
        bar = ocean_ref[4:5, row * B : (row + 1) * B] * row_block(field, row)
        out_ref[:, row * B : (row + 1) * B] = bar
    for row in range(2):
        cells = slice(row * B, (row + 1) * B)
        backward, forward = out_ref[:, cells], out_ref[:, (row + 2) * B : (row + 3) * B]
        on_edge_ref[:, cells] = chosen(place_ref, forward, backward)
        off_edge_ref[:, cells] = chosen(place_ref, backward, forward)


def coef_sums(weight, center, north, south):
    base = column_sum(weight * center)
    return [
        column_sum(weight * north) - base,
        column_sum(weight * south) - base,
        column_sum(weight * west_of(center)) - base,
        column_sum(weight * east_of(center)) - base,
    ]


def coef_kernel(
    place_ref, bar_off_ref, bar_on_ref, bar_ref, own_ref, first_ref, prior_ref,
    prior_north_ref, prior_south_ref,
    first_bar_ref, coef_ref,
):
    north_ref, south_ref = sides(place_ref, bar_on_ref, bar_off_ref)
    fields = field_rows(own_ref, prior_north_ref, prior_south_ref)
    bars = (
        [row_block(north_ref[...], r) for r in range(2)]
        + [row_block(bar_ref[...], r) for r in range(4)]
        + [row_block(south_ref[...], r) for r in range(2)]
    )
    prior = (
        [row_block(prior_north_ref[:B], 1)]
        + [row_block(prior_ref[...], r) for r in range(4)]
        + [row_block(prior_south_ref[:B], 0)]
    )
    first_bars = []
    for row in range(1, 7):
        value = fields[row][4:5] * transposed(
            fields, row, bars[row], bars[row - 1], bars[row + 1]
        )
        first_bar_ref[:, (row - 1) * B : row * B] = value
        first_bars.append(value)
    for row in range(4):
        second = coef_sums(
            bars[row + 2],
            row_block(first_ref[...], row + 1),
            row_block(first_ref[...], row),
            row_block(first_ref[...], row + 2),
        )
        first = coef_sums(first_bars[row + 1], prior[row + 1], prior[row], prior[row + 2])
        for k in range(4):
            for copy in range(4):
                coef_ref[copy, k * 4 + row : k * 4 + row + 1] = second[k] + first[k]


def transposed(fields, row, center, north, south):
    return transpose_row(
        center,
        north,
        south,
        coef_rows(fields, row),
        fields[row - 1][1:2],
        fields[row + 1][0:1],
    )


def grad_kernel(first_bar_ref, own_ref, prior_north_ref, prior_south_ref, grad_ref):
    fields = field_rows(own_ref, prior_north_ref, prior_south_ref)
    bars = [row_block(first_bar_ref[...], row) for row in range(6)]
    for row in range(4):
        grad_ref[:, row, :] = transposed(
            fields, row + 2, bars[row + 1], bars[row], bars[row + 2]
        )


def call(kernel, outs, scratch=(), smem=False):
    def shaped(s):
        return jax.ShapeDtypeStruct(s, f32)

    def run(*operands):
        specs = [pl.BlockSpec(memory_space=pltpu.VMEM)] * len(operands)
        if smem:
            specs[0] = pl.BlockSpec(memory_space=pltpu.SMEM)
        single = isinstance(outs[0], int)
        return pl.pallas_call(
            kernel,
            out_shape=shaped(outs) if single else [shaped(s) for s in outs],
            in_specs=specs,
            out_specs=pl.BlockSpec(memory_space=pltpu.VMEM)
            if single
            else [pl.BlockSpec(memory_space=pltpu.VMEM)] * len(outs),
            scratch_shapes=list(scratch),
            compiler_params=pltpu.CompilerParams(vmem_limit_bytes=VMEM_BYTES),
        )(*operands)

    return run


def edge_kernel(
    place_ref, prior_ref, coef_ref, mask_ref, off_edge_ref, on_edge_ref, prior_out, field_ref
):
    members = prior_ref.shape[0]
    mask = mask_ref[...].astype(f32)
    for row in range(4):
        cells = slice(row * B, (row + 1) * B)
        value = prior_ref[:, row, :]
        rows = jnp.concatenate(
            [coef_ref[k, row : row + 1, :] for k in range(4)]
            + [mask[row : row + 1], jnp.zeros((3, B), f32)],
            axis=0,
        )
        prior_out[:, cells] = value
        field_ref[:, cells] = rows
    for row in range(2):
        cells = slice(row * B, (row + 1) * B)
        later = slice((row + 2) * B, (row + 3) * B)
        for top, value_ref in ((0, prior_out), (members, field_ref)):
            backward, forward = value_ref[:, cells], value_ref[:, later]
            rows = slice(top, top + value_ref.shape[0])
            on_edge_ref[rows, cells] = chosen(place_ref, forward, backward)
            off_edge_ref[rows, cells] = chosen(place_ref, backward, forward)


def spread_kernel(cot_ref, out_ref):
    for row in range(4):
        value = cot_ref[:, row, :]
        for copy in range(4):
            out_ref[copy, :, row * B : (row + 1) * B] = value


def exchange(on_edge, off_edge):
    count = lax.axis_size(STRIPS)

    def pairs(start):
        low = [(i, i + 1) for i in range(start, count - 1, 2)]
        return low + [(target, source) for source, target in low]

    off = lax.ppermute(off_edge, STRIPS, pairs(1))
    return lax.ppermute(on_edge, STRIPS, pairs(0)), off


def trade(parts, axes):
    return lax.all_to_all(parts, axes, 0, 0, tiled=True)


def sum_kernel(parts_ref, out_ref):
    value = parts_ref[0]
    for i in range(1, parts_ref.shape[0]):
        value += parts_ref[i]
    for copy in range(out_ref.shape[0]):
        out_ref[copy] = value


def summed_copies(parts, count):
    return call(sum_kernel, (count,) + parts.shape[1:])(parts)


def strip_sum(payload):
    pieces = trade(payload.reshape(16, PART, B), ("y", "z_low", "core"))
    pairs = trade(summed_copies(pieces, lax.axis_size("z")), "z")
    mine = trade(summed_copies(pairs, 32), ("z_low", "y", "x"))
    return mine, lax.ppermute(mine, "core", [(0, 1), (1, 0)])


def coef_total_kernel(parts_ref, out_ref):
    value = parts_ref[0] + parts_ref[1] + parts_ref[2] + parts_ref[3]
    out_ref[...] = value / jnp.sqrt(jnp.full((1, 1), TOTAL, f32))


def local(
    prior_ensemble,
    stencil_factors,
    sea_mask,
    measured_site_positions,
    measured_data,
    measurement_precision,
    cotangent,
):
    members = prior_ensemble.shape[0]
    own = lax.axis_index("x")
    place = jnp.stack([own, lax.axis_index("core")]).astype(jnp.int32)
    off_edge, on_edge, prior, own_field = call(
        edge_kernel,
        [(members + 8, 2 * B), (members + 8, 2 * B), (members, CELLS), (8, CELLS)],
        smem=True,
    )(place, prior_ensemble, stencil_factors, sea_mask)
    on, off = exchange(on_edge, off_edge)
    cots = trade(call(spread_kernel, (4, members, CELLS))(cotangent), "x")

    sites = measured_site_positions
    precision = measurement_precision.reshape(1, B)
    data = measured_data.reshape(1, B)

    first, state, bent, outgoing, data, precision, north, south = call(
        forecast_kernel, [(members, 6 * B), (members, CELLS), (B, B), (4, OBS_ROWS, B), (1, B), (1, B)]
        + [(members + 8, 2 * B)] * 2,
        smem=True,
    )(place, off, on, prior, own_field, sites, data, precision)
    outgoing, cots = lax.optimization_barrier((outgoing, cots))
    gathered = trade(outgoing, "x")
    payload, anom, innovation = call(
        partial_kernel, [(PAYLOAD_ROWS, B), (TOTAL, B), (1, B)], smem=True
    )(place, gathered, state, cots, data, precision)
    mine, other = strip_sum(payload)
    square = (TOTAL, TOTAL)
    bar_off_edge, bar_on_edge, bar = call(
        assimilate_kernel,
        [(members, 2 * B), (members, 2 * B), (members, CELLS)],
        scratch=[pltpu.VMEM((4, PAYLOAD_ROWS, B), f32)]
        + [pltpu.VMEM(square, f32)] * 4
        + [pltpu.VMEM(square, jnp.bfloat16)] * 2,
        smem=True,
    )(place, mine, other, cots, anom, innovation, precision, bent, sites, own_field)
    bar_on, bar_off = exchange(bar_on_edge, bar_off_edge)
    first_bar, coef = call(coef_kernel, [(members, 6 * B), (4, 16, B)], smem=True)(
        place, bar_off, bar_on, bar, own_field, first, prior, north, south
    )
    grad = call(grad_kernel, (members, 4, B))(first_bar, own_field, north, south)
    coef = call(coef_total_kernel, (16, B))(trade(coef, "x"))
    return (
        grad,
        coef.reshape(4, 4, B),
    )


def solution(mesh):
    strips, parts = mesh.devices.shape
    grid = Mesh(mesh.devices.reshape(strips // 16, 2, 4, 2, parts), STRIPS + ("x",))
    placed = (
        P("x", STRIPS, None),
        P(None, STRIPS, None),
        P(STRIPS, None),
        P(STRIPS, None),
        P(STRIPS),
        P(STRIPS),
        P("x", STRIPS, None),
    )
    return jax.shard_map(
        local,
        mesh=grid,
        in_specs=placed,
        out_specs=(P("x", STRIPS, None), P(None, STRIPS, None)),
        check_vma=False,
    )
```
